32 devices in a mesh: grid: 16 (over z, x, core), rep: 2 (over y).
Axes of the slice: x: 2, y: 2, z: 4, core: 2. Of those that a mesh axis runs over, the one named last changes fastest.
Arguments:
- density: bfloat16 [1280, 1280], P('grid', 'rep'), may hold values from -0.625 to 0.625
- density_pattern: int32 [10, 10], replicated, may hold values 0 or 1
- square_pattern: int32 [10, 10], replicated, may hold values 0 or 1
- cube_pattern: int32 [10, 10], replicated, may hold values 0 or 1
- block_order: int32 [10], replicated, may hold values from 0 to 9, each once
Outputs:
- purified: float32 [1280, 1280], P('grid', 'rep')
The draws below stay inside these ranges and needn't reach their ends.
All inputs are finite; a program needn't handle non-finite values.
Results may differ from the reference program's by a relative error of at most 0.0025.
Values may be sent and summed in bfloat16 or wider, within the bound.
No kernel may reach another device: no remote copies, remote signals or barrier semaphores. Data moves between devices by JAX's collectives and lax.ppermute only.
A program may use at most 64 MiB of HBM per device.

```python
import jax
import jax.numpy as jnp

BLOCK = 128
ORDER = 1280
NBLK = 10


def with_ends(values, stream_key, least, high):
    spot = [jax.random.randint(jax.random.fold_in(stream_key, axis), (), 0, length) for axis, length in enumerate(values.shape)]
    main_axis = values.shape.index(max(values.shape))
    beside = spot[:main_axis] + [(spot[main_axis] + 1) % values.shape[main_axis]] + spot[main_axis + 1:]
    return values.at[tuple(spot)].set(least).at[tuple(beside)].set(high)


def steps_of(own_key, dims, pieces, least, largest):
    loudness, own = 1.0, jax.random.fold_in(own_key, 6)
    for axis_at, blocks in pieces:
        steps = jnp.exp(jax.random.uniform(jax.random.fold_in(own, axis_at), (blocks,), jnp.float32, least / len(pieces), largest / len(pieces)))
        loudness = loudness * jnp.repeat(steps, dims[axis_at] // blocks).reshape([-1 if axis == axis_at else 1 for axis in range(len(dims))])
    return loudness


def noise(stream_key, dims, deviation, most, pieces=(), held_as=jnp.bfloat16):
    result = deviation * jax.random.normal(stream_key, dims, jnp.float32)
    if pieces:
        result = result * steps_of(stream_key, dims, pieces, -0.22, 0.18)
    return jnp.clip(result, -most, most).astype(held_as)


def setup_inputs(seed: int = 0) -> dict:
    splits = jax.random.split(jax.random.key(seed), 6)
    density = noise(splits[0], (ORDER, ORDER), (ORDER // 16) ** -0.5, 0.625, ((0, 16), (1, 2)))
    density_pattern = with_ends((jax.random.randint(splits[1], (NBLK, NBLK), 0, 2) < 1).astype(jnp.int32), jax.random.fold_in(splits[1], 1), 0, 1)
    square_pattern = with_ends((jax.random.randint(splits[2], (NBLK, NBLK), 0, 4) < 3).astype(jnp.int32), jax.random.fold_in(splits[2], 1), 0, 1)
    cube_pattern = with_ends((jax.random.randint(splits[3], (NBLK, NBLK), 0, 4) < 3).astype(jnp.int32), jax.random.fold_in(splits[3], 1), 0, 1)
    block_order = jax.random.permutation(splits[4], NBLK).astype(jnp.int32)
    return dict(density=density, density_pattern=density_pattern, square_pattern=square_pattern, cube_pattern=cube_pattern, block_order=block_order)


def stored_mask(pattern, block_order):
    stored = pattern[block_order][:, block_order]
    return jnp.repeat(jnp.repeat(stored, BLOCK, axis=0), BLOCK, axis=1)


def reference(density, density_pattern, square_pattern, cube_pattern, block_order):
    masked = density * stored_mask(density_pattern, block_order).astype(jnp.bfloat16)
    square = jnp.dot(masked, masked, preferred_element_type=jnp.float32)
    square = square * stored_mask(square_pattern, block_order).astype(jnp.float32)
    square_half = square.astype(jnp.bfloat16)
    cube = jnp.dot(square_half, masked, preferred_element_type=jnp.float32)
    cube = cube * stored_mask(cube_pattern, block_order).astype(jnp.float32)
    return 3.0 * square - 2.0 * cube
```

```python
import functools

import jax
import jax.numpy as jnp
from jax import lax
from jax.experimental import pallas as pl
from jax.experimental.pallas import tpu as pltpu
from jax.sharding import PartitionSpec as P

BLOCK = 128
VMEM_LIMIT = 56 * 1024 * 1024
IN_SMEM = pl.BlockSpec(memory_space=pltpu.SMEM)
ANYWHERE = pl.BlockSpec(memory_space=pl.ANY)
IN_VMEM = pl.BlockSpec(memory_space=pltpu.VMEM)


def factors(size):
    pair = 2 if size % 2 == 0 else 1
    rest = size // pair
    outer = 4 if rest % 4 == 0 else 1
    return outer, rest // outer, pair


def shift_pairs(dims, axis, step):
    outer, inner, pair = dims
    pairs = []
    for source in range(outer * inner * pair):
        place = [source // (inner * pair), source // pair % inner, source % pair]
        place[axis] = (place[axis] + step) % dims[axis]
        pairs.append((source, (place[0] * inner + place[1]) * pair + place[2]))
    return pairs


def gather_pieces(own, dims):
    held = {(0, 0, 0): own}
    for axis in range(3):
        before = dict(held)
        for step in range(1, dims[axis]):
            pairs = shift_pairs(dims, axis, step)
            for key, piece in before.items():
                new = list(key)
                new[axis] = step
                held[tuple(new)] = lax.ppermute(piece, "grid", pairs)
    return held


def source_index(here, key, dims):
    outer, inner, pair = dims
    at = (here // (inner * pair), here // pair % inner, here % pair)
    z, x, c = [lax.rem(a - k + d, d) for a, k, d in zip(at, key, dims)]
    return (z * inner + x) * pair + c


def pick(pattern, order, row_block, col_block):
    return pattern[order[row_block], order[col_block]].astype(jnp.float32)


def band_mask(pattern, order, first_row, rows, first_col_block, col_blocks):
    top = first_row // BLOCK
    low = (first_row + rows - 1) // BLOCK
    split = (top + 1) * BLOCK - first_row
    upper = lax.broadcasted_iota(jnp.int32, (rows, BLOCK), 0) < split
    tiles = []
    for j in range(col_blocks):
        a = pick(pattern, order, top, first_col_block + j)
        b = pick(pattern, order, low, first_col_block + j)
        tiles.append(jnp.where(upper, a, b))
    return jnp.concatenate(tiles, axis=1)


def square_kernel(keys, dims, reps, *refs):
    density_pattern, square_pattern, order = refs[:3]
    panel = refs[3:3 + reps]
    pieces = refs[3 + reps:3 + reps + len(keys)]
    band, square, square_half, landed = refs[3 + reps + len(keys):]
    here, rep = lax.axis_index("grid"), lax.axis_index("rep")
    rows, cols = panel[0].shape
    col_blocks = cols // BLOCK
    copies = []
    for at, (key, piece) in enumerate(zip(keys, pieces)):
        start = pl.multiple_of(source_index(here, key, dims) * rows, 16)
        copies.append(pltpu.make_async_copy(piece, band.at[pl.ds(start, rows)], landed.at[at]))
        copies[-1].start()
    for copy in copies:
        copy.wait()
    first_col = rep * col_blocks

    def keep_row(i, _):
        for j in range(col_blocks):
            keep = pick(density_pattern, order, i, first_col + j)
            where = (pl.ds(pl.multiple_of(i * BLOCK, BLOCK), BLOCK), pl.ds(j * BLOCK, BLOCK))
            band[where] = band[where] * jnp.full((BLOCK, BLOCK), keep, jnp.float32).astype(jnp.bfloat16)
        return 0

    row_blocks = band.shape[0] // BLOCK
    lax.fori_loop(0, row_blocks, keep_row, 0, unroll=row_blocks <= 16)
    total = jnp.zeros((rows, cols), jnp.float32)
    for q in range(reps):
        at = lax.rem(rep - q + reps, reps)
        keep = band_mask(density_pattern, order, here * rows, rows, at * col_blocks, col_blocks)
        left = panel[q][...] * keep.astype(jnp.bfloat16)
        right = band[pl.ds(pl.multiple_of(at * cols, BLOCK), cols), :]
        total += jnp.dot(left, right, preferred_element_type=jnp.float32)
    total *= band_mask(square_pattern, order, here * rows, rows, first_col, col_blocks)
    square[...] = total
    square_half[...] = total.astype(jnp.bfloat16)


def cube_kernel(reps, *refs):
    cube_pattern, order = refs[:2]
    panel = refs[2:2 + reps]
    band, square, out = refs[2 + reps:]
    here, rep = lax.axis_index("grid"), lax.axis_index("rep")
    rows, cols = square.shape
    col_blocks = cols // BLOCK
    total = jnp.zeros((rows, cols), jnp.float32)
    for q in range(reps):
        at = lax.rem(rep - q + reps, reps)
        right = band[pl.ds(pl.multiple_of(at * cols, BLOCK), cols), :]
        total += jnp.dot(panel[q][...], right, preferred_element_type=jnp.float32)
    total *= band_mask(cube_pattern, order, here * rows, rows, rep * col_blocks, col_blocks)
    out[...] = 3.0 * square[...] - 2.0 * total


def row_panel(own, reps):
    shifts = [[(s, (s + q) % reps) for s in range(reps)] for q in range(1, reps)]
    return [own] + [lax.ppermute(own, "rep", pairs) for pairs in shifts]


def on_device(grid, reps, density, density_pattern, square_pattern, cube_pattern, block_order):
    rows, cols = density.shape
    dims = factors(grid)
    params = pltpu.CompilerParams(vmem_limit_bytes=VMEM_LIMIT)
    panel = row_panel(density, reps)
    held = gather_pieces(density, dims)
    keys = sorted(held)
    band, square, square_half = pl.pallas_call(
        functools.partial(square_kernel, keys, dims, reps),
        out_shape=(
            jax.ShapeDtypeStruct((grid * rows, cols), jnp.bfloat16),
            jax.ShapeDtypeStruct((rows, cols), jnp.float32),
            jax.ShapeDtypeStruct((rows, cols), jnp.bfloat16),
        ),
        in_specs=[IN_SMEM] * 3 + [IN_VMEM] * reps + [ANYWHERE] * len(keys),
        out_specs=(IN_VMEM,) * 3,
        scratch_shapes=[pltpu.SemaphoreType.DMA((len(keys),))],
        compiler_params=params,
        name="square",
    )(density_pattern, square_pattern, block_order, *panel, *[held[key] for key in keys])
    half_panel = row_panel(square_half, reps)
    return pl.pallas_call(
        functools.partial(cube_kernel, reps),
        out_shape=jax.ShapeDtypeStruct((rows, cols), jnp.float32),
        in_specs=[IN_SMEM] * 2 + [IN_VMEM] * (reps + 2),
        out_specs=IN_VMEM,
        compiler_params=params,
        name="cube",
    )(cube_pattern, block_order, *half_panel, band, square)


def solution(mesh):
    placed = (P("grid", "rep"), P(), P(), P(), P())
    return jax.shard_map(
        functools.partial(on_device, mesh.shape["grid"], mesh.shape["rep"]),
        mesh=mesh, in_specs=placed, out_specs=P("grid", "rep"), check_vma=False,
    )
```

```python
import functools

import jax
import jax.numpy as jnp
from jax import lax
from jax.experimental import pallas as pl
from jax.experimental.pallas import tpu as pltpu
from jax.sharding import PartitionSpec as P

BLOCK = 128
IN_SMEM = pl.BlockSpec(memory_space=pltpu.SMEM)
IN_VMEM = pl.BlockSpec(memory_space=pltpu.VMEM)


def pick(pattern, order, row_block, col_block):
    return pattern[order[row_block], order[col_block]].astype(jnp.float32)


def rows_mask(pattern, order, first_row, rows, first_col_block, col_blocks):
    top = first_row // BLOCK
    low = (first_row + rows - 1) // BLOCK
    split = (top + 1) * BLOCK - first_row
    upper = lax.broadcasted_iota(jnp.int32, (rows, BLOCK), 0) < split
    tiles = []
    for j in range(col_blocks):
        a = pick(pattern, order, top, first_col_block + j)
        b = pick(pattern, order, low, first_col_block + j)
        tiles.append(jnp.where(upper, a, b))
    return jnp.concatenate(tiles, axis=1)


def keep_blocks(pattern, order, source, target, source_col, target_col, col_blocks, first_col):
    row_blocks = source.shape[0] // BLOCK

    def keep_row(i, _):
        down = pl.ds(pl.multiple_of(i * BLOCK, BLOCK), BLOCK)
        for j in range(col_blocks):
            keep = pick(pattern, order, i, first_col + j)
            factor = jnp.full((BLOCK, BLOCK), keep, jnp.float32).astype(jnp.bfloat16)
            value = source[down, pl.ds(source_col + j * BLOCK, BLOCK)]
            target[down, pl.ds(target_col + j * BLOCK, BLOCK)] = value * factor
        return 0

    lax.fori_loop(0, row_blocks, keep_row, 0, unroll=row_blocks <= 16)


def square_kernel(reps, parts, *refs):
    density_pattern, square_pattern, order = refs[:3]
    panel = refs[3:3 + reps]
    pieces = refs[3 + reps:3 + reps + parts]
    band, tripled, square_half = refs[3 + reps + parts:]
    here, rep = lax.axis_index("grid"), lax.axis_index("rep")
    rows, cols = panel[0].shape
    col_blocks = cols // BLOCK
    first_col = rep * col_blocks
    done = 0
    for piece in pieces:
        count = piece.shape[1] // BLOCK
        keep_blocks(density_pattern, order, piece, band, 0, done * BLOCK, count, first_col + done)
        done += count
    total = jnp.zeros((rows, cols), jnp.float32)
    for q in range(reps):
        at = lax.rem(rep - q + reps, reps)
        keep = rows_mask(density_pattern, order, here * rows, rows, at * col_blocks, col_blocks)
        left = panel[q][...] * keep.astype(jnp.bfloat16)
        right = band[pl.ds(pl.multiple_of(at * cols, BLOCK), cols), :]
        total += jnp.dot(left, right, preferred_element_type=jnp.float32)
    total *= rows_mask(square_pattern, order, here * rows, rows, first_col, col_blocks)
    tripled[...] = 3.0 * total
    square_half[...] = total.astype(jnp.bfloat16)


def cube_kernel(shift, cube_pattern, order, half, band, before, out):
    here, rep = lax.axis_index("grid"), lax.axis_index("rep")
    reps = lax.axis_size("rep")
    rows, cols = before.shape
    col_blocks = cols // BLOCK
    at = lax.rem(rep - shift + reps, reps)
    right = band[pl.ds(pl.multiple_of(at * cols, BLOCK), cols), :]
    part = jnp.dot(half[...], right, preferred_element_type=jnp.float32)
    keep = rows_mask(cube_pattern, order, here * rows, rows, rep * col_blocks, col_blocks)
    out[...] = before[...] - 2.0 * (part * keep)


def shifted(own, reps):
    return [
        lax.ppermute(own, "rep", [(s, (s + q) % reps) for s in range(reps)])
        for q in range(1, reps)
    ]


def on_device(grid, reps, density, density_pattern, square_pattern, cube_pattern, block_order):
    rows, cols = density.shape
    band_bytes = grid * rows * cols * 2
    room = min(3 * band_bytes + (4 << 20), 56 << 20)
    params = pltpu.CompilerParams(vmem_limit_bytes=room)
    panel = [density] + shifted(density, reps)
    cut = (cols // BLOCK + 1) // 2 * BLOCK
    pieces = [
        lax.all_gather(part, "grid", axis=0, tiled=True)
        for part in (density[:, :cut], density[:, cut:])
    ]
    product = 2 * rows * cols
    band, tripled, square_half = pl.pallas_call(
        functools.partial(square_kernel, reps, len(pieces)),
        out_shape=(
            jax.ShapeDtypeStruct((grid * rows, cols), jnp.bfloat16),
            jax.ShapeDtypeStruct((rows, cols), jnp.float32),
            jax.ShapeDtypeStruct((rows, cols), jnp.bfloat16),
        ),
        in_specs=[IN_SMEM] * 3 + [IN_VMEM] * (reps + len(pieces)),
        out_specs=(IN_VMEM,) * 3,
        compiler_params=params,
        cost_estimate=pl.CostEstimate(
            flops=product * grid * rows, bytes_accessed=2 * band_bytes, transcendentals=0
        ),
        name="square",
    )(density_pattern, square_pattern, block_order, *panel, *pieces)
    out = tripled
    for shift, half in enumerate([square_half] + shifted(square_half, reps)):
        out = pl.pallas_call(
            functools.partial(cube_kernel, shift),
            out_shape=jax.ShapeDtypeStruct((rows, cols), jnp.float32),
            in_specs=[IN_SMEM] * 2 + [IN_VMEM] * 3,
            out_specs=IN_VMEM,
            compiler_params=params,
            cost_estimate=pl.CostEstimate(
                flops=product * cols, bytes_accessed=band_bytes, transcendentals=0
            ),
            name="cube_part",
        )(cube_pattern, block_order, half, band, out)
    return out


def solution(mesh):
    placed = (P("grid", "rep"), P(), P(), P(), P())
    return jax.shard_map(
        functools.partial(on_device, mesh.shape["grid"], mesh.shape["rep"]),
        mesh=mesh, in_specs=placed, out_specs=P("grid", "rep"), check_vma=False,
    )
```

```python
import functools

import jax
import jax.numpy as jnp
from jax import lax
from jax.experimental import pallas as pl
from jax.experimental.pallas import tpu as pltpu
from jax.sharding import PartitionSpec as P

BLOCK = 128
TILE = 16
IN_SMEM = pl.BlockSpec(memory_space=pltpu.SMEM)
IN_VMEM = pl.BlockSpec(memory_space=pltpu.VMEM)


def factors(size):
    pair = 2 if size % 2 == 0 else 1
    rest = size // pair
    outer = 4 if rest % 4 == 0 else 1
    return outer, rest // outer, pair


def send(value, dims, axis, step):
    outer, inner, pair = dims
    pairs = []
    for source in range(outer * inner * pair):
        place = [source // (inner * pair), source // pair % inner, source % pair]
        place[axis] = (place[axis] + step) % dims[axis]
        pairs.append((source, (place[0] * inner + place[1]) * pair + place[2]))
    return lax.ppermute(value, "grid", pairs)


def source_index(here, key, dims):
    outer, inner, pair = dims
    at = (here // (inner * pair), here // pair % inner, here % pair)
    z, x, c = [lax.rem(a - k + d, d) for a, k, d in zip(at, key, dims)]
    return (z * inner + x) * pair + c


def after(value, *others):
    return lax.optimization_barrier((value,) + others)[0]


def gather_band(own, dims):
    outer, inner, pair = dims
    held = {(0, 0, 0): own}
    steps = sorted(range(1, outer), key=lambda step: min(step, outer - step), reverse=True)
    for step in steps:
        held[step, 0, 0] = send(own, dims, 0, step)
    for step in [0] + steps:
        for hop in range(1, inner):
            held[step, hop, 0] = send(held[step, 0, 0], dims, 1, hop)
    behind = [held[step, 0, 0] for step in steps]
    if steps and inner > 1:
        behind += [held[0, 1, 0], held[steps[0], 1, 0]]
    late = after(own, *behind)
    if pair > 1:
        for key, piece in list(held.items()):
            held[key[:2] + (1,)] = send(after(piece, *behind), dims, 2, 1)
    return held, late


def pick(pattern, order, row_block, col_block):
    return pattern[order[row_block], order[col_block]].astype(jnp.float32)


def rows_mask(pattern, order, first_row, rows, first_col_block, col_blocks):
    top = first_row // BLOCK
    low = (first_row + rows - 1) // BLOCK
    split = (top + 1) * BLOCK - first_row
    upper = lax.broadcasted_iota(jnp.int32, (rows, BLOCK), 0) < split
    tiles = []
    for j in range(col_blocks):
        a = pick(pattern, order, top, first_col_block + j)
        b = pick(pattern, order, low, first_col_block + j)
        tiles.append(jnp.where(upper, a, b))
    return jnp.concatenate(tiles, axis=1)


def keep_blocks(pattern, order, band, first_col):
    row_blocks, col_blocks = band.shape[0] // BLOCK, band.shape[1] // BLOCK

    def keep_row(i, _):
        down = pl.ds(pl.multiple_of(i * BLOCK, BLOCK), BLOCK)
        for j in range(col_blocks):
            keep = pick(pattern, order, i, first_col + j)
            factor = jnp.full((BLOCK, BLOCK), keep, jnp.float32).astype(jnp.bfloat16)
            across = pl.ds(j * BLOCK, BLOCK)
            band[down, across] = band[down, across] * factor
        return 0

    lax.fori_loop(0, row_blocks, keep_row, 0, unroll=row_blocks <= 16)


def square_kernel(reps, keys, dims, *refs):
    density_pattern, square_pattern, order = refs[:3]
    panel = refs[3:3 + reps]
    pieces = refs[3 + reps:3 + reps + len(keys)]
    band, tripled, square_half = refs[3 + reps + len(keys):]
    here, rep = lax.axis_index("grid"), lax.axis_index("rep")
    rows, cols = panel[0].shape
    col_blocks = cols // BLOCK
    first_col = rep * col_blocks
    for key, piece in zip(keys, pieces):
        start = pl.multiple_of(source_index(here, key, dims) * rows, TILE)
        band[pl.ds(start, rows), :] = piece[...]
    keep_blocks(density_pattern, order, band, first_col)
    total = jnp.zeros((rows, cols), jnp.float32)
    for q in range(reps):
        at = lax.rem(rep - q + reps, reps)
        keep = rows_mask(density_pattern, order, here * rows, rows, at * col_blocks, col_blocks)
        left = panel[q][...] * keep.astype(jnp.bfloat16)
        right = band[pl.ds(pl.multiple_of(at * cols, BLOCK), cols), :]
        total += jnp.dot(left, right, preferred_element_type=jnp.float32)
    total *= rows_mask(square_pattern, order, here * rows, rows, first_col, col_blocks)
    tripled[...] = 3.0 * total
    square_half[...] = total.astype(jnp.bfloat16)


def cube_kernel(shift, cube_pattern, order, half, band, before, out):
    here, rep = lax.axis_index("grid"), lax.axis_index("rep")
    reps = lax.axis_size("rep")
    rows, cols = before.shape
    col_blocks = cols // BLOCK
    at = lax.rem(rep - shift + reps, reps)
    right = band[pl.ds(pl.multiple_of(at * cols, BLOCK), cols), :]
    part = jnp.dot(half[...], right, preferred_element_type=jnp.float32)
    keep = rows_mask(cube_pattern, order, here * rows, rows, rep * col_blocks, col_blocks)
    out[...] = before[...] - 2.0 * (part * keep)


def shifted(own, reps):
    return [
        lax.ppermute(own, "rep", [(s, (s + q) % reps) for s in range(reps)])
        for q in range(1, reps)
    ]


def on_device(grid, reps, density, density_pattern, square_pattern, cube_pattern, block_order):
    rows, cols = density.shape
    band_bytes = grid * rows * cols * 2
    room = min(3 * band_bytes + (4 << 20), 56 << 20)
    params = pltpu.CompilerParams(vmem_limit_bytes=room)
    dims = factors(grid)
    held, late = gather_band(density, dims)
    keys = sorted(held)
    panel = [density] + shifted(late, reps)
    product = 2 * rows * cols
    band, tripled, square_half = pl.pallas_call(
        functools.partial(square_kernel, reps, keys, dims),
        out_shape=(
            jax.ShapeDtypeStruct((grid * rows, cols), jnp.bfloat16),
            jax.ShapeDtypeStruct((rows, cols), jnp.float32),
            jax.ShapeDtypeStruct((rows, cols), jnp.bfloat16),
        ),
        in_specs=[IN_SMEM] * 3 + [IN_VMEM] * (reps + len(keys)),
        out_specs=(IN_VMEM,) * 3,
        compiler_params=params,
        cost_estimate=pl.CostEstimate(
            flops=product * grid * rows, bytes_accessed=2 * band_bytes, transcendentals=0
        ),
        name="square",
    )(density_pattern, square_pattern, block_order, *panel, *[held[key] for key in keys])
    out = tripled
    for shift, half in enumerate([square_half] + shifted(square_half, reps)):
        out = pl.pallas_call(
            functools.partial(cube_kernel, shift),
            out_shape=jax.ShapeDtypeStruct((rows, cols), jnp.float32),
            in_specs=[IN_SMEM] * 2 + [IN_VMEM] * 3,
            out_specs=IN_VMEM,
            compiler_params=params,
            cost_estimate=pl.CostEstimate(
                flops=product * cols, bytes_accessed=band_bytes, transcendentals=0
            ),
            name="cube_part",
        )(cube_pattern, block_order, half, band, out)
    return out


def solution(mesh):
    placed = (P("grid", "rep"), P(), P(), P(), P())
    return jax.shard_map(
        functools.partial(on_device, mesh.shape["grid"], mesh.shape["rep"]),
        mesh=mesh, in_specs=placed, out_specs=P("grid", "rep"), check_vma=False,
    )
```

```python
import functools
import math

import jax
import jax.numpy as jnp
from jax import lax
from jax.experimental import pallas as pl
from jax.experimental.pallas import tpu as pltpu
from jax.sharding import PartitionSpec as P

BLOCK = 128
TILE = 16
IN_SMEM = pl.BlockSpec(memory_space=pltpu.SMEM)
IN_VMEM = pl.BlockSpec(memory_space=pltpu.VMEM)


def factors(size):
    pair = 2 if size % 2 == 0 else 1
    rest = size // pair
    outer = 4 if rest % 4 == 0 else 1
    return outer, rest // outer, pair


def partner(place, step, length):
    if length & (length - 1):
        return (place - step) % length
    return place ^ step


def send(value, dims, axis, step):
    outer, inner, pair = dims
    pairs = []
    for target in range(outer * inner * pair):
        place = [target // (inner * pair), target // pair % inner, target % pair]
        place[axis] = partner(place[axis], step, dims[axis])
        pairs.append(((place[0] * inner + place[1]) * pair + place[2], target))
    return lax.ppermute(value, "grid", sorted(pairs))


def source_row(piece, dims, rows):
    outer, inner, pair = dims
    here = lax.axis_index("grid")
    at = (here // (inner * pair), here // pair % inner, here % pair)
    z, x, c = [
        lax.rem(a - k + d, d) if d & (d - 1) else a ^ k for a, k, d in zip(at, piece[:3], dims)
    ]
    return pl.multiple_of(((z * inner + x) * pair + c) * rows + piece[3], TILE)


def after(value, *others):
    return lax.optimization_barrier((value,) + others)[0]


def pick(pattern, order, row_block, col_block):
    return pattern[order[row_block], order[col_block]].astype(jnp.float32)


def rows_mask(pattern, order, first_row, rows, first_col_block, col_blocks):
    top = first_row // BLOCK
    low = (first_row + rows - 1) // BLOCK
    split = (top + 1) * BLOCK - first_row
    upper = lax.broadcasted_iota(jnp.int32, (rows, BLOCK), 0) < split
    tiles = []
    for j in range(col_blocks):
        a = pick(pattern, order, top, first_col_block + j)
        b = pick(pattern, order, low, first_col_block + j)
        tiles.append(jnp.where(upper, a, b))
    return jnp.concatenate(tiles, axis=1)


def prepare_kernel(reps, packed, table, panel_keep, square_keep, cube_keep):
    count = packed.shape[1]
    density_pattern, square_pattern, cube_pattern = [
        packed.at[pl.ds(at * count, count), :] for at in range(3)
    ]
    order = packed.at[3 * count]
    here, rep = lax.axis_index("grid"), lax.axis_index("rep")
    row_blocks, _, cols = table.shape
    rows = square_keep.shape[0]
    col_blocks = cols // BLOCK
    first_col = rep * col_blocks

    def fill(i, _):
        for j in range(col_blocks):
            keep = pick(density_pattern, order, i, first_col + j)
            tile = jnp.full((TILE, BLOCK), keep, jnp.float32).astype(jnp.bfloat16)
            table[i, :, j * BLOCK:(j + 1) * BLOCK] = tile
        return 0

    lax.fori_loop(0, row_blocks, fill, 0, unroll=row_blocks <= 16)
    for q in range(reps):
        at = lax.rem(rep - q + reps, reps) * col_blocks
        keep = rows_mask(density_pattern, order, here * rows, rows, at, col_blocks)
        panel_keep[q] = keep.astype(jnp.bfloat16)
    square_keep[...] = rows_mask(square_pattern, order, here * rows, rows, first_col, col_blocks)
    cube_keep[...] = rows_mask(cube_pattern, order, here * rows, rows, first_col, col_blocks)


def masked_tile(source, at, table, stored_row):
    return source[at:at + TILE, :] * table[stored_row // BLOCK]


def early_kernel(reps, pieces, late, dims, panel_keep, table, *refs):
    panel, held = refs[:reps], refs[reps:reps + len(pieces)]
    left, band, partial = refs[reps + len(pieces):]
    rep = lax.axis_index("rep")
    rows, cols = panel[0].shape
    for q in range(reps):
        at = pl.multiple_of(lax.rem(rep - q + reps, reps) * cols, BLOCK)
        left[:, pl.ds(at, cols)] = panel[q][...] * panel_keep[q] if q else panel[q][...]
    for piece, ref in zip(pieces, held):
        row = source_row(piece, dims, rows)
        for at in range(0, ref.shape[0], TILE):
            tile = masked_tile(ref, at, table, row + at)
            band[pl.ds(pl.multiple_of(row + at, TILE), TILE), :] = tile
    for piece in late:
        count = piece[4] - piece[3]
        band[pl.ds(source_row(piece, dims, rows), count), :] = jnp.zeros((count, cols), band.dtype)
    partial[...] = jnp.dot(left[...], band[...], preferred_element_type=jnp.float32)


def late_kernel(late, dims, table, square_keep, left, old_band, partial, *refs):
    pieces, (band, tripled, square_half, window) = refs[:len(late)], refs[len(late):]
    rows, cols = partial.shape
    pair = dims[2]
    total = partial[...]
    for first in range(0, len(late), pair):
        base = late[first]
        start = source_row(base, dims, rows)
        start = start - lax.rem(start, rows * pair)
        low = jnp.minimum(start // BLOCK * BLOCK, band.shape[0] - window.shape[0])
        low = pl.multiple_of(low, BLOCK)
        window[...] = jnp.zeros(window.shape, window.dtype)
        for piece, ref in zip(late[first:first + pair], pieces[first:first + pair]):
            row = source_row(piece, dims, rows)
            for at in range(0, ref.shape[0], TILE):
                tile = masked_tile(ref, at, table, row + at)
                window[pl.ds(pl.multiple_of(row + at - low, TILE), TILE), :] = tile
                band[pl.ds(pl.multiple_of(row + at, TILE), TILE), :] = tile
        total += jnp.dot(
            left[:, pl.ds(low, window.shape[0])], window[...], preferred_element_type=jnp.float32
        )
    total *= square_keep[...]
    tripled[...] = 3.0 * total
    square_half[...] = total.astype(jnp.bfloat16)


def cube_kernel(shift, keep, half, band, before, out):
    rep, reps = lax.axis_index("rep"), lax.axis_size("rep")
    cols = before.shape[1]
    at = lax.rem(rep - shift + reps, reps)
    right = band[pl.ds(pl.multiple_of(at * cols, BLOCK), cols), :]
    part = jnp.dot(half[...], right, preferred_element_type=jnp.float32)
    out[...] = before[...] - 2.0 * (part * keep[...])


def shifted(own, reps):
    return [
        lax.ppermute(own, "rep", [(s, (s + q) % reps) for s in range(reps)])
        for q in range(1, reps)
    ]


def on_device(grid, reps, density, density_pattern, square_pattern, cube_pattern, block_order):
    rows, cols = density.shape
    order = grid * rows
    dims = factors(grid)
    outer, inner, pair = dims
    band_bytes = order * cols * 2
    room = min(3 * band_bytes + (4 << 20), 56 << 20)
    bf16, f32 = jnp.bfloat16, jnp.float32

    def call(kernel, name, flops, moved, out, operands, spec=IN_VMEM, **more):
        return pl.pallas_call(
            kernel,
            out_shape=[jax.ShapeDtypeStruct(shape, dtype) for shape, dtype in out],
            in_specs=[spec] * len(operands),
            out_specs=[IN_VMEM] * len(out),
            compiler_params=pltpu.CompilerParams(vmem_limit_bytes=room),
            cost_estimate=pl.CostEstimate(flops=flops, bytes_accessed=moved, transcendentals=0),
            name=name,
            **more,
        )(*operands)

    packed = jnp.concatenate(
        [density_pattern, square_pattern, cube_pattern, block_order[None]], axis=0
    )
    table, panel_keep, square_keep, cube_keep = call(
        functools.partial(prepare_kernel, reps), "prepare", 0, 2 * band_bytes,
        [((order // BLOCK, TILE, cols), bf16), ((reps, rows, cols), bf16),
         ((rows, cols), f32), ((rows, cols), f32)],
        [packed], spec=IN_SMEM,
    )

    held = {(0, 0): density}
    steps = sorted(range(1, outer), key=lambda step: (step != outer // 2, step))
    for step in steps:
        held[step, 0] = send(density, dims, 0, step)
    for hop in range(1, inner):
        for step in [0] + steps:
            held[step, hop] = send(after(held[step, 0], table) if step else density, dims, 1, hop)
    last = ([0] + steps)[-1]
    first = [held[steps[0], 0]] if steps else []
    behind = [held[step, 0] for step in steps]
    if steps and inner > 1:
        behind += [held[0, 1], held[steps[0], 1]]
    own = density * panel_keep[0]
    panel = [own] + shifted(after(density, table), reps)

    early, late = [], []
    for (step, hop), value in held.items():
        group = late if hop and step == last else early
        group.append(((step, hop, 0, 0, rows), value if (step, hop) != (0, 0) else own))
        if pair > 1:
            if group is early:
                value = after(value, *([own] + behind if (step, hop) != (0, 0) else first))
            group.append(((step, hop, 1, 0, rows), send(value, dims, 2, 1)))
    late_pieces, late_values = [piece for piece, _ in late], [value for _, value in late]

    left, band, partial = call(
        functools.partial(early_kernel, reps, [piece for piece, _ in early], late_pieces, dims),
        "square_early", 2 * rows * order * cols, 2 * band_bytes,
        [((rows, reps * cols), bf16), ((order, cols), bf16), ((rows, cols), f32)],
        [panel_keep, table, *panel, *[value for _, value in early]],
    )
    span = BLOCK - math.gcd(pair * rows, BLOCK) + pair * rows
    span = min((span + BLOCK - 1) // BLOCK * BLOCK, order)
    band, tripled, square_half = call(
        functools.partial(late_kernel, late_pieces, dims), "square_late",
        2 * rows * span * cols, 4 * rows * cols,
        [((order, cols), bf16), ((rows, cols), f32), ((rows, cols), bf16)],
        [table, square_keep, left, band, partial, *late_values],
        input_output_aliases={3: 0},
        scratch_shapes=[pltpu.VMEM((span, cols), bf16)],
    )
    out = tripled
    for shift, half in enumerate([square_half] + shifted(square_half, reps)):
        (out,) = call(
            functools.partial(cube_kernel, shift), "cube_part",
            2 * rows * cols * cols, band_bytes // reps, [((rows, cols), f32)],
            [cube_keep, half, band, out],
        )
    return out


def solution(mesh):
    placed = (P("grid", "rep"), P(), P(), P(), P())
    return jax.shard_map(
        functools.partial(on_device, mesh.shape["grid"], mesh.shape["rep"]),
        mesh=mesh, in_specs=placed, out_specs=P("grid", "rep"), check_vma=False,
    )
```

```python
import functools
import math

import jax
import jax.numpy as jnp
from jax import lax
from jax.experimental import pallas as pl
from jax.experimental.pallas import tpu as pltpu
from jax.sharding import PartitionSpec as P

BLOCK = 128
TILE = 16
IN_SMEM = pl.BlockSpec(memory_space=pltpu.SMEM)
IN_VMEM = pl.BlockSpec(memory_space=pltpu.VMEM)


def factors(size):
    pair = 2 if size % 2 == 0 else 1
    rest = size // pair
    outer = 4 if rest % 4 == 0 else 1
    return outer, rest // outer, pair


def partner(place, step, length):
    if length & (length - 1):
        return (place - step) % length
    return place ^ step


def send(value, dims, axis, step):
    outer, inner, pair = dims
    pairs = []
    for target in range(outer * inner * pair):
        place = [target // (inner * pair), target // pair % inner, target % pair]
        place[axis] = partner(place[axis], step, dims[axis])
        pairs.append(((place[0] * inner + place[1]) * pair + place[2], target))
    return lax.ppermute(value, "grid", sorted(pairs))


def source_row(piece, dims, rows):
    outer, inner, pair = dims
    here = lax.axis_index("grid")
    at = (here // (inner * pair), here // pair % inner, here % pair)
    z, x, c = [
        lax.rem(a - k + d, d) if d & (d - 1) else a ^ k for a, k, d in zip(at, piece[:3], dims)
    ]
    return pl.multiple_of(((z * inner + x) * pair + c) * rows + piece[3], TILE)


def after(value, *others):
    return lax.optimization_barrier((value,) + others)[0]


def pick(pattern, order, row_block, col_block):
    return pattern[order[row_block], order[col_block]].astype(jnp.float32)


def rows_mask(pattern, order, first_row, rows, first_col_block, col_blocks):
    top = first_row // BLOCK
    low = (first_row + rows - 1) // BLOCK
    split = (top + 1) * BLOCK - first_row
    upper = lax.broadcasted_iota(jnp.int32, (rows, BLOCK), 0) < split
    tiles = []
    for j in range(col_blocks):
        a = pick(pattern, order, top, first_col_block + j)
        b = pick(pattern, order, low, first_col_block + j)
        tiles.append(jnp.where(upper, a, b))
    return jnp.concatenate(tiles, axis=1)


def prepare_kernel(reps, packed, table, panel_keep, square_keep, cube_keep):
    count = packed.shape[1]
    density_pattern, square_pattern, cube_pattern = [
        packed.at[pl.ds(at * count, count), :] for at in range(3)
    ]
    order = packed.at[3 * count]
    here, rep = lax.axis_index("grid"), lax.axis_index("rep")
    row_blocks, _, cols = table.shape
    rows = square_keep.shape[0]
    col_blocks = cols // BLOCK
    first_col = rep * col_blocks

    def fill(i, _):
        for j in range(col_blocks):
            keep = pick(density_pattern, order, i, first_col + j)
            tile = jnp.full((TILE, BLOCK), keep, jnp.float32).astype(jnp.bfloat16)
            table[i, :, j * BLOCK:(j + 1) * BLOCK] = tile
        return 0

    lax.fori_loop(0, row_blocks, fill, 0, unroll=row_blocks <= 16)
    for q in range(reps):
        at = lax.rem(rep - q + reps, reps) * col_blocks
        keep = rows_mask(density_pattern, order, here * rows, rows, at, col_blocks)
        panel_keep[q] = keep.astype(jnp.bfloat16)
    square_keep[...] = rows_mask(square_pattern, order, here * rows, rows, first_col, col_blocks)
    cube_keep[...] = rows_mask(cube_pattern, order, here * rows, rows, first_col, col_blocks)


def masked_tile(source, at, table, stored_row):
    return source[at:at + TILE, :] * table[stored_row // BLOCK]


def early_kernel(reps, pieces, late, dims, panel_keep, table, *refs):
    panel, held = refs[:reps], refs[reps:reps + len(pieces)]
    left, band, partial = refs[reps + len(pieces):]
    rep = lax.axis_index("rep")
    rows, cols = panel[0].shape
    for q in range(reps):
        at = pl.multiple_of(lax.rem(rep - q + reps, reps) * cols, BLOCK)
        left[:, pl.ds(at, cols)] = panel[q][...] * panel_keep[q] if q else panel[q][...]
    for piece, ref in zip(pieces, held):
        row = source_row(piece, dims, rows)
        for at in range(0, ref.shape[0], TILE):
            tile = masked_tile(ref, at, table, row + at)
            band[pl.ds(pl.multiple_of(row + at, TILE), TILE), :] = tile
    for piece in late:
        count = piece[4] - piece[3]
        band[pl.ds(source_row(piece, dims, rows), count), :] = jnp.zeros((count, cols), band.dtype)
    partial[...] = jnp.dot(left[...], band[...], preferred_element_type=jnp.float32)


def late_kernel(late, dims, table, square_keep, left, old_band, partial, *refs):
    pieces, (band, tripled, square_half, window) = refs[:len(late)], refs[len(late):]
    rows, cols = partial.shape
    pair = dims[2]
    total = partial[...]
    for first in range(0, len(late), pair):
        base = late[first]
        start = source_row(base, dims, rows)
        start = start - lax.rem(start, rows * pair)
        low = jnp.minimum(start // BLOCK * BLOCK, band.shape[0] - window.shape[0])
        low = pl.multiple_of(low, BLOCK)
        window[...] = jnp.zeros(window.shape, window.dtype)
        for piece, ref in zip(late[first:first + pair], pieces[first:first + pair]):
            row = source_row(piece, dims, rows)
            for at in range(0, ref.shape[0], TILE):
                tile = masked_tile(ref, at, table, row + at)
                window[pl.ds(pl.multiple_of(row + at - low, TILE), TILE), :] = tile
                band[pl.ds(pl.multiple_of(row + at, TILE), TILE), :] = tile
        total += jnp.dot(
            left[:, pl.ds(low, window.shape[0])], window[...], preferred_element_type=jnp.float32
        )
    total *= square_keep[...]
    tripled[...] = 3.0 * total
    square_half[...] = total.astype(jnp.bfloat16)


def cube_kernel(shift, keep, half, band, before, out):
    rep, reps = lax.axis_index("rep"), lax.axis_size("rep")
    cols = before.shape[1]
    at = lax.rem(rep - shift + reps, reps)
    right = band[pl.ds(pl.multiple_of(at * cols, BLOCK), cols), :]
    part = jnp.dot(half[...], right, preferred_element_type=jnp.float32)
    out[...] = before[...] - 2.0 * (part * keep[...])


def shifted(own, reps):
    return [
        lax.ppermute(own, "rep", [(s, (s + q) % reps) for s in range(reps)])
        for q in range(1, reps)
    ]


def on_device(grid, reps, density, density_pattern, square_pattern, cube_pattern, block_order):
    rows, cols = density.shape
    order = grid * rows
    dims = factors(grid)
    outer, inner, pair = dims
    band_bytes = order * cols * 2
    room = min(3 * band_bytes + (4 << 20), 56 << 20)
    bf16, f32 = jnp.bfloat16, jnp.float32

    def call(kernel, name, flops, moved, out, operands, spec=IN_VMEM, **more):
        return pl.pallas_call(
            kernel,
            out_shape=[jax.ShapeDtypeStruct(shape, dtype) for shape, dtype in out],
            in_specs=[spec] * len(operands),
            out_specs=[IN_VMEM] * len(out),
            compiler_params=pltpu.CompilerParams(vmem_limit_bytes=room),
            cost_estimate=pl.CostEstimate(flops=flops, bytes_accessed=moved, transcendentals=0),
            name=name,
            **more,
        )(*operands)

    steps, hops = list(range(1, outer)), list(range(1, inner))
    last = outer // 2 if steps and hops else None
    before = [step for step in steps if step != last][-1:]

    held = {(0, 0): density}
    for step in steps:
        held[step, 0] = send(density, dims, 0, step)
    for hop in hops:
        held[0, hop] = send(density, dims, 1, hop)
    packed = jnp.concatenate(
        [density_pattern, square_pattern, cube_pattern, block_order[None]], axis=0
    )
    table, panel_keep, square_keep, cube_keep = call(
        functools.partial(prepare_kernel, reps), "prepare", 0, 2 * band_bytes,
        [((order // BLOCK, TILE, cols), bf16), ((reps, rows, cols), bf16),
         ((rows, cols), f32), ((rows, cols), f32)],
        [packed], spec=IN_SMEM,
    )
    for step in steps:
        for hop in hops:
            value = held[step, 0]
            held[step, hop] = send(after(value, table) if step == last else value, dims, 1, hop)
    panel = shifted(density, reps)
    own = density * panel_keep[0]
    behind = panel + [held[step, hop] for step in before for hop in hops[:1]]

    early, late = [], []
    for hop in [0] + hops:
        for step in [0] + steps:
            value = held[step, hop]
            group = late if hop and step == last else early
            group.append(((step, hop, 0, 0, rows), value if step or hop else own))
            if pair > 1:
                if not step or not hop:
                    value = after(value, *behind, *([own] if step == last else []))
                group.append(((step, hop, 1, 0, rows), send(value, dims, 2, 1)))
    panel = [own] + panel
    late_pieces, late_values = [piece for piece, _ in late], [value for _, value in late]

    left, band, partial = call(
        functools.partial(early_kernel, reps, [piece for piece, _ in early], late_pieces, dims),
        "square_early", 2 * rows * order * cols, 2 * band_bytes,
        [((rows, reps * cols), bf16), ((order, cols), bf16), ((rows, cols), f32)],
        [panel_keep, table, *panel, *[value for _, value in early]],
    )
    span = BLOCK - math.gcd(pair * rows, BLOCK) + pair * rows
    span = min((span + BLOCK - 1) // BLOCK * BLOCK, order)
    band, tripled, square_half = call(
        functools.partial(late_kernel, late_pieces, dims), "square_late",
        2 * rows * span * cols, 4 * rows * cols,
        [((order, cols), bf16), ((rows, cols), f32), ((rows, cols), bf16)],
        [table, square_keep, left, band, partial, *late_values],
        input_output_aliases={3: 0},
        scratch_shapes=[pltpu.VMEM((span, cols), bf16)],
    )
    out = tripled
    for shift, half in enumerate([square_half] + shifted(square_half, reps)):
        (out,) = call(
            functools.partial(cube_kernel, shift), "cube_part",
            2 * rows * cols * cols, band_bytes // reps, [((rows, cols), f32)],
            [cube_keep, half, band, out],
        )
    return out


def solution(mesh):
    placed = (P("grid", "rep"), P(), P(), P(), P())
    return jax.shard_map(
        functools.partial(on_device, mesh.shape["grid"], mesh.shape["rep"]),
        mesh=mesh, in_specs=placed, out_specs=P("grid", "rep"), check_vma=False,
    )
```

```python
import functools
import math

import jax
import jax.numpy as jnp
from jax import lax
from jax.experimental import pallas as pl
from jax.experimental.pallas import tpu as pltpu
from jax.sharding import PartitionSpec as P

BLOCK = 128
TILE = 16
IN_SMEM = pl.BlockSpec(memory_space=pltpu.SMEM)
IN_VMEM = pl.BlockSpec(memory_space=pltpu.VMEM)


def factors(size):
    pair = 2 if size % 2 == 0 else 1
    rest = size // pair
    outer = 4 if rest % 4 == 0 else 1
    return outer, rest // outer, pair


def partner(place, step, length):
    if length & (length - 1):
        return (place - step) % length
    return place ^ step


def send(value, dims, axis, step):
    outer, inner, pair = dims
    pairs = []
    for target in range(outer * inner * pair):
        place = [target // (inner * pair), target // pair % inner, target % pair]
        place[axis] = partner(place[axis], step, dims[axis])
        pairs.append(((place[0] * inner + place[1]) * pair + place[2], target))
    return lax.ppermute(value, "grid", sorted(pairs))


def source_row(piece, dims, rows):
    outer, inner, pair = dims
    here = lax.axis_index("grid")
    at = (here // (inner * pair), here // pair % inner, here % pair)
    z, x, c = [
        lax.rem(a - k + d, d) if d & (d - 1) else a ^ k for a, k, d in zip(at, piece[:3], dims)
    ]
    return pl.multiple_of(((z * inner + x) * pair + c) * rows + piece[3], TILE)


def after(value, *others):
    return lax.optimization_barrier((value,) + others)[0]


def pick(pattern, order, row_block, col_block):
    return pattern[order[row_block], order[col_block]].astype(jnp.float32)


def rows_mask(pattern, order, first_row, rows, first_col_block, col_blocks):
    top = first_row // BLOCK
    low = (first_row + rows - 1) // BLOCK
    split = (top + 1) * BLOCK - first_row
    upper = lax.broadcasted_iota(jnp.int32, (rows, BLOCK), 0) < split
    tiles = []
    for j in range(col_blocks):
        a = pick(pattern, order, top, first_col_block + j)
        b = pick(pattern, order, low, first_col_block + j)
        tiles.append(jnp.where(upper, a, b))
    return jnp.concatenate(tiles, axis=1)


def prepare_kernel(reps, packed, table, panel_keep, square_keep, cube_keep):
    count = packed.shape[1]
    density_pattern, square_pattern, cube_pattern = [
        packed.at[pl.ds(at * count, count), :] for at in range(3)
    ]
    order = packed.at[3 * count]
    here, rep = lax.axis_index("grid"), lax.axis_index("rep")
    row_blocks, _, cols = table.shape
    rows = square_keep.shape[0]
    col_blocks = cols // BLOCK
    first_col = rep * col_blocks

    def fill(i, _):
        for j in range(col_blocks):
            keep = pick(density_pattern, order, i, first_col + j)
            tile = jnp.full((TILE, BLOCK), keep, jnp.float32).astype(jnp.bfloat16)
            table[i, :, j * BLOCK:(j + 1) * BLOCK] = tile
        return 0

    lax.fori_loop(0, row_blocks, fill, 0, unroll=row_blocks <= 16)
    for q in range(reps):
        at = lax.rem(rep - q + reps, reps) * col_blocks
        keep = rows_mask(density_pattern, order, here * rows, rows, at, col_blocks)
        panel_keep[q] = keep.astype(jnp.bfloat16)
    square_keep[...] = rows_mask(square_pattern, order, here * rows, rows, first_col, col_blocks)
    cube_keep[...] = rows_mask(cube_pattern, order, here * rows, rows, first_col, col_blocks)


def masked_tile(source, at, table, stored_row):
    return source[at:at + TILE, :] * table[stored_row // BLOCK]


def early_kernel(reps, pieces, late, dims, panel_keep, table, *refs):
    panel, held = refs[:reps], refs[reps:reps + len(pieces)]
    left, band, partial = refs[reps + len(pieces):]
    rep = lax.axis_index("rep")
    rows, cols = panel[0].shape
    for q in range(reps):
        at = pl.multiple_of(lax.rem(rep - q + reps, reps) * cols, BLOCK)
        left[:, pl.ds(at, cols)] = panel[q][...] * panel_keep[q] if q else panel[q][...]
    for piece, ref in zip(pieces, held):
        row = source_row(piece, dims, rows)
        for at in range(0, ref.shape[0], TILE):
            tile = masked_tile(ref, at, table, row + at)
            band[pl.ds(pl.multiple_of(row + at, TILE), TILE), :] = tile
    for piece in late:
        count = piece[4] - piece[3]
        band[pl.ds(source_row(piece, dims, rows), count), :] = jnp.zeros((count, cols), band.dtype)
    partial[...] = jnp.dot(left[...], band[...], preferred_element_type=jnp.float32)


def late_kernel(late, dims, table, square_keep, left, old_band, partial, *refs):
    pieces, (band, tripled, square_half, window) = refs[:len(late)], refs[len(late):]
    rows, cols = partial.shape
    pair = dims[2]
    total = partial[...]
    for first in range(0, len(late), pair):
        base = late[first]
        start = source_row(base, dims, rows)
        start = start - lax.rem(start, rows * pair)
        low = jnp.minimum(start // BLOCK * BLOCK, band.shape[0] - window.shape[0])
        low = pl.multiple_of(low, BLOCK)
        window[...] = jnp.zeros(window.shape, window.dtype)
        for piece, ref in zip(late[first:first + pair], pieces[first:first + pair]):
            row = source_row(piece, dims, rows)
            for at in range(0, ref.shape[0], TILE):
                tile = masked_tile(ref, at, table, row + at)
                window[pl.ds(pl.multiple_of(row + at - low, TILE), TILE), :] = tile
                band[pl.ds(pl.multiple_of(row + at, TILE), TILE), :] = tile
        total += jnp.dot(
            left[:, pl.ds(low, window.shape[0])], window[...], preferred_element_type=jnp.float32
        )
    total *= square_keep[...]
    tripled[...] = 3.0 * total
    square_half[...] = total.astype(jnp.bfloat16)


def cube_kernel(shift, keep, half, band, before, out):
    rep, reps = lax.axis_index("rep"), lax.axis_size("rep")
    cols = before.shape[1]
    at = lax.rem(rep - shift + reps, reps)
    right = band[pl.ds(pl.multiple_of(at * cols, BLOCK), cols), :]
    part = jnp.dot(half[...], right, preferred_element_type=jnp.float32)
    out[...] = before[...] - 2.0 * (part * keep[...])


def shifted(own, reps):
    return [
        lax.ppermute(own, "rep", [(s, (s + q) % reps) for s in range(reps)])
        for q in range(1, reps)
    ]


def on_device(grid, reps, density, density_pattern, square_pattern, cube_pattern, block_order):
    rows, cols = density.shape
    order = grid * rows
    dims = factors(grid)
    outer, inner, pair = dims
    band_bytes = order * cols * 2
    room = min(3 * band_bytes + (4 << 20), 56 << 20)
    bf16, f32 = jnp.bfloat16, jnp.float32

    def call(kernel, name, flops, moved, out, operands, spec=IN_VMEM, **more):
        return pl.pallas_call(
            kernel,
            out_shape=[jax.ShapeDtypeStruct(shape, dtype) for shape, dtype in out],
            in_specs=[spec] * len(operands),
            out_specs=[IN_VMEM] * len(out),
            compiler_params=pltpu.CompilerParams(vmem_limit_bytes=room),
            cost_estimate=pl.CostEstimate(flops=flops, bytes_accessed=moved, transcendentals=0),
            name=name,
            **more,
        )(*operands)

    steps, hops = list(range(1, outer)), list(range(1, inner))
    last = outer // 2 if steps and hops else None
    before = [step for step in steps if step != last][-1:]

    held = {(0, 0): density}
    for step in steps:
        held[step, 0] = send(after(density), dims, 0, step)
    for hop in hops:
        held[0, hop] = send(after(density), dims, 1, hop)
    packed = jnp.concatenate(
        [density_pattern, square_pattern, cube_pattern, after(block_order)[None]], axis=0
    )
    table, panel_keep, square_keep, cube_keep = call(
        functools.partial(prepare_kernel, reps), "prepare", 0, 2 * band_bytes,
        [((order // BLOCK, TILE, cols), bf16), ((reps, rows, cols), bf16),
         ((rows, cols), f32), ((rows, cols), f32)],
        [packed], spec=IN_SMEM,
    )
    for step in steps:
        for hop in hops:
            ready = [table] if step == last else []
            held[step, hop] = send(after(held[step, 0], *ready), dims, 1, hop)
    panel = shifted(after(density), reps)
    own = density * after(panel_keep)[0]

    behind = panel + [held[step, hop] for step in before for hop in hops[:1]]
    crossed = {(0, 0): after(density, *behind)}
    for step in steps:
        for hop in hops:
            crossed[step, hop] = after(held[step, hop])
    paired = {}
    if pair > 1:
        for key, value in crossed.items():
            paired[key] = send(value, dims, 2, 1)
        behind = behind + [
            value for (step, hop), value in paired.items() if step != last and hop < 2
        ]
        for key, value in held.items():
            if key not in paired:
                ready = behind + ([own] if key[0] == last else [])
                paired[key] = send(after(value, *ready), dims, 2, 1)

    early, late = [], []
    for hop in [0] + hops:
        for step in [0] + steps:
            key = (step, hop)
            group = late if hop and step == last else early
            group.append(((step, hop, 0, 0, rows), held[key] if step or hop else own))
            if pair > 1:
                group.append(((step, hop, 1, 0, rows), paired[key]))
    panel = [own] + panel
    late_pieces, late_values = [piece for piece, _ in late], [value for _, value in late]

    left, band, partial = call(
        functools.partial(early_kernel, reps, [piece for piece, _ in early], late_pieces, dims),
        "square_early", 2 * rows * order * cols, 2 * band_bytes,
        [((rows, reps * cols), bf16), ((order, cols), bf16), ((rows, cols), f32)],
        [panel_keep, table, *panel, *[value for _, value in early]],
    )
    span = BLOCK - math.gcd(pair * rows, BLOCK) + pair * rows
    span = min((span + BLOCK - 1) // BLOCK * BLOCK, order)
    band, tripled, square_half = call(
        functools.partial(late_kernel, late_pieces, dims), "square_late",
        2 * rows * span * cols, 4 * rows * cols,
        [((order, cols), bf16), ((rows, cols), f32), ((rows, cols), bf16)],
        [table, square_keep, left, band, partial, *late_values],
        input_output_aliases={3: 0},
        scratch_shapes=[pltpu.VMEM((span, cols), bf16)],
    )
    out = tripled
    for shift, half in enumerate([square_half] + shifted(square_half, reps)):
        (out,) = call(
            functools.partial(cube_kernel, shift), "cube_part",
            2 * rows * cols * cols, band_bytes // reps, [((rows, cols), f32)],
            [cube_keep, half, band, out],
        )
    return out


def solution(mesh):
    placed = (P("grid", "rep"), P(), P(), P(), P())
    return jax.shard_map(
        functools.partial(on_device, mesh.shape["grid"], mesh.shape["rep"]),
        mesh=mesh, in_specs=placed, out_specs=P("grid", "rep"), check_vma=False,
    )
```

```python
import functools
import math

import jax
import jax.numpy as jnp
from jax import lax
from jax.experimental import pallas as pl
from jax.experimental.pallas import tpu as pltpu
from jax.sharding import PartitionSpec as P

BLOCK = 128
TILE = 16
PLACE = 10**9
IN_SMEM = pl.BlockSpec(memory_space=pltpu.SMEM)
IN_VMEM = pl.BlockSpec(memory_space=pltpu.VMEM)


def factors(size):
    pair = 2 if size % 2 == 0 else 1
    rest = size // pair
    outer = 4 if rest % 4 == 0 else 1
    return outer, rest // outer, pair


def partner(place, step, length):
    if length & (length - 1):
        return (place - step) % length
    return place ^ step


def send(value, dims, axis, step):
    outer, inner, pair = dims
    pairs = []
    for target in range(outer * inner * pair):
        place = [target // (inner * pair), target // pair % inner, target % pair]
        place[axis] = partner(place[axis], step, dims[axis])
        pairs.append(((place[0] * inner + place[1]) * pair + place[2], target))
    return lax.ppermute(value, "grid", sorted(pairs))


def source_row(piece, dims, rows):
    outer, inner, pair = dims
    here = lax.axis_index("grid")
    at = (here // (inner * pair), here // pair % inner, here % pair)
    z, x, c = [
        lax.rem(a - k + d, d) if d & (d - 1) else a ^ k for a, k, d in zip(at, piece[:3], dims)
    ]
    return pl.multiple_of(((z * inner + x) * pair + c) * rows + piece[3], TILE)


def after(value, *others):
    return lax.optimization_barrier((value,) + others)[0]


def pick(pattern, order, row_block, col_block):
    return pattern[order[row_block], order[col_block]].astype(jnp.float32)


def rows_mask(pattern, order, first_row, rows, first_col_block, col_blocks):
    top = first_row // BLOCK
    low = (first_row + rows - 1) // BLOCK
    split = (top + 1) * BLOCK - first_row
    upper = lax.broadcasted_iota(jnp.int32, (rows, BLOCK), 0) < split
    tiles = []
    for j in range(col_blocks):
        a = pick(pattern, order, top, first_col_block + j)
        b = pick(pattern, order, low, first_col_block + j)
        tiles.append(jnp.where(upper, a, b))
    return jnp.concatenate(tiles, axis=1)


def parts_of(packed):
    count = packed.shape[1]
    patterns = [packed.at[pl.ds(at * count, count), :] for at in range(3)]
    return (*patterns, packed.at[3 * count])


def prepare_kernel(reps, packed, density, own, table, panel_keep):
    density_pattern, _, _, order = parts_of(packed)
    here, rep = lax.axis_index("grid"), lax.axis_index("rep")
    row_blocks, _, cols = table.shape
    rows = own.shape[0]
    col_blocks = cols // BLOCK
    first_col = rep * col_blocks

    def fill(i, _):
        for j in range(col_blocks):
            keep = pick(density_pattern, order, i, first_col + j)
            tile = jnp.full((TILE, BLOCK), keep, jnp.float32).astype(jnp.bfloat16)
            table[i, :, j * BLOCK:(j + 1) * BLOCK] = tile
        return 0

    lax.fori_loop(0, row_blocks, fill, 0, unroll=row_blocks <= 16)
    for q in range(1, reps):
        at = lax.rem(rep - q + reps, reps) * col_blocks
        keep = rows_mask(density_pattern, order, here * rows, rows, at, col_blocks)
        panel_keep[q - 1] = keep.astype(jnp.bfloat16)
    for at in range(0, rows, TILE):
        own[at:at + TILE, :] = masked_tile(density, at, table, here * rows + at)


def products_kernel(packed, square_keep, cube_keep):
    _, square_pattern, cube_pattern, order = parts_of(packed)
    here, rep = lax.axis_index("grid"), lax.axis_index("rep")
    rows, cols = square_keep.shape
    col_blocks = cols // BLOCK
    for pattern, keep in ((square_pattern, square_keep), (cube_pattern, cube_keep)):
        keep[...] = rows_mask(pattern, order, here * rows, rows, rep * col_blocks, col_blocks)


def masked_tile(source, at, table, stored_row):
    return source[at:at + TILE, :] * table[stored_row // BLOCK]


def early_kernel(reps, pieces, late, dims, panel_keep, table, *refs):
    panel, held = refs[:reps], refs[reps:reps + len(pieces)]
    left, band, partial = refs[reps + len(pieces):]
    rep = lax.axis_index("rep")
    rows, cols = panel[0].shape
    for q in range(reps):
        at = pl.multiple_of(lax.rem(rep - q + reps, reps) * cols, BLOCK)
        left[:, pl.ds(at, cols)] = panel[q][...] * panel_keep[q - 1] if q else panel[q][...]
    for piece, ref in zip(pieces, held):
        row = source_row(piece, dims, rows)
        for at in range(0, ref.shape[0], TILE):
            tile = masked_tile(ref, at, table, row + at)
            band[pl.ds(pl.multiple_of(row + at, TILE), TILE), :] = tile
    for piece in late:
        count = piece[4] - piece[3]
        band[pl.ds(source_row(piece, dims, rows), count), :] = jnp.zeros((count, cols), band.dtype)
    partial[...] = jnp.dot(left[...], band[...], preferred_element_type=jnp.float32)


def late_kernel(late, dims, table, square_keep, left, old_band, partial, *refs):
    pieces, (band, tripled, square_half, window) = refs[:len(late)], refs[len(late):]
    rows, cols = partial.shape
    pair = dims[2]
    total = partial[...]
    for first in range(0, len(late), pair):
        base = late[first]
        start = source_row(base, dims, rows)
        start = start - lax.rem(start, rows * pair)
        low = jnp.minimum(start // BLOCK * BLOCK, band.shape[0] - window.shape[0])
        low = pl.multiple_of(low, BLOCK)
        window[...] = jnp.zeros(window.shape, window.dtype)
        for piece, ref in zip(late[first:first + pair], pieces[first:first + pair]):
            row = source_row(piece, dims, rows)
            for at in range(0, ref.shape[0], TILE):
                tile = masked_tile(ref, at, table, row + at)
                window[pl.ds(pl.multiple_of(row + at - low, TILE), TILE), :] = tile
                band[pl.ds(pl.multiple_of(row + at, TILE), TILE), :] = tile
        total += jnp.dot(
            left[:, pl.ds(low, window.shape[0])], window[...], preferred_element_type=jnp.float32
        )
    total *= square_keep[...]
    tripled[...] = 3.0 * total
    square_half[...] = total.astype(jnp.bfloat16)


def cube_kernel(shift, keep, half, band, before, out):
    rep, reps = lax.axis_index("rep"), lax.axis_size("rep")
    cols = before.shape[1]
    at = lax.rem(rep - shift + reps, reps)
    right = band[pl.ds(pl.multiple_of(at * cols, BLOCK), cols), :]
    part = jnp.dot(half[...], right, preferred_element_type=jnp.float32)
    out[...] = before[...] - 2.0 * (part * keep[...])


def shifted(own, reps):
    return [
        lax.ppermute(own, "rep", [(s, (s + q) % reps) for s in range(reps)])
        for q in range(1, reps)
    ]


def on_device(grid, reps, density, density_pattern, square_pattern, cube_pattern, block_order):
    rows, cols = density.shape
    order = grid * rows
    dims = factors(grid)
    outer, inner, pair = dims
    band_bytes = order * cols * 2
    room = min(3 * band_bytes + (4 << 20), 56 << 20)
    bf16, f32 = jnp.bfloat16, jnp.float32

    def call(kernel, name, flops, moved, out, operands, spec=None, **more):
        return pl.pallas_call(
            kernel,
            out_shape=[jax.ShapeDtypeStruct(shape, dtype) for shape, dtype in out],
            in_specs=spec or [IN_VMEM] * len(operands),
            out_specs=[IN_VMEM] * len(out),
            compiler_params=pltpu.CompilerParams(vmem_limit_bytes=room),
            cost_estimate=pl.CostEstimate(flops=flops, bytes_accessed=moved, transcendentals=0),
            name=name,
            **more,
        )(*operands)

    steps, hops = list(range(1, outer)), list(range(1, inner))
    last = outer // 2 if steps and hops else None
    before = [step for step in steps if step != last][-1:]

    held = {(0, 0): density}
    for step in steps:
        held[step, 0] = send(after(density), dims, 0, step)
    for hop in hops:
        held[0, hop] = send(after(density), dims, 1, hop)
    packed = jnp.concatenate(
        [density_pattern, square_pattern, cube_pattern, after(block_order)[None]], axis=0
    )
    own, table, panel_keep = call(
        functools.partial(prepare_kernel, reps), "prepare", PLACE, 2 * band_bytes,
        [((rows, cols), bf16), ((order // BLOCK, TILE, cols), bf16),
         ((max(reps - 1, 1), rows, cols), bf16)],
        [packed, after(density)], spec=[IN_SMEM, IN_VMEM],
    )
    for step in steps:
        for hop in hops:
            ready = [table] if step == last else []
            held[step, hop] = send(after(held[step, 0], *ready), dims, 1, hop)
    panel = shifted(after(density), reps)
    square_keep, cube_keep = call(
        products_kernel, "products", 2 * PLACE, 2 * band_bytes, [((rows, cols), f32)] * 2,
        [after(packed)], spec=[IN_SMEM],
    )

    behind = panel + [held[step, hop] for step in before for hop in hops[:1]]
    crossed = {(0, 0): after(density, *behind)}
    for step in steps:
        for hop in hops:
            crossed[step, hop] = after(held[step, hop])
    paired = {}
    if pair > 1:
        for key, value in crossed.items():
            paired[key] = send(value, dims, 2, 1)
        behind = behind + [
            value for (step, hop), value in paired.items() if step != last and hop < 2
        ]
        for key, value in held.items():
            if key not in paired:
                ready = behind + ([square_keep] if key[0] == last else [])
                paired[key] = send(after(value, *ready), dims, 2, 1)

    early, late = [], []
    for hop in [0] + hops:
        for step in [0] + steps:
            key = (step, hop)
            group = late if hop and step == last else early
            group.append(((step, hop, 0, 0, rows), held[key] if step or hop else own))
            if pair > 1:
                group.append(((step, hop, 1, 0, rows), paired[key]))
    panel = [own] + panel
    late_pieces, late_values = [piece for piece, _ in late], [value for _, value in late]

    left, band, partial = call(
        functools.partial(early_kernel, reps, [piece for piece, _ in early], late_pieces, dims),
        "square_early", 2 * rows * order * cols, 2 * band_bytes,
        [((rows, reps * cols), bf16), ((order, cols), bf16), ((rows, cols), f32)],
        [panel_keep, table, *panel, *[value for _, value in early]],
    )
    span = BLOCK - math.gcd(pair * rows, BLOCK) + pair * rows
    span = min((span + BLOCK - 1) // BLOCK * BLOCK, order)
    band, tripled, square_half = call(
        functools.partial(late_kernel, late_pieces, dims), "square_late",
        2 * rows * span * cols, 4 * rows * cols,
        [((order, cols), bf16), ((rows, cols), f32), ((rows, cols), bf16)],
        [table, square_keep, left, band, partial, *late_values],
        input_output_aliases={3: 0},
        scratch_shapes=[pltpu.VMEM((span, cols), bf16)],
    )
    out = tripled
    for shift, half in enumerate([square_half] + shifted(square_half, reps)):
        (out,) = call(
            functools.partial(cube_kernel, shift), "cube_part",
            2 * rows * cols * cols, band_bytes // reps, [((rows, cols), f32)],
            [cube_keep, half, band, out],
        )
    return out


def solution(mesh):
    placed = (P("grid", "rep"), P(), P(), P(), P())
    return jax.shard_map(
        functools.partial(on_device, mesh.shape["grid"], mesh.shape["rep"]),
        mesh=mesh, in_specs=placed, out_specs=P("grid", "rep"), check_vma=False,
    )
```

```python
import functools
import math

import jax
import jax.numpy as jnp
from jax import lax
from jax.experimental import pallas as pl
from jax.experimental.pallas import tpu as pltpu
from jax.sharding import PartitionSpec as P

BLOCK = 128
TILE = 16
PLACE = 10**9
IN_SMEM = pl.BlockSpec(memory_space=pltpu.SMEM)
IN_VMEM = pl.BlockSpec(memory_space=pltpu.VMEM)


def factors(size):
    pair = 2 if size % 2 == 0 else 1
    rest = size // pair
    outer = 4 if rest % 4 == 0 else 1
    return outer, rest // outer, pair


def partner(place, step, length):
    if length & (length - 1):
        return (place - step) % length
    return place ^ step


def send(value, dims, axis, step):
    outer, inner, pair = dims
    pairs = []
    for target in range(outer * inner * pair):
        place = [target // (inner * pair), target // pair % inner, target % pair]
        place[axis] = partner(place[axis], step, dims[axis])
        pairs.append(((place[0] * inner + place[1]) * pair + place[2], target))
    return lax.ppermute(value, "grid", sorted(pairs))


def source_row(piece, dims, rows):
    outer, inner, pair = dims
    here = lax.axis_index("grid")
    at = (here // (inner * pair), here // pair % inner, here % pair)
    z, x, c = [
        lax.rem(a - k + d, d) if d & (d - 1) else a ^ k for a, k, d in zip(at, piece[:3], dims)
    ]
    return pl.multiple_of(((z * inner + x) * pair + c) * rows + piece[3], TILE)


def after(value, *others):
    return lax.optimization_barrier((value,) + others)[0]


def pick(pattern, order, row_block, col_block):
    return pattern[order[row_block], order[col_block]].astype(jnp.float32)


def rows_mask(pattern, order, first_row, rows, first_col_block, col_blocks):
    top = first_row // BLOCK
    low = (first_row + rows - 1) // BLOCK
    split = (top + 1) * BLOCK - first_row
    upper = lax.broadcasted_iota(jnp.int32, (rows, BLOCK), 0) < split
    tiles = []
    for j in range(col_blocks):
        a = pick(pattern, order, top, first_col_block + j)
        b = pick(pattern, order, low, first_col_block + j)
        tiles.append(jnp.where(upper, a, b))
    return jnp.concatenate(tiles, axis=1)


def parts_of(packed):
    count = packed.shape[1]
    patterns = [packed.at[pl.ds(at * count, count), :] for at in range(3)]
    return (*patterns, packed.at[3 * count])


def prepare_kernel(reps, packed, table, panel_keep, square_keep, cube_keep):
    density_pattern, square_pattern, cube_pattern, order = parts_of(packed)
    here, rep = lax.axis_index("grid"), lax.axis_index("rep")
    row_blocks, _, cols = table.shape
    rows = square_keep.shape[0]
    col_blocks = cols // BLOCK
    first_col = rep * col_blocks

    def fill(i, _):
        for j in range(col_blocks):
            keep = pick(density_pattern, order, i, first_col + j)
            tile = jnp.full((TILE, BLOCK), keep, jnp.float32).astype(jnp.bfloat16)
            table[i, :, j * BLOCK:(j + 1) * BLOCK] = tile
        return 0

    lax.fori_loop(0, row_blocks, fill, 0, unroll=row_blocks <= 16)
    for q in range(reps):
        at = lax.rem(rep - q + reps, reps) * col_blocks
        keep = rows_mask(density_pattern, order, here * rows, rows, at, col_blocks)
        panel_keep[q] = keep.astype(jnp.bfloat16)
    for pattern, keep in ((square_pattern, square_keep), (cube_pattern, cube_keep)):
        keep[...] = rows_mask(pattern, order, here * rows, rows, first_col, col_blocks)


def panel_kernel(reps, panel_keep, *refs):
    panel, (left, own) = refs[:reps], refs[reps:]
    rep = lax.axis_index("rep")
    cols = panel[0].shape[1]
    for q in range(reps):
        at = pl.multiple_of(lax.rem(rep - q + reps, reps) * cols, BLOCK)
        part = panel[q][...] * panel_keep[q]
        left[:, pl.ds(at, cols)] = part
        if q == 0:
            own[...] = part


def masked_tile(source, at, table, stored_row):
    return source[at:at + TILE, :] * table[stored_row // BLOCK]


def early_kernel(pieces, late, dims, left, table, *refs):
    held, (band, partial) = refs[:len(pieces)], refs[len(pieces):]
    rows, cols = partial.shape
    for piece, ref in zip(pieces, held):
        row = source_row(piece, dims, rows)
        for at in range(0, ref.shape[0], TILE):
            tile = masked_tile(ref, at, table, row + at)
            band[pl.ds(pl.multiple_of(row + at, TILE), TILE), :] = tile
    for piece in late:
        count = piece[4] - piece[3]
        band[pl.ds(source_row(piece, dims, rows), count), :] = jnp.zeros((count, cols), band.dtype)
    partial[...] = jnp.dot(left[...], band[...], preferred_element_type=jnp.float32)


def late_kernel(late, dims, table, square_keep, left, old_band, partial, *refs):
    pieces, (band, tripled, square_half, window) = refs[:len(late)], refs[len(late):]
    rows, cols = partial.shape
    pair = dims[2]
    total = partial[...]
    for first in range(0, len(late), pair):
        base = late[first]
        start = source_row(base, dims, rows)
        start = start - lax.rem(start, rows * pair)
        low = jnp.minimum(start // BLOCK * BLOCK, band.shape[0] - window.shape[0])
        low = pl.multiple_of(low, BLOCK)
        window[...] = jnp.zeros(window.shape, window.dtype)
        for piece, ref in zip(late[first:first + pair], pieces[first:first + pair]):
            row = source_row(piece, dims, rows)
            for at in range(0, ref.shape[0], TILE):
                tile = masked_tile(ref, at, table, row + at)
                window[pl.ds(pl.multiple_of(row + at - low, TILE), TILE), :] = tile
                band[pl.ds(pl.multiple_of(row + at, TILE), TILE), :] = tile
        total += jnp.dot(
            left[:, pl.ds(low, window.shape[0])], window[...], preferred_element_type=jnp.float32
        )
    total *= square_keep[...]
    tripled[...] = 3.0 * total
    square_half[...] = total.astype(jnp.bfloat16)


def cube_kernel(shift, keep, half, band, before, out):
    rep, reps = lax.axis_index("rep"), lax.axis_size("rep")
    cols = before.shape[1]
    at = lax.rem(rep - shift + reps, reps)
    right = band[pl.ds(pl.multiple_of(at * cols, BLOCK), cols), :]
    part = jnp.dot(half[...], right, preferred_element_type=jnp.float32)
    out[...] = before[...] - 2.0 * (part * keep[...])


def shifted(own, reps):
    return [
        lax.ppermute(own, "rep", [(s, (s + q) % reps) for s in range(reps)])
        for q in range(1, reps)
    ]


def on_device(grid, reps, density, density_pattern, square_pattern, cube_pattern, block_order):
    rows, cols = density.shape
    order = grid * rows
    dims = factors(grid)
    outer, inner, pair = dims
    band_bytes = order * cols * 2
    room = min(3 * band_bytes + (4 << 20), 56 << 20)
    bf16, f32 = jnp.bfloat16, jnp.float32

    def call(kernel, name, flops, moved, out, operands, spec=None, **more):
        return pl.pallas_call(
            kernel,
            out_shape=[jax.ShapeDtypeStruct(shape, dtype) for shape, dtype in out],
            in_specs=spec or [IN_VMEM] * len(operands),
            out_specs=[IN_VMEM] * len(out),
            compiler_params=pltpu.CompilerParams(vmem_limit_bytes=room),
            cost_estimate=pl.CostEstimate(flops=flops, bytes_accessed=moved, transcendentals=0),
            name=name,
            **more,
        )(*operands)

    steps, hops = list(range(1, outer)), list(range(1, inner))
    last = outer // 2 if steps and hops else None
    before = [step for step in steps if step != last][-1:]

    held = {(0, 0): density}
    for step in steps:
        held[step, 0] = send(after(density), dims, 0, step)
    for hop in hops:
        held[0, hop] = send(after(density), dims, 1, hop)
    packed = jnp.concatenate(
        [density_pattern, square_pattern, cube_pattern, after(block_order)[None]], axis=0
    )
    table, panel_keep, square_keep, cube_keep = call(
        functools.partial(prepare_kernel, reps), "prepare", PLACE, 2 * band_bytes,
        [((order // BLOCK, TILE, cols), bf16), ((reps, rows, cols), bf16),
         ((rows, cols), f32), ((rows, cols), f32)],
        [packed], spec=[IN_SMEM],
    )
    for step in steps:
        for hop in hops:
            ready = [table] if step == last else []
            held[step, hop] = send(after(held[step, 0], *ready), dims, 1, hop)
    panel = shifted(after(density), reps)
    left, own = call(
        functools.partial(panel_kernel, reps), "panel", 2 * PLACE, 2 * band_bytes,
        [((rows, reps * cols), bf16), ((rows, cols), bf16)],
        [panel_keep, after(density), *panel],
    )

    behind = panel + [held[step, hop] for step in before for hop in hops[:1]]
    crossed = {(0, 0): after(density, *behind)}
    for step in steps:
        for hop in hops:
            crossed[step, hop] = after(held[step, hop])
    paired = {}
    if pair > 1:
        for key, value in crossed.items():
            paired[key] = send(value, dims, 2, 1)
        behind = behind + [
            value for (step, hop), value in paired.items() if step != last and hop < 2
        ]
        for key, value in held.items():
            if key not in paired:
                ready = behind + ([left] if key[0] == last else [])
                paired[key] = send(after(value, *ready), dims, 2, 1)

    early, late = [], []
    for hop in [0] + hops:
        for step in [0] + steps:
            key = (step, hop)
            group = late if hop and step == last else early
            group.append(((step, hop, 0, 0, rows), held[key] if step or hop else own))
            if pair > 1:
                group.append(((step, hop, 1, 0, rows), paired[key]))
    late_pieces, late_values = [piece for piece, _ in late], [value for _, value in late]

    band, partial = call(
        functools.partial(early_kernel, [piece for piece, _ in early], late_pieces, dims),
        "square_early", 2 * rows * order * cols, 2 * band_bytes,
        [((order, cols), bf16), ((rows, cols), f32)],
        [left, table, *[value for _, value in early]],
    )
    span = BLOCK - math.gcd(pair * rows, BLOCK) + pair * rows
    span = min((span + BLOCK - 1) // BLOCK * BLOCK, order)
    band, tripled, square_half = call(
        functools.partial(late_kernel, late_pieces, dims), "square_late",
        2 * rows * span * cols, 4 * rows * cols,
        [((order, cols), bf16), ((rows, cols), f32), ((rows, cols), bf16)],
        [table, square_keep, left, band, partial, *late_values],
        input_output_aliases={3: 0},
        scratch_shapes=[pltpu.VMEM((span, cols), bf16)],
    )
    out = tripled
    for shift, half in enumerate([square_half] + shifted(square_half, reps)):
        (out,) = call(
            functools.partial(cube_kernel, shift), "cube_part",
            2 * rows * cols * cols, band_bytes // reps, [((rows, cols), f32)],
            [cube_keep, half, band, out],
        )
    return out


def solution(mesh):
    placed = (P("grid", "rep"), P(), P(), P(), P())
    return jax.shard_map(
        functools.partial(on_device, mesh.shape["grid"], mesh.shape["rep"]),
        mesh=mesh, in_specs=placed, out_specs=P("grid", "rep"), check_vma=False,
    )
```

```python
import functools
import math

import jax
import jax.numpy as jnp
from jax import lax
from jax.experimental import pallas as pl
from jax.experimental.pallas import tpu as pltpu
from jax.sharding import PartitionSpec as P

BLOCK = 128
TILE = 16
PLACE = 10**9
IN_SMEM = pl.BlockSpec(memory_space=pltpu.SMEM)
IN_VMEM = pl.BlockSpec(memory_space=pltpu.VMEM)


def factors(size):
    pair = 2 if size % 2 == 0 else 1
    rest = size // pair
    outer = 4 if rest % 4 == 0 else 1
    return outer, rest // outer, pair


def partner(place, step, length):
    if length & (length - 1):
        return (place - step) % length
    return place ^ step


def send(value, dims, axis, step):
    outer, inner, pair = dims
    pairs = []
    for target in range(outer * inner * pair):
        place = [target // (inner * pair), target // pair % inner, target % pair]
        place[axis] = partner(place[axis], step, dims[axis])
        pairs.append(((place[0] * inner + place[1]) * pair + place[2], target))
    return lax.ppermute(value, "grid", sorted(pairs))


def source_row(piece, dims, rows):
    outer, inner, pair = dims
    here = lax.axis_index("grid")
    at = (here // (inner * pair), here // pair % inner, here % pair)
    z, x, c = [
        lax.rem(a - k + d, d) if d & (d - 1) else a ^ k for a, k, d in zip(at, piece[:3], dims)
    ]
    return pl.multiple_of(((z * inner + x) * pair + c) * rows + piece[3], TILE)


def after(value, *others):
    return lax.optimization_barrier((value,) + others)[0]


def pick(pattern, order, row_block, col_block):
    return pattern[order[row_block], order[col_block]].astype(jnp.float32)


def rows_mask(pattern, order, first_row, rows, first_col_block, col_blocks):
    top = first_row // BLOCK
    low = (first_row + rows - 1) // BLOCK
    split = (top + 1) * BLOCK - first_row
    upper = lax.broadcasted_iota(jnp.int32, (rows, BLOCK), 0) < split
    tiles = []
    for j in range(col_blocks):
        a = pick(pattern, order, top, first_col_block + j)
        b = pick(pattern, order, low, first_col_block + j)
        tiles.append(jnp.where(upper, a, b))
    return jnp.concatenate(tiles, axis=1)


def parts_of(packed):
    count = packed.shape[1]
    patterns = [packed.at[pl.ds(at * count, count), :] for at in range(3)]
    return (*patterns, packed.at[3 * count])


def prepare_kernel(reps, packed, table, panel_keep, square_keep, cube_keep):
    density_pattern, square_pattern, cube_pattern, order = parts_of(packed)
    here, rep = lax.axis_index("grid"), lax.axis_index("rep")
    row_blocks, _, cols = table.shape
    rows = square_keep.shape[0]
    col_blocks = cols // BLOCK
    first_col = rep * col_blocks

    def fill(i, _):
        for j in range(col_blocks):
            keep = pick(density_pattern, order, i, first_col + j)
            tile = jnp.full((TILE, BLOCK), keep, jnp.float32).astype(jnp.bfloat16)
            table[i, :, j * BLOCK:(j + 1) * BLOCK] = tile
        return 0

    lax.fori_loop(0, row_blocks, fill, 0, unroll=row_blocks <= 16)
    for q in range(reps):
        at = lax.rem(rep - q + reps, reps) * col_blocks
        keep = rows_mask(density_pattern, order, here * rows, rows, at, col_blocks)
        panel_keep[q] = keep.astype(jnp.bfloat16)
    for pattern, keep in ((square_pattern, square_keep), (cube_pattern, cube_keep)):
        keep[...] = rows_mask(pattern, order, here * rows, rows, first_col, col_blocks)


def panel_kernel(reps, panel_keep, *refs):
    panel, (left, own) = refs[:reps], refs[reps:]
    rep = lax.axis_index("rep")
    cols = panel[0].shape[1]
    for q in range(reps):
        at = pl.multiple_of(lax.rem(rep - q + reps, reps) * cols, BLOCK)
        part = panel[q][...] * panel_keep[q]
        left[:, pl.ds(at, cols)] = part
        if q == 0:
            own[...] = part


def masked_tile(source, at, table, stored_row):
    return source[at:at + TILE, :] * table[stored_row // BLOCK]


def early_kernel(pieces, late, dims, left, table, *refs):
    held, (band, partial) = refs[:len(pieces)], refs[len(pieces):]
    rows, cols = partial.shape
    for piece, ref in zip(pieces, held):
        row = source_row(piece, dims, rows)
        for at in range(0, ref.shape[0], TILE):
            tile = masked_tile(ref, at, table, row + at)
            band[pl.ds(pl.multiple_of(row + at, TILE), TILE), :] = tile
    for piece in late:
        count = piece[4] - piece[3]
        band[pl.ds(source_row(piece, dims, rows), count), :] = jnp.zeros((count, cols), band.dtype)
    partial[...] = jnp.dot(left[...], band[...], preferred_element_type=jnp.float32)


def late_kernel(late, dims, table, square_keep, left, old_band, partial, *refs):
    pieces, (band, tripled, square_half, window) = refs[:len(late)], refs[len(late):]
    rows, cols = partial.shape
    pair = dims[2]
    total = partial[...]
    for first in range(0, len(late), pair):
        base = late[first]
        start = source_row(base, dims, rows)
        start = start - lax.rem(start, rows * pair)
        low = jnp.minimum(start // BLOCK * BLOCK, band.shape[0] - window.shape[0])
        low = pl.multiple_of(low, BLOCK)
        window[...] = jnp.zeros(window.shape, window.dtype)
        for piece, ref in zip(late[first:first + pair], pieces[first:first + pair]):
            row = source_row(piece, dims, rows)
            for at in range(0, ref.shape[0], TILE):
                tile = masked_tile(ref, at, table, row + at)
                window[pl.ds(pl.multiple_of(row + at - low, TILE), TILE), :] = tile
                band[pl.ds(pl.multiple_of(row + at, TILE), TILE), :] = tile
        total += jnp.dot(
            left[:, pl.ds(low, window.shape[0])], window[...], preferred_element_type=jnp.float32
        )
    total *= square_keep[...]
    tripled[...] = 3.0 * total
    square_half[...] = total.astype(jnp.bfloat16)


def cube_kernel(shift, keep, half, band, before, out):
    rep, reps = lax.axis_index("rep"), lax.axis_size("rep")
    cols = before.shape[1]
    at = lax.rem(rep - shift + reps, reps)
    right = band[pl.ds(pl.multiple_of(at * cols, BLOCK), cols), :]
    part = jnp.dot(half[...], right, preferred_element_type=jnp.float32)
    out[...] = before[...] - 2.0 * (part * keep[...])


def shifted(own, reps):
    return [
        lax.ppermute(own, "rep", [(s, (s + q) % reps) for s in range(reps)])
        for q in range(1, reps)
    ]


def on_device(grid, reps, density, density_pattern, square_pattern, cube_pattern, block_order):
    rows, cols = density.shape
    order = grid * rows
    dims = factors(grid)
    outer, inner, pair = dims
    band_bytes = order * cols * 2
    room = min(3 * band_bytes + (4 << 20), 56 << 20)
    bf16, f32 = jnp.bfloat16, jnp.float32

    def call(kernel, name, flops, moved, out, operands, spec=None, **more):
        return pl.pallas_call(
            kernel,
            out_shape=[jax.ShapeDtypeStruct(shape, dtype) for shape, dtype in out],
            in_specs=spec or [IN_VMEM] * len(operands),
            out_specs=[IN_VMEM] * len(out),
            compiler_params=pltpu.CompilerParams(vmem_limit_bytes=room),
            cost_estimate=pl.CostEstimate(flops=flops, bytes_accessed=moved, transcendentals=0),
            name=name,
            **more,
        )(*operands)

    steps, hops = list(range(1, outer)), list(range(1, inner))
    last = outer // 2 if steps and hops else None
    before = [step for step in steps if step != last][-1:]

    held = {(0, 0): density}
    for step in steps:
        ready = [held[1, 0]] if step == last and step > 1 else []
        held[step, 0] = send(after(density, *ready), dims, 0, step)
    for hop in hops:
        held[0, hop] = send(after(density), dims, 1, hop)
    packed = jnp.concatenate(
        [density_pattern, square_pattern, cube_pattern, after(block_order)[None]], axis=0
    )
    table, panel_keep, square_keep, cube_keep = call(
        functools.partial(prepare_kernel, reps), "prepare", PLACE, 2 * band_bytes,
        [((order // BLOCK, TILE, cols), bf16), ((reps, rows, cols), bf16),
         ((rows, cols), f32), ((rows, cols), f32)],
        [packed], spec=[IN_SMEM],
    )
    for step in steps:
        for hop in hops:
            ready = [table] if step == last else []
            held[step, hop] = send(after(held[step, 0], *ready), dims, 1, hop)
    panel = shifted(after(density), reps)
    left, own = call(
        functools.partial(panel_kernel, reps), "panel", 2 * PLACE, 2 * band_bytes,
        [((rows, reps * cols), bf16), ((rows, cols), bf16)],
        [panel_keep, after(density), *panel],
    )

    behind = panel + [held[step, hop] for step in before for hop in hops[:1]]
    crossed = {(0, 0): after(density, *behind)}
    for step in steps:
        for hop in hops:
            crossed[step, hop] = after(held[step, hop])
    paired = {}
    if pair > 1:
        for key, value in crossed.items():
            paired[key] = send(value, dims, 2, 1)
        behind = behind + [
            value for (step, hop), value in paired.items() if step != last and hop < 2
        ]
        for key, value in held.items():
            if key not in paired:
                ready = behind + ([left] if key[0] == last else [])
                paired[key] = send(after(value, *ready), dims, 2, 1)

    early, late = [], []
    for hop in [0] + hops:
        for step in [0] + steps:
            key = (step, hop)
            group = late if hop and step == last else early
            group.append(((step, hop, 0, 0, rows), held[key] if step or hop else own))
            if pair > 1:
                group.append(((step, hop, 1, 0, rows), paired[key]))
    late_pieces, late_values = [piece for piece, _ in late], [value for _, value in late]

    band, partial = call(
        functools.partial(early_kernel, [piece for piece, _ in early], late_pieces, dims),
        "square_early", 2 * rows * order * cols, 2 * band_bytes,
        [((order, cols), bf16), ((rows, cols), f32)],
        [left, table, *[value for _, value in early]],
    )
    span = BLOCK - math.gcd(pair * rows, BLOCK) + pair * rows
    span = min((span + BLOCK - 1) // BLOCK * BLOCK, order)
    band, tripled, square_half = call(
        functools.partial(late_kernel, late_pieces, dims), "square_late",
        2 * rows * span * cols, 4 * rows * cols,
        [((order, cols), bf16), ((rows, cols), f32), ((rows, cols), bf16)],
        [table, square_keep, left, band, partial, *late_values],
        input_output_aliases={3: 0},
        scratch_shapes=[pltpu.VMEM((span, cols), bf16)],
    )
    out = tripled
    for shift, half in enumerate([square_half] + shifted(square_half, reps)):
        (out,) = call(
            functools.partial(cube_kernel, shift), "cube_part",
            2 * rows * cols * cols, band_bytes // reps, [((rows, cols), f32)],
            [cube_keep, half, band, out],
        )
    return out


def solution(mesh):
    placed = (P("grid", "rep"), P(), P(), P(), P())
    return jax.shard_map(
        functools.partial(on_device, mesh.shape["grid"], mesh.shape["rep"]),
        mesh=mesh, in_specs=placed, out_specs=P("grid", "rep"), check_vma=False,
    )
```

```python
import functools
import math

import jax
import jax.numpy as jnp
from jax import lax
from jax.experimental import pallas as pl
from jax.experimental.pallas import tpu as pltpu
from jax.sharding import PartitionSpec as P

BLOCK = 128
TILE = 16
PLACE = 10**9
IN_SMEM = pl.BlockSpec(memory_space=pltpu.SMEM)
IN_VMEM = pl.BlockSpec(memory_space=pltpu.VMEM)


def factors(size):
    pair = 2 if size % 2 == 0 else 1
    rest = size // pair
    outer = 4 if rest % 4 == 0 else 1
    return outer, rest // outer, pair


def send(value, dims, axis, step):
    outer, inner, pair = dims
    pairs = []
    for source in range(outer * inner * pair):
        place = [source // (inner * pair), source // pair % inner, source % pair]
        place[axis] = (place[axis] + step) % dims[axis]
        pairs.append((source, (place[0] * inner + place[1]) * pair + place[2]))
    return lax.ppermute(value, "grid", pairs)


def source_row(piece, dims, rows):
    outer, inner, pair = dims
    here = lax.axis_index("grid")
    at = (here // (inner * pair), here // pair % inner, here % pair)
    z, x, c = [lax.rem(a - k + d, d) for a, k, d in zip(at, piece[:3], dims)]
    return pl.multiple_of(((z * inner + x) * pair + c) * rows + piece[3], TILE)


def after(value, *others):
    return lax.optimization_barrier((value,) + others)[0]


def pick(pattern, order, row_block, col_block):
    return pattern[order[row_block], order[col_block]].astype(jnp.float32)


def rows_mask(pattern, order, first_row, rows, first_col_block, col_blocks):
    top = first_row // BLOCK
    low = (first_row + rows - 1) // BLOCK
    split = (top + 1) * BLOCK - first_row
    upper = lax.broadcasted_iota(jnp.int32, (rows, BLOCK), 0) < split
    tiles = []
    for j in range(col_blocks):
        a = pick(pattern, order, top, first_col_block + j)
        b = pick(pattern, order, low, first_col_block + j)
        tiles.append(jnp.where(upper, a, b))
    return jnp.concatenate(tiles, axis=1)


def parts_of(packed):
    count = packed.shape[1]
    patterns = [packed.at[pl.ds(at * count, count), :] for at in range(3)]
    return (*patterns, packed.at[3 * count])


def prepare_kernel(reps, packed, table, panel_keep, square_keep, cube_keep):
    density_pattern, square_pattern, cube_pattern, order = parts_of(packed)
    here, rep = lax.axis_index("grid"), lax.axis_index("rep")
    row_blocks, _, cols = table.shape
    rows = square_keep.shape[0]
    col_blocks = cols // BLOCK
    first_col = rep * col_blocks

    def fill(i, _):
        for j in range(col_blocks):
            keep = pick(density_pattern, order, i, first_col + j)
            tile = jnp.full((TILE, BLOCK), keep, jnp.float32).astype(jnp.bfloat16)
            table[i, :, j * BLOCK:(j + 1) * BLOCK] = tile
        return 0

    lax.fori_loop(0, row_blocks, fill, 0, unroll=row_blocks <= 16)
    for q in range(reps):
        at = lax.rem(rep - q + reps, reps) * col_blocks
        keep = rows_mask(density_pattern, order, here * rows, rows, at, col_blocks)
        panel_keep[q] = keep.astype(jnp.bfloat16)
    for pattern, keep in ((square_pattern, square_keep), (cube_pattern, cube_keep)):
        keep[...] = rows_mask(pattern, order, here * rows, rows, first_col, col_blocks)


def panel_kernel(reps, panel_keep, *refs):
    panel, (left, own) = refs[:reps], refs[reps:]
    rep = lax.axis_index("rep")
    cols = panel[0].shape[1]
    for q in range(reps):
        at = pl.multiple_of(lax.rem(rep - q + reps, reps) * cols, BLOCK)
        part = panel[q][...] * panel_keep[q]
        left[:, pl.ds(at, cols)] = part
        if q == 0:
            own[...] = part


def masked_tile(source, at, table, stored_row):
    return source[at:at + TILE, :] * table[stored_row // BLOCK]


def early_kernel(pieces, late, dims, left, table, *refs):
    held, (band, partial) = refs[:len(pieces)], refs[len(pieces):]
    rows, cols = partial.shape
    for piece, ref in zip(pieces, held):
        row = source_row(piece, dims, rows)
        for at in range(0, ref.shape[0], TILE):
            tile = masked_tile(ref, at, table, row + at)
            band[pl.ds(pl.multiple_of(row + at, TILE), TILE), :] = tile
    for piece in late:
        count = piece[4] - piece[3]
        band[pl.ds(source_row(piece, dims, rows), count), :] = jnp.zeros((count, cols), band.dtype)
    partial[...] = jnp.dot(left[...], band[...], preferred_element_type=jnp.float32)


def late_kernel(late, dims, table, square_keep, left, old_band, partial, *refs):
    pieces, (band, tripled, square_half, window) = refs[:len(late)], refs[len(late):]
    rows, cols = partial.shape
    pair = dims[2]
    total = partial[...]
    for first in range(0, len(late), pair):
        base = late[first]
        start = source_row(base, dims, rows)
        start = start - lax.rem(start, rows * pair)
        low = jnp.minimum(start // BLOCK * BLOCK, band.shape[0] - window.shape[0])
        low = pl.multiple_of(low, BLOCK)
        window[...] = jnp.zeros(window.shape, window.dtype)
        for piece, ref in zip(late[first:first + pair], pieces[first:first + pair]):
            row = source_row(piece, dims, rows)
            for at in range(0, ref.shape[0], TILE):
                tile = masked_tile(ref, at, table, row + at)
                window[pl.ds(pl.multiple_of(row + at - low, TILE), TILE), :] = tile
                band[pl.ds(pl.multiple_of(row + at, TILE), TILE), :] = tile
        total += jnp.dot(
            left[:, pl.ds(low, window.shape[0])], window[...], preferred_element_type=jnp.float32
        )
    total *= square_keep[...]
    tripled[...] = 3.0 * total
    square_half[...] = total.astype(jnp.bfloat16)


def cube_kernel(shift, chunks, keep, half, band, before, out, staged=None, sent=None):
    rep, reps = lax.axis_index("rep"), lax.axis_size("rep")
    cols = before.shape[1]
    at = lax.rem(rep - shift + reps, reps)
    down = pl.ds(pl.multiple_of(at * cols, BLOCK), cols)
    copies = []
    for first in range(0, cols, cols // chunks):
        across = slice(first, first + cols // chunks)
        part = jnp.dot(half[...], band[down, across], preferred_element_type=jnp.float32)
        value = before[:, across] - 2.0 * (part * keep[:, across])
        if staged is None:
            out[:, across] = value
        else:
            staged[:, across] = value
            copies.append(
                pltpu.make_async_copy(staged.at[:, across], out.at[:, across], sent.at[len(copies)])
            )
            copies[-1].start()
    for copy in copies:
        copy.wait()


def shifted(own, reps):
    return [
        lax.ppermute(own, "rep", [(s, (s + q) % reps) for s in range(reps)])
        for q in range(1, reps)
    ]


def on_device(grid, reps, density, density_pattern, square_pattern, cube_pattern, block_order):
    rows, cols = density.shape
    order = grid * rows
    dims = factors(grid)
    outer, inner, pair = dims
    band_bytes = order * cols * 2
    room = min(3 * band_bytes + (4 << 20), 56 << 20)
    bf16, f32 = jnp.bfloat16, jnp.float32

    def call(kernel, name, flops, moved, out, operands, spec=None, out_specs=None, **more):
        return pl.pallas_call(
            kernel,
            out_shape=[jax.ShapeDtypeStruct(shape, dtype) for shape, dtype in out],
            in_specs=spec or [IN_VMEM] * len(operands),
            out_specs=out_specs or [IN_VMEM] * len(out),
            compiler_params=pltpu.CompilerParams(vmem_limit_bytes=room),
            cost_estimate=pl.CostEstimate(flops=flops, bytes_accessed=moved, transcendentals=0),
            name=name,
            **more,
        )(*operands)

    steps, hops = list(range(1, outer)), list(range(1, inner))
    last = outer // 2 if steps and hops else None
    before = [step for step in steps if step != last][-1:]

    held = {(0, 0): density}
    for step in steps:
        held[step, 0] = send(after(density), dims, 0, step)
    for hop in hops:
        held[0, hop] = send(after(density), dims, 1, hop)
    packed = jnp.concatenate(
        [density_pattern, square_pattern, cube_pattern, after(block_order)[None]], axis=0
    )
    table, panel_keep, square_keep, cube_keep = call(
        functools.partial(prepare_kernel, reps), "prepare", PLACE, 2 * band_bytes,
        [((order // BLOCK, TILE, cols), bf16), ((reps, rows, cols), bf16),
         ((rows, cols), f32), ((rows, cols), f32)],
        [packed], spec=[IN_SMEM],
    )
    for step in steps:
        for hop in hops:
            ready = [table] if step == last else []
            held[step, hop] = send(after(held[step, 0], *ready), dims, 1, hop)
    panel = shifted(after(density), reps)
    left, own = call(
        functools.partial(panel_kernel, reps), "panel", 2 * PLACE, 2 * band_bytes,
        [((rows, reps * cols), bf16), ((rows, cols), bf16)],
        [panel_keep, after(density), *panel],
    )

    behind = panel + [held[step, hop] for step in before for hop in hops[:1]]
    crossed = {(0, 0): after(density, *behind)}
    for step in steps:
        for hop in hops:
            crossed[step, hop] = after(held[step, hop])
    paired = {}
    if pair > 1:
        for key, value in crossed.items():
            paired[key] = send(value, dims, 2, 1)
        behind = behind + [
            value for (step, hop), value in paired.items() if step != last and hop < 2
        ]
        for key, value in held.items():
            if key not in paired:
                ready = behind + ([left] if key[0] == last else [])
                paired[key] = send(after(value, *ready), dims, 2, 1)

    early, late = [], []
    for hop in [0] + hops:
        for step in [0] + steps:
            key = (step, hop)
            group = late if hop and step == last else early
            group.append(((step, hop, 0, 0, rows), held[key] if step or hop else own))
            if pair > 1:
                group.append(((step, hop, 1, 0, rows), paired[key]))
    late_pieces, late_values = [piece for piece, _ in late], [value for _, value in late]

    band, partial = call(
        functools.partial(early_kernel, [piece for piece, _ in early], late_pieces, dims),
        "square_early", 2 * rows * order * cols, 2 * band_bytes,
        [((order, cols), bf16), ((rows, cols), f32)],
        [left, table, *[value for _, value in early]],
    )
    span = BLOCK - math.gcd(pair * rows, BLOCK) + pair * rows
    span = min((span + BLOCK - 1) // BLOCK * BLOCK, order)
    band, tripled, square_half = call(
        functools.partial(late_kernel, late_pieces, dims), "square_late",
        2 * rows * span * cols, 4 * rows * cols,
        [((order, cols), bf16), ((rows, cols), f32), ((rows, cols), bf16)],
        [table, square_keep, left, band, partial, *late_values],
        input_output_aliases={3: 0},
        scratch_shapes=[pltpu.VMEM((span, cols), bf16)],
    )
    out = tripled
    halves = [square_half] + shifted(square_half, reps)
    for shift, half in enumerate(halves):
        final = shift == len(halves) - 1
        chunks = cols // BLOCK if final else 1
        scratch = [pltpu.VMEM((rows, cols), f32), pltpu.SemaphoreType.DMA((chunks,))]
        (out,) = call(
            functools.partial(cube_kernel, shift, chunks), "cube_part",
            2 * rows * cols * cols, band_bytes // reps, [((rows, cols), f32)],
            [cube_keep, half, band, out], scratch_shapes=scratch if final else [],
            out_specs=[pl.BlockSpec(memory_space=pl.ANY)] if final else None,
        )
    return out


def solution(mesh):
    placed = (P("grid", "rep"), P(), P(), P(), P())
    return jax.shard_map(
        functools.partial(on_device, mesh.shape["grid"], mesh.shape["rep"]),
        mesh=mesh, in_specs=placed, out_specs=P("grid", "rep"), check_vma=False,
    )
```

```python
import functools
import math

import jax
import jax.numpy as jnp
from jax import lax
from jax.experimental import pallas as pl
from jax.experimental.pallas import tpu as pltpu
from jax.sharding import PartitionSpec as P

BLOCK = 128
TILE = 16
PLACE = 10**9
IN_SMEM = pl.BlockSpec(memory_space=pltpu.SMEM)
IN_VMEM = pl.BlockSpec(memory_space=pltpu.VMEM)


def factors(size):
    pair = 2 if size % 2 == 0 else 1
    rest = size // pair
    outer = 4 if rest % 4 == 0 else 1
    return outer, rest // outer, pair


def send(value, dims, axis, step):
    outer, inner, pair = dims
    pairs = []
    for source in range(outer * inner * pair):
        place = [source // (inner * pair), source // pair % inner, source % pair]
        place[axis] = (place[axis] + step) % dims[axis]
        pairs.append((source, (place[0] * inner + place[1]) * pair + place[2]))
    return lax.ppermute(value, "grid", pairs)


def source_row(piece, dims, rows):
    outer, inner, pair = dims
    here = lax.axis_index("grid")
    at = (here // (inner * pair), here // pair % inner, here % pair)
    z, x, c = [lax.rem(a - k + d, d) for a, k, d in zip(at, piece[:3], dims)]
    return pl.multiple_of(((z * inner + x) * pair + c) * rows + piece[3], TILE)


def after(value, *others):
    return lax.optimization_barrier((value,) + others)[0]


def pick(pattern, order, row_block, col_block):
    return pattern[order[row_block], order[col_block]].astype(jnp.float32)


def rows_mask(pattern, order, first_row, rows, first_col_block, col_blocks):
    top = first_row // BLOCK
    low = (first_row + rows - 1) // BLOCK
    split = (top + 1) * BLOCK - first_row
    upper = lax.broadcasted_iota(jnp.int32, (rows, BLOCK), 0) < split
    tiles = []
    for j in range(col_blocks):
        a = pick(pattern, order, top, first_col_block + j)
        b = pick(pattern, order, low, first_col_block + j)
        tiles.append(jnp.where(upper, a, b))
    return jnp.concatenate(tiles, axis=1)


def parts_of(packed):
    count = packed.shape[1]
    patterns = [packed.at[pl.ds(at * count, count), :] for at in range(3)]
    return (*patterns, packed.at[3 * count])


def prepare_kernel(reps, packed, table, panel_keep, square_keep, cube_keep):
    density_pattern, square_pattern, cube_pattern, order = parts_of(packed)
    here, rep = lax.axis_index("grid"), lax.axis_index("rep")
    row_blocks, _, cols = table.shape
    rows = square_keep.shape[0]
    col_blocks = cols // BLOCK
    first_col = rep * col_blocks

    def fill(i, _):
        for j in range(col_blocks):
            keep = pick(density_pattern, order, i, first_col + j)
            tile = jnp.full((TILE, BLOCK), keep, jnp.float32).astype(jnp.bfloat16)
            table[i, :, j * BLOCK:(j + 1) * BLOCK] = tile
        return 0

    lax.fori_loop(0, row_blocks, fill, 0, unroll=row_blocks <= 16)
    for q in range(reps):
        at = lax.rem(rep - q + reps, reps) * col_blocks
        keep = rows_mask(density_pattern, order, here * rows, rows, at, col_blocks)
        panel_keep[q] = keep.astype(jnp.bfloat16)
    for pattern, keep in ((square_pattern, square_keep), (cube_pattern, cube_keep)):
        keep[...] = rows_mask(pattern, order, here * rows, rows, first_col, col_blocks)


def panel_kernel(reps, panel_keep, *refs):
    panel, (left, own) = refs[:reps], refs[reps:]
    rep = lax.axis_index("rep")
    cols = panel[0].shape[1]
    for q in range(reps):
        at = pl.multiple_of(lax.rem(rep - q + reps, reps) * cols, BLOCK)
        part = panel[q][...] * panel_keep[q]
        left[:, pl.ds(at, cols)] = part
        if q == 0:
            own[...] = part


def masked_tile(source, at, table, stored_row):
    return source[at:at + TILE, :] * table[stored_row // BLOCK]


def stack_kernel(*refs):
    out, done = refs[-1], 0
    for ref in refs[:-1]:
        out[done:done + ref.shape[0], :] = ref[...]
        done += ref.shape[0]


def early_kernel(groups, late, dims, left, table, *refs):
    held, (band, partial) = refs[:len(groups)], refs[len(groups):]
    rows, cols = partial.shape
    for pieces, ref in zip(groups, held):
        done = 0
        for piece in pieces:
            row = source_row(piece, dims, rows)
            for at in range(0, piece[4] - piece[3], TILE):
                tile = masked_tile(ref, done, table, row + at)
                band[pl.ds(pl.multiple_of(row + at, TILE), TILE), :] = tile
                done += TILE
    for piece in late:
        count = piece[4] - piece[3]
        band[pl.ds(source_row(piece, dims, rows), count), :] = jnp.zeros((count, cols), band.dtype)
    partial[...] = jnp.dot(left[...], band[...], preferred_element_type=jnp.float32)


def late_kernel(late, dims, table, square_keep, left, old_band, partial, *refs):
    pieces, (band, tripled, square_half, window) = refs[:len(late)], refs[len(late):]
    rows, cols = partial.shape
    pair = dims[2]
    total = partial[...]
    for first in range(0, len(late), pair):
        base = late[first]
        start = source_row(base, dims, rows)
        start = start - lax.rem(start, rows * pair)
        low = jnp.minimum(start // BLOCK * BLOCK, band.shape[0] - window.shape[0])
        low = pl.multiple_of(low, BLOCK)
        window[...] = jnp.zeros(window.shape, window.dtype)
        for piece, ref in zip(late[first:first + pair], pieces[first:first + pair]):
            row = source_row(piece, dims, rows)
            for at in range(0, ref.shape[0], TILE):
                tile = masked_tile(ref, at, table, row + at)
                window[pl.ds(pl.multiple_of(row + at - low, TILE), TILE), :] = tile
                band[pl.ds(pl.multiple_of(row + at, TILE), TILE), :] = tile
        total += jnp.dot(
            left[:, pl.ds(low, window.shape[0])], window[...], preferred_element_type=jnp.float32
        )
    total *= square_keep[...]
    tripled[...] = 3.0 * total
    square_half[...] = total.astype(jnp.bfloat16)


def cube_kernel(shift, keep, half, band, before, out):
    rep, reps = lax.axis_index("rep"), lax.axis_size("rep")
    cols = before.shape[1]
    at = lax.rem(rep - shift + reps, reps)
    right = band[pl.ds(pl.multiple_of(at * cols, BLOCK), cols), :]
    part = jnp.dot(half[...], right, preferred_element_type=jnp.float32)
    out[...] = before[...] - 2.0 * (part * keep[...])


def shifted(own, reps):
    return [
        lax.ppermute(own, "rep", [(s, (s + q) % reps) for s in range(reps)])
        for q in range(1, reps)
    ]


def on_device(grid, reps, density, density_pattern, square_pattern, cube_pattern, block_order):
    rows, cols = density.shape
    order = grid * rows
    dims = factors(grid)
    outer, inner, pair = dims
    band_bytes = order * cols * 2
    room = min(3 * band_bytes + (4 << 20), 56 << 20)
    bf16, f32 = jnp.bfloat16, jnp.float32

    def call(kernel, name, flops, moved, out, operands, spec=None, **more):
        return pl.pallas_call(
            kernel,
            out_shape=[jax.ShapeDtypeStruct(shape, dtype) for shape, dtype in out],
            in_specs=spec or [IN_VMEM] * len(operands),
            out_specs=[IN_VMEM] * len(out),
            compiler_params=pltpu.CompilerParams(vmem_limit_bytes=room),
            cost_estimate=pl.CostEstimate(flops=flops, bytes_accessed=moved, transcendentals=0),
            name=name,
            **more,
        )(*operands)

    steps, hops = list(range(1, outer)), list(range(1, inner))
    last = outer // 2 if steps and hops else None
    before = [step for step in steps if step != last][-1:]

    held = {(0, 0): density}
    for step in steps:
        held[step, 0] = send(after(density), dims, 0, step)
    for hop in hops:
        held[0, hop] = send(after(density), dims, 1, hop)
    packed = jnp.concatenate(
        [density_pattern, square_pattern, cube_pattern, after(block_order)[None]], axis=0
    )
    table, panel_keep, square_keep, cube_keep = call(
        functools.partial(prepare_kernel, reps), "prepare", PLACE, 2 * band_bytes,
        [((order // BLOCK, TILE, cols), bf16), ((reps, rows, cols), bf16),
         ((rows, cols), f32), ((rows, cols), f32)],
        [packed], spec=[IN_SMEM],
    )
    for step in steps:
        for hop in hops:
            ready = [table] if step == last else []
            held[step, hop] = send(after(held[step, 0], *ready), dims, 1, hop)
    panel = shifted(after(density), reps)
    left, own = call(
        functools.partial(panel_kernel, reps), "panel", 4 * PLACE, 2 * band_bytes,
        [((rows, reps * cols), bf16), ((rows, cols), bf16)],
        [panel_keep, after(density), *panel],
    )

    lone = [(0, 0)] + [key for key in held if key[0] == last]
    lone += [key for key in held if key[0] in before and key[1]]
    stack = [key for key in held if key not in lone]
    whole = lambda key, core: (*key, core, 0, rows)
    early, late = [], []
    for key in lone:
        group = late if key[0] == last and key[1] else early
        group.append(([whole(key, 0)], held[key] if key != (0, 0) else own))
        if pair > 1:
            value = after(held[key], *([] if group is late else [left]))
            group.append(([whole(key, 1)], send(value, dims, 2, 1)))
    early += [([whole(key, 0)], held[key]) for key in stack]
    if pair > 1 and stack:
        ready = panel + ([held[last, 0]] if hops else [])
        (stacked,) = call(
            stack_kernel, "stack", 0, 0, [((len(stack) * rows, cols), bf16)],
            [after(held[key], *ready) for key in stack],
        )
        early.append(([whole(key, 1) for key in stack], send(after(stacked), dims, 2, 1)))
    late_pieces, late_values = [piece[0] for piece, _ in late], [value for _, value in late]

    band, partial = call(
        functools.partial(early_kernel, [pieces for pieces, _ in early], late_pieces, dims),
        "square_early", 2 * rows * order * cols, 2 * band_bytes,
        [((order, cols), bf16), ((rows, cols), f32)],
        [left, table, *[value for _, value in early]],
    )
    span = BLOCK - math.gcd(pair * rows, BLOCK) + pair * rows
    span = min((span + BLOCK - 1) // BLOCK * BLOCK, order)
    band, tripled, square_half = call(
        functools.partial(late_kernel, late_pieces, dims), "square_late",
        2 * rows * span * cols, 4 * rows * cols,
        [((order, cols), bf16), ((rows, cols), f32), ((rows, cols), bf16)],
        [table, square_keep, left, band, partial, *late_values],
        input_output_aliases={3: 0},
        scratch_shapes=[pltpu.VMEM((span, cols), bf16)],
    )
    out = tripled
    for shift, half in enumerate([square_half] + shifted(square_half, reps)):
        (out,) = call(
            functools.partial(cube_kernel, shift), "cube_part",
            2 * rows * cols * cols, band_bytes // reps, [((rows, cols), f32)],
            [cube_keep, half, band, out],
        )
    return out


def solution(mesh):
    placed = (P("grid", "rep"), P(), P(), P(), P())
    return jax.shard_map(
        functools.partial(on_device, mesh.shape["grid"], mesh.shape["rep"]),
        mesh=mesh, in_specs=placed, out_specs=P("grid", "rep"), check_vma=False,
    )
```

```python
import functools
import math

import jax
import jax.numpy as jnp
from jax import lax
from jax.experimental import pallas as pl
from jax.experimental.pallas import tpu as pltpu
from jax.sharding import PartitionSpec as P

BLOCK = 128
TILE = 16
PLACE = 10**9
IN_SMEM = pl.BlockSpec(memory_space=pltpu.SMEM)
IN_VMEM = pl.BlockSpec(memory_space=pltpu.VMEM)


def factors(size):
    pair = 2 if size % 2 == 0 else 1
    rest = size // pair
    outer = 4 if rest % 4 == 0 else 1
    return outer, rest // outer, pair


def send(value, dims, axis, step):
    outer, inner, pair = dims
    pairs = []
    for source in range(outer * inner * pair):
        place = [source // (inner * pair), source // pair % inner, source % pair]
        place[axis] = (place[axis] + step) % dims[axis]
        pairs.append((source, (place[0] * inner + place[1]) * pair + place[2]))
    return lax.ppermute(value, "grid", pairs)


def source_row(piece, dims, rows):
    outer, inner, pair = dims
    here = lax.axis_index("grid")
    at = (here // (inner * pair), here // pair % inner, here % pair)
    z, x, c = [lax.rem(a - k + d, d) for a, k, d in zip(at, piece[:3], dims)]
    return pl.multiple_of(((z * inner + x) * pair + c) * rows + piece[3], TILE)


def after(value, *others):
    return lax.optimization_barrier((value,) + others)[0]


def pick(pattern, order, row_block, col_block):
    return pattern[order[row_block], order[col_block]].astype(jnp.float32)


def rows_mask(pattern, order, first_row, rows, first_col_block, col_blocks):
    top = first_row // BLOCK
    low = (first_row + rows - 1) // BLOCK
    split = (top + 1) * BLOCK - first_row
    upper = lax.broadcasted_iota(jnp.int32, (rows, BLOCK), 0) < split
    tiles = []
    for j in range(col_blocks):
        a = pick(pattern, order, top, first_col_block + j)
        b = pick(pattern, order, low, first_col_block + j)
        tiles.append(jnp.where(upper, a, b))
    return jnp.concatenate(tiles, axis=1)


def parts_of(packed):
    count = packed.shape[1]
    patterns = [packed.at[pl.ds(at * count, count), :] for at in range(3)]
    return (*patterns, packed.at[3 * count])


def prepare_kernel(reps, packed, table, panel_keep, square_keep, cube_keep):
    density_pattern, square_pattern, cube_pattern, order = parts_of(packed)
    here, rep = lax.axis_index("grid"), lax.axis_index("rep")
    row_blocks, _, cols = table.shape
    rows = square_keep.shape[0]
    col_blocks = cols // BLOCK
    first_col = rep * col_blocks

    def fill(i, _):
        for j in range(col_blocks):
            keep = pick(density_pattern, order, i, first_col + j)
            tile = jnp.full((TILE, BLOCK), keep, jnp.float32).astype(jnp.bfloat16)
            table[i, :, j * BLOCK:(j + 1) * BLOCK] = tile
        return 0

    lax.fori_loop(0, row_blocks, fill, 0, unroll=row_blocks <= 16)
    for q in range(reps):
        at = lax.rem(rep - q + reps, reps) * col_blocks
        keep = rows_mask(density_pattern, order, here * rows, rows, at, col_blocks)
        panel_keep[q] = keep.astype(jnp.bfloat16)
    for pattern, keep in ((square_pattern, square_keep), (cube_pattern, cube_keep)):
        keep[...] = rows_mask(pattern, order, here * rows, rows, first_col, col_blocks)


def panel_kernel(reps, panel_keep, *refs):
    panel, (left, own) = refs[:reps], refs[reps:]
    rep = lax.axis_index("rep")
    cols = panel[0].shape[1]
    for q in range(reps):
        at = pl.multiple_of(lax.rem(rep - q + reps, reps) * cols, BLOCK)
        part = panel[q][...] * panel_keep[q]
        left[:, pl.ds(at, cols)] = part
        if q == 0:
            own[...] = part


def masked_tile(source, at, table, stored_row):
    return source[at:at + TILE, :] * table[stored_row // BLOCK]


def stack_kernel(*refs):
    out, done = refs[-1], 0
    for ref in refs[:-1]:
        out[done:done + ref.shape[0], :] = ref[...]
        done += ref.shape[0]


def early_kernel(groups, late, dims, left, table, *refs):
    held, (band, partial) = refs[:len(groups)], refs[len(groups):]
    rows, cols = partial.shape
    for pieces, ref in zip(groups, held):
        done = 0
        for piece in pieces:
            row = source_row(piece, dims, rows)
            for at in range(0, piece[4] - piece[3], TILE):
                tile = masked_tile(ref, done, table, row + at)
                band[pl.ds(pl.multiple_of(row + at, TILE), TILE), :] = tile
                done += TILE
    for piece in late:
        count = piece[4] - piece[3]
        band[pl.ds(source_row(piece, dims, rows), count), :] = jnp.zeros((count, cols), band.dtype)
    partial[...] = jnp.dot(left[...], band[...], preferred_element_type=jnp.float32)


def late_kernel(late, dims, table, square_keep, left, old_band, partial, *refs):
    pieces, (band, tripled, square_half, window) = refs[:len(late)], refs[len(late):]
    rows, cols = partial.shape
    pair = dims[2]
    total = partial[...]
    for first in range(0, len(late), pair):
        base = late[first]
        start = source_row(base, dims, rows)
        start = start - lax.rem(start, rows * pair)
        low = jnp.minimum(start // BLOCK * BLOCK, band.shape[0] - window.shape[0])
        low = pl.multiple_of(low, BLOCK)
        window[...] = jnp.zeros(window.shape, window.dtype)
        for piece, ref in zip(late[first:first + pair], pieces[first:first + pair]):
            row = source_row(piece, dims, rows)
            for at in range(0, ref.shape[0], TILE):
                tile = masked_tile(ref, at, table, row + at)
                window[pl.ds(pl.multiple_of(row + at - low, TILE), TILE), :] = tile
                band[pl.ds(pl.multiple_of(row + at, TILE), TILE), :] = tile
        total += jnp.dot(
            left[:, pl.ds(low, window.shape[0])], window[...], preferred_element_type=jnp.float32
        )
    total *= square_keep[...]
    tripled[...] = 3.0 * total
    square_half[...] = total.astype(jnp.bfloat16)


def cube_kernel(shift, keep, half, band, before, out):
    rep, reps = lax.axis_index("rep"), lax.axis_size("rep")
    cols = before.shape[1]
    at = lax.rem(rep - shift + reps, reps)
    right = band[pl.ds(pl.multiple_of(at * cols, BLOCK), cols), :]
    part = jnp.dot(half[...], right, preferred_element_type=jnp.float32)
    out[...] = before[...] - 2.0 * (part * keep[...])


def shifted(own, reps):
    return [
        lax.ppermute(own, "rep", [(s, (s + q) % reps) for s in range(reps)])
        for q in range(1, reps)
    ]


def on_device(grid, reps, density, density_pattern, square_pattern, cube_pattern, block_order):
    rows, cols = density.shape
    order = grid * rows
    dims = factors(grid)
    outer, inner, pair = dims
    band_bytes = order * cols * 2
    room = min(3 * band_bytes + (4 << 20), 56 << 20)
    bf16, f32 = jnp.bfloat16, jnp.float32

    def call(kernel, name, flops, moved, out, operands, spec=None, **more):
        return pl.pallas_call(
            kernel,
            out_shape=[jax.ShapeDtypeStruct(shape, dtype) for shape, dtype in out],
            in_specs=spec or [IN_VMEM] * len(operands),
            out_specs=[IN_VMEM] * len(out),
            compiler_params=pltpu.CompilerParams(vmem_limit_bytes=room),
            cost_estimate=pl.CostEstimate(flops=flops, bytes_accessed=moved, transcendentals=0),
            name=name,
            **more,
        )(*operands)

    steps, hops = list(range(1, outer)), list(range(1, inner))
    last = outer // 2 if steps and hops else None
    before = [step for step in steps if step != last][-1:]

    held = {(0, 0): density}
    for step in steps:
        held[step, 0] = send(after(density), dims, 0, step)
    for hop in hops:
        held[0, hop] = send(after(density), dims, 1, hop)
    packed = jnp.concatenate(
        [density_pattern, square_pattern, cube_pattern, after(block_order)[None]], axis=0
    )
    table, panel_keep, square_keep, cube_keep = call(
        functools.partial(prepare_kernel, reps), "prepare", PLACE, 2 * band_bytes,
        [((order // BLOCK, TILE, cols), bf16), ((reps, rows, cols), bf16),
         ((rows, cols), f32), ((rows, cols), f32)],
        [packed], spec=[IN_SMEM],
    )
    for step in steps:
        for hop in hops:
            ready = [table] if step == last else []
            held[step, hop] = send(after(held[step, 0], *ready), dims, 1, hop)
    panel = shifted(after(density), reps)
    left, own = call(
        functools.partial(panel_kernel, reps), "panel", 4 * PLACE, 2 * band_bytes,
        [((rows, reps * cols), bf16), ((rows, cols), bf16)],
        [panel_keep, after(density), *panel],
    )

    keys = [(0, 0)] + [(0, hop) for hop in hops] + [(step, 0) for step in steps]
    keys += [(step, hop) for step in steps for hop in hops]
    lone = [(0, 0)] + [key for key in keys if key[0] == last or key[0] in before and key[1]]
    stack = [key for key in keys if key not in lone]
    whole = lambda key, core: (*key, core, 0, rows)
    early, late = [], []
    for key in keys:
        group = late if key[0] == last and key[1] else early
        group.append(([whole(key, 0)], held[key] if key != (0, 0) else own))
        if pair > 1 and key in lone:
            value = after(held[key], *([] if group is late else [left]))
            group.append(([whole(key, 1)], send(value, dims, 2, 1)))
    if pair > 1 and stack:
        ready = panel + ([held[last, 0]] if hops else [])
        (stacked,) = call(
            stack_kernel, "stack", 0, 0, [((len(stack) * rows, cols), bf16)],
            [after(held[key], *ready) for key in stack],
        )
        early.append(([whole(key, 1) for key in stack], send(after(stacked), dims, 2, 1)))
    late_pieces, late_values = [piece[0] for piece, _ in late], [value for _, value in late]

    band, partial = call(
        functools.partial(early_kernel, [pieces for pieces, _ in early], late_pieces, dims),
        "square_early", 2 * rows * order * cols, 2 * band_bytes,
        [((order, cols), bf16), ((rows, cols), f32)],
        [left, table, *[value for _, value in early]],
    )
    span = BLOCK - math.gcd(pair * rows, BLOCK) + pair * rows
    span = min((span + BLOCK - 1) // BLOCK * BLOCK, order)
    band, tripled, square_half = call(
        functools.partial(late_kernel, late_pieces, dims), "square_late",
        2 * rows * span * cols, 4 * rows * cols,
        [((order, cols), bf16), ((rows, cols), f32), ((rows, cols), bf16)],
        [table, square_keep, left, band, partial, *late_values],
        input_output_aliases={3: 0},
        scratch_shapes=[pltpu.VMEM((span, cols), bf16)],
    )
    out = tripled
    for shift, half in enumerate([square_half] + shifted(square_half, reps)):
        (out,) = call(
            functools.partial(cube_kernel, shift), "cube_part",
            2 * rows * cols * cols, band_bytes // reps, [((rows, cols), f32)],
            [cube_keep, half, band, out],
        )
    return out


def solution(mesh):
    placed = (P("grid", "rep"), P(), P(), P(), P())
    return jax.shard_map(
        functools.partial(on_device, mesh.shape["grid"], mesh.shape["rep"]),
        mesh=mesh, in_specs=placed, out_specs=P("grid", "rep"), check_vma=False,
    )
```

```python
import functools
import math

import jax
import jax.numpy as jnp
from jax import lax
from jax.experimental import pallas as pl
from jax.experimental.pallas import tpu as pltpu
from jax.sharding import PartitionSpec as P

BLOCK = 128
TILE = 16
PLACE = 10**9
IN_SMEM = pl.BlockSpec(memory_space=pltpu.SMEM)
IN_VMEM = pl.BlockSpec(memory_space=pltpu.VMEM)


def factors(size):
    pair = 2 if size % 2 == 0 else 1
    rest = size // pair
    outer = 4 if rest % 4 == 0 else 1
    return outer, rest // outer, pair


def send(value, dims, axis, step):
    outer, inner, pair = dims
    pairs = []
    for source in range(outer * inner * pair):
        place = [source // (inner * pair), source // pair % inner, source % pair]
        place[axis] = (place[axis] + step) % dims[axis]
        pairs.append((source, (place[0] * inner + place[1]) * pair + place[2]))
    return lax.ppermute(value, "grid", pairs)


def source_row(piece, dims, rows):
    outer, inner, pair = dims
    here = lax.axis_index("grid")
    at = (here // (inner * pair), here // pair % inner, here % pair)
    z, x, c = [lax.rem(a - k + d, d) for a, k, d in zip(at, piece[:3], dims)]
    return pl.multiple_of(((z * inner + x) * pair + c) * rows + piece[3], TILE)


def after(value, *others):
    return lax.optimization_barrier((value,) + others)[0]


def pick(pattern, order, row_block, col_block):
    return pattern[order[row_block], order[col_block]].astype(jnp.float32)


def rows_mask(pattern, order, first_row, rows, first_col_block, col_blocks):
    top = first_row // BLOCK
    low = (first_row + rows - 1) // BLOCK
    split = (top + 1) * BLOCK - first_row
    upper = lax.broadcasted_iota(jnp.int32, (rows, BLOCK), 0) < split
    tiles = []
    for j in range(col_blocks):
        a = pick(pattern, order, top, first_col_block + j)
        b = pick(pattern, order, low, first_col_block + j)
        tiles.append(jnp.where(upper, a, b))
    return jnp.concatenate(tiles, axis=1)


def parts_of(packed):
    count = packed.shape[1]
    patterns = [packed.at[pl.ds(at * count, count), :] for at in range(3)]
    return (*patterns, packed.at[3 * count])


def prepare_kernel(reps, packed, table, panel_keep, square_keep, cube_keep):
    density_pattern, square_pattern, cube_pattern, order = parts_of(packed)
    here, rep = lax.axis_index("grid"), lax.axis_index("rep")
    row_blocks, _, cols = table.shape
    rows = square_keep.shape[0]
    col_blocks = cols // BLOCK
    first_col = rep * col_blocks

    def fill(i, _):
        for j in range(col_blocks):
            keep = pick(density_pattern, order, i, first_col + j)
            tile = jnp.full((TILE, BLOCK), keep, jnp.float32).astype(jnp.bfloat16)
            table[i, :, j * BLOCK:(j + 1) * BLOCK] = tile
        return 0

    lax.fori_loop(0, row_blocks, fill, 0, unroll=row_blocks <= 16)
    for q in range(reps):
        at = lax.rem(rep - q + reps, reps) * col_blocks
        keep = rows_mask(density_pattern, order, here * rows, rows, at, col_blocks)
        panel_keep[q] = keep.astype(jnp.bfloat16)
    for pattern, keep in ((square_pattern, square_keep), (cube_pattern, cube_keep)):
        keep[...] = rows_mask(pattern, order, here * rows, rows, first_col, col_blocks)


def panel_kernel(reps, panel_keep, *refs):
    panel, (left, own) = refs[:reps], refs[reps:]
    rep = lax.axis_index("rep")
    cols = panel[0].shape[1]
    for q in range(reps):
        at = pl.multiple_of(lax.rem(rep - q + reps, reps) * cols, BLOCK)
        part = panel[q][...] * panel_keep[q]
        left[:, pl.ds(at, cols)] = part
        if q == 0:
            own[...] = part


def masked_tile(source, at, table, stored_row):
    return source[at:at + TILE, :] * table[stored_row // BLOCK]


def stack_kernel(*refs):
    out, done = refs[-1], 0
    for ref in refs[:-1]:
        out[done:done + ref.shape[0], :] = ref[...]
        done += ref.shape[0]


def early_kernel(groups, late, dims, left, table, *refs):
    held, (band, partial) = refs[:len(groups)], refs[len(groups):]
    rows, cols = partial.shape
    for pieces, ref in zip(groups, held):
        done = 0
        for piece in pieces:
            row = source_row(piece, dims, rows)
            for at in range(0, piece[4] - piece[3], TILE):
                tile = masked_tile(ref, done, table, row + at)
                band[pl.ds(pl.multiple_of(row + at, TILE), TILE), :] = tile
                done += TILE
    for piece in late:
        count = piece[4] - piece[3]
        band[pl.ds(source_row(piece, dims, rows), count), :] = jnp.zeros((count, cols), band.dtype)
    partial[...] = jnp.dot(left[...], band[...], preferred_element_type=jnp.float32)


def late_kernel(late, dims, table, square_keep, left, old_band, partial, *refs):
    pieces, (band, tripled, square_half, window) = refs[:len(late)], refs[len(late):]
    rows, cols = partial.shape
    pair = dims[2]
    total = partial[...]
    for first in range(0, len(late), pair):
        base = late[first]
        start = source_row(base, dims, rows)
        start = start - lax.rem(start, rows * pair)
        low = jnp.minimum(start // BLOCK * BLOCK, band.shape[0] - window.shape[0])
        low = pl.multiple_of(low, BLOCK)
        window[...] = jnp.zeros(window.shape, window.dtype)
        for piece, ref in zip(late[first:first + pair], pieces[first:first + pair]):
            row = source_row(piece, dims, rows)
            for at in range(0, ref.shape[0], TILE):
                tile = masked_tile(ref, at, table, row + at)
                window[pl.ds(pl.multiple_of(row + at - low, TILE), TILE), :] = tile
                band[pl.ds(pl.multiple_of(row + at, TILE), TILE), :] = tile
        total += jnp.dot(
            left[:, pl.ds(low, window.shape[0])], window[...], preferred_element_type=jnp.float32
        )
    total *= square_keep[...]
    tripled[...] = 3.0 * total
    square_half[...] = total.astype(jnp.bfloat16)


def cube_kernel(shift, keep, half, band, before, out, *own_copies):
    rep, reps = lax.axis_index("rep"), lax.axis_size("rep")
    rows, cols = before.shape
    at = lax.rem(rep - shift + reps, reps)
    right = band[pl.ds(pl.multiple_of(at * cols, BLOCK), cols), :]
    part = jnp.dot(half[...], right, preferred_element_type=jnp.float32)
    if not own_copies:
        out[...] = before[...] - 2.0 * (part * keep[...])
        return
    staged, sent = own_copies
    copies = []
    for first in range(0, rows, TILE):
        down = slice(first, first + TILE)
        staged[down, :] = before[down, :] - 2.0 * (part[down, :] * keep[down, :])
        copies.append(
            pltpu.make_async_copy(staged.at[down], out.at[down], sent.at[first // TILE])
        )
        copies[-1].start()
    for copy in copies:
        copy.wait()


def shifted(own, reps):
    return [
        lax.ppermute(own, "rep", [(s, (s + q) % reps) for s in range(reps)])
        for q in range(1, reps)
    ]


def on_device(grid, reps, density, density_pattern, square_pattern, cube_pattern, block_order):
    rows, cols = density.shape
    order = grid * rows
    dims = factors(grid)
    outer, inner, pair = dims
    band_bytes = order * cols * 2
    room = min(3 * band_bytes + (4 << 20), 56 << 20)
    bf16, f32 = jnp.bfloat16, jnp.float32

    def call(kernel, name, flops, moved, out, operands, spec=None, out_specs=None, **more):
        return pl.pallas_call(
            kernel,
            out_shape=[jax.ShapeDtypeStruct(shape, dtype) for shape, dtype in out],
            in_specs=spec or [IN_VMEM] * len(operands),
            out_specs=out_specs or [IN_VMEM] * len(out),
            compiler_params=pltpu.CompilerParams(vmem_limit_bytes=room),
            cost_estimate=pl.CostEstimate(flops=flops, bytes_accessed=moved, transcendentals=0),
            name=name,
            **more,
        )(*operands)

    steps, hops = list(range(1, outer)), list(range(1, inner))
    last = outer // 2 if steps and hops else None
    before = [step for step in steps if step != last][-1:]

    held = {(0, 0): density}
    for step in steps:
        held[step, 0] = send(after(density), dims, 0, step)
    for hop in hops:
        held[0, hop] = send(after(density), dims, 1, hop)
    packed = jnp.concatenate(
        [density_pattern, square_pattern, cube_pattern, after(block_order)[None]], axis=0
    )
    table, panel_keep, square_keep, cube_keep = call(
        functools.partial(prepare_kernel, reps), "prepare", PLACE, 2 * band_bytes,
        [((order // BLOCK, TILE, cols), bf16), ((reps, rows, cols), bf16),
         ((rows, cols), f32), ((rows, cols), f32)],
        [packed], spec=[IN_SMEM],
    )
    for step in steps:
        for hop in hops:
            ready = [table] if step == last else []
            held[step, hop] = send(after(held[step, 0], *ready), dims, 1, hop)
    panel = shifted(after(density), reps)
    left, own = call(
        functools.partial(panel_kernel, reps), "panel", 4 * PLACE, 2 * band_bytes,
        [((rows, reps * cols), bf16), ((rows, cols), bf16)],
        [panel_keep, after(density), *panel],
    )

    lone = [(0, 0)] + [key for key in held if key[0] == last]
    lone += [key for key in held if key[0] in before and key[1]]
    stack = [key for key in held if key not in lone]
    whole = lambda key, core: (*key, core, 0, rows)
    early, late = [], []
    for key in lone:
        group = late if key[0] == last and key[1] else early
        group.append(([whole(key, 0)], held[key] if key != (0, 0) else own))
        if pair > 1:
            value = after(held[key], *([] if group is late else [left]))
            group.append(([whole(key, 1)], send(value, dims, 2, 1)))
    early += [([whole(key, 0)], held[key]) for key in stack]
    if pair > 1 and stack:
        ready = panel + ([held[last, 0]] if hops else [])
        (stacked,) = call(
            stack_kernel, "stack", 0, 0, [((len(stack) * rows, cols), bf16)],
            [after(held[key], *ready) for key in stack],
        )
        early.append(([whole(key, 1) for key in stack], send(after(stacked), dims, 2, 1)))
    late_pieces, late_values = [piece[0] for piece, _ in late], [value for _, value in late]

    band, partial = call(
        functools.partial(early_kernel, [pieces for pieces, _ in early], late_pieces, dims),
        "square_early", 2 * rows * order * cols, 2 * band_bytes,
        [((order, cols), bf16), ((rows, cols), f32)],
        [left, table, *[value for _, value in early]],
    )
    span = BLOCK - math.gcd(pair * rows, BLOCK) + pair * rows
    span = min((span + BLOCK - 1) // BLOCK * BLOCK, order)
    band, tripled, square_half = call(
        functools.partial(late_kernel, late_pieces, dims), "square_late",
        2 * rows * span * cols, 4 * rows * cols,
        [((order, cols), bf16), ((rows, cols), f32), ((rows, cols), bf16)],
        [table, square_keep, left, band, partial, *late_values],
        input_output_aliases={3: 0},
        scratch_shapes=[pltpu.VMEM((span, cols), bf16)],
    )
    out = tripled
    halves = [square_half] + shifted(square_half, reps)
    for shift, half in enumerate(halves):
        final = shift == len(halves) - 1
        scratch = [pltpu.VMEM((rows, cols), f32), pltpu.SemaphoreType.DMA((rows // TILE,))]
        (out,) = call(
            functools.partial(cube_kernel, shift), "cube_part",
            2 * rows * cols * cols, band_bytes // reps, [((rows, cols), f32)],
            [cube_keep, half, band, out], scratch_shapes=scratch if final else [],
            out_specs=[pl.BlockSpec(memory_space=pl.ANY)] if final else None,
        )
    return out


def solution(mesh):
    placed = (P("grid", "rep"), P(), P(), P(), P())
    return jax.shard_map(
        functools.partial(on_device, mesh.shape["grid"], mesh.shape["rep"]),
        mesh=mesh, in_specs=placed, out_specs=P("grid", "rep"), check_vma=False,
    )
```

```python
import functools
import math

import jax
import jax.numpy as jnp
from jax import lax
from jax.experimental import pallas as pl
from jax.experimental.pallas import tpu as pltpu
from jax.sharding import PartitionSpec as P

BLOCK = 128
TILE = 16
PLACE = 10**9
IN_SMEM = pl.BlockSpec(memory_space=pltpu.SMEM)
IN_VMEM = pl.BlockSpec(memory_space=pltpu.VMEM)


def factors(size):
    pair = 2 if size % 2 == 0 else 1
    rest = size // pair
    outer = 4 if rest % 4 == 0 else 1
    return outer, rest // outer, pair


def send(value, dims, axis, step):
    outer, inner, pair = dims
    pairs = []
    for source in range(outer * inner * pair):
        place = [source // (inner * pair), source // pair % inner, source % pair]
        place[axis] = (place[axis] + step) % dims[axis]
        pairs.append((source, (place[0] * inner + place[1]) * pair + place[2]))
    return lax.ppermute(value, "grid", pairs)


def source_row(piece, dims, rows):
    outer, inner, pair = dims
    here = lax.axis_index("grid")
    at = (here // (inner * pair), here // pair % inner, here % pair)
    z, x, c = [lax.rem(a - k + d, d) for a, k, d in zip(at, piece[:3], dims)]
    return pl.multiple_of(((z * inner + x) * pair + c) * rows + piece[3], TILE)


def after(value, *others):
    return lax.optimization_barrier((value,) + others)[0]


def pick(pattern, order, row_block, col_block):
    return pattern[order[row_block], order[col_block]].astype(jnp.float32)


def rows_mask(pattern, order, first_row, rows, first_col_block, col_blocks):
    top = first_row // BLOCK
    low = (first_row + rows - 1) // BLOCK
    split = (top + 1) * BLOCK - first_row
    upper = lax.broadcasted_iota(jnp.int32, (rows, BLOCK), 0) < split
    tiles = []
    for j in range(col_blocks):
        a = pick(pattern, order, top, first_col_block + j)
        b = pick(pattern, order, low, first_col_block + j)
        tiles.append(jnp.where(upper, a, b))
    return jnp.concatenate(tiles, axis=1)


def parts_of(packed):
    count = packed.shape[1]
    patterns = [packed.at[pl.ds(at * count, count), :] for at in range(3)]
    return (*patterns, packed.at[3 * count])


def prepare_kernel(reps, packed, table, panel_keep, square_keep, cube_keep):
    density_pattern, square_pattern, cube_pattern, order = parts_of(packed)
    here, rep = lax.axis_index("grid"), lax.axis_index("rep")
    row_blocks, _, cols = table.shape
    rows = square_keep.shape[0]
    col_blocks = cols // BLOCK
    first_col = rep * col_blocks

    def fill(i, _):
        for j in range(col_blocks):
            keep = pick(density_pattern, order, i, first_col + j)
            tile = jnp.full((TILE, BLOCK), keep, jnp.float32).astype(jnp.bfloat16)
            table[i, :, j * BLOCK:(j + 1) * BLOCK] = tile
        return 0

    lax.fori_loop(0, row_blocks, fill, 0, unroll=row_blocks <= 16)
    for q in range(reps):
        at = lax.rem(rep - q + reps, reps) * col_blocks
        keep = rows_mask(density_pattern, order, here * rows, rows, at, col_blocks)
        panel_keep[q] = keep.astype(jnp.bfloat16)
    for pattern, keep in ((square_pattern, square_keep), (cube_pattern, cube_keep)):
        keep[...] = rows_mask(pattern, order, here * rows, rows, first_col, col_blocks)


def panel_kernel(reps, panel_keep, *refs):
    panel, (left, own) = refs[:reps], refs[reps:]
    rep = lax.axis_index("rep")
    cols = panel[0].shape[1]
    for q in range(reps):
        at = pl.multiple_of(lax.rem(rep - q + reps, reps) * cols, BLOCK)
        part = panel[q][...] * panel_keep[q]
        left[:, pl.ds(at, cols)] = part
        if q == 0:
            own[...] = part


def masked_tile(source, at, table, stored_row):
    return source[at:at + TILE, :] * table[stored_row // BLOCK]


def stack_kernel(*refs):
    out, done = refs[-1], 0
    for ref in refs[:-1]:
        out[done:done + ref.shape[0], :] = ref[...]
        done += ref.shape[0]


def early_kernel(groups, late, dims, left, table, *refs):
    held, (band, partial) = refs[:len(groups)], refs[len(groups):]
    rows, cols = partial.shape
    for pieces, ref in zip(groups, held):
        done = 0
        for piece in pieces:
            row = source_row(piece, dims, rows)
            for at in range(0, piece[4] - piece[3], TILE):
                tile = masked_tile(ref, done, table, row + at)
                band[pl.ds(pl.multiple_of(row + at, TILE), TILE), :] = tile
                done += TILE
    for piece in late:
        count = piece[4] - piece[3]
        band[pl.ds(source_row(piece, dims, rows), count), :] = jnp.zeros((count, cols), band.dtype)
    partial[...] = jnp.dot(left[...], band[...], preferred_element_type=jnp.float32)


def late_kernel(late, dims, table, square_keep, left, old_band, partial, *refs):
    pieces, (band, tripled, square_half, window) = refs[:len(late)], refs[len(late):]
    rows, cols = partial.shape
    pair = dims[2]
    total = partial[...]
    for first in range(0, len(late), pair):
        base = late[first]
        start = source_row(base, dims, rows)
        start = start - lax.rem(start, rows * pair)
        low = jnp.minimum(start // BLOCK * BLOCK, band.shape[0] - window.shape[0])
        low = pl.multiple_of(low, BLOCK)
        window[...] = jnp.zeros(window.shape, window.dtype)
        for piece, ref in zip(late[first:first + pair], pieces[first:first + pair]):
            row = source_row(piece, dims, rows)
            for at in range(0, ref.shape[0], TILE):
                tile = masked_tile(ref, at, table, row + at)
                window[pl.ds(pl.multiple_of(row + at - low, TILE), TILE), :] = tile
                band[pl.ds(pl.multiple_of(row + at, TILE), TILE), :] = tile
        total += jnp.dot(
            left[:, pl.ds(low, window.shape[0])], window[...], preferred_element_type=jnp.float32
        )
    total *= square_keep[...]
    tripled[...] = 3.0 * total
    square_half[...] = total.astype(jnp.bfloat16)


def cube_kernel(shift, keep, half, band, before, out, *own_copies):
    rep, reps = lax.axis_index("rep"), lax.axis_size("rep")
    rows, cols = before.shape
    at = lax.rem(rep - shift + reps, reps)
    right = band[pl.ds(pl.multiple_of(at * cols, BLOCK), cols), :]
    part = jnp.dot(half[...], right, preferred_element_type=jnp.float32)
    if not own_copies:
        out[...] = before[...] - 2.0 * (part * keep[...])
        return
    staged, sent = own_copies
    copies = []
    for first in range(0, rows, TILE):
        down = slice(first, first + TILE)
        staged[down, :] = before[down, :] - 2.0 * (part[down, :] * keep[down, :])
        copies.append(
            pltpu.make_async_copy(staged.at[down], out.at[down], sent.at[first // TILE])
        )
        copies[-1].start()
    for copy in copies:
        copy.wait()


def shifted(own, reps):
    return [
        lax.ppermute(own, "rep", [(s, (s + q) % reps) for s in range(reps)])
        for q in range(1, reps)
    ]


def on_device(grid, reps, density, density_pattern, square_pattern, cube_pattern, block_order):
    rows, cols = density.shape
    order = grid * rows
    dims = factors(grid)
    outer, inner, pair = dims
    band_bytes = order * cols * 2
    room = min(3 * band_bytes + (4 << 20), 56 << 20)
    bf16, f32 = jnp.bfloat16, jnp.float32

    def call(kernel, name, flops, moved, out, operands, spec=None, out_specs=None, **more):
        return pl.pallas_call(
            kernel,
            out_shape=[jax.ShapeDtypeStruct(shape, dtype) for shape, dtype in out],
            in_specs=spec or [IN_VMEM] * len(operands),
            out_specs=out_specs or [IN_VMEM] * len(out),
            compiler_params=pltpu.CompilerParams(vmem_limit_bytes=room),
            cost_estimate=pl.CostEstimate(flops=flops, bytes_accessed=moved, transcendentals=0),
            name=name,
            **more,
        )(*operands)

    steps, hops = list(range(1, outer)), list(range(1, inner))
    last = steps[-1] if steps and hops else None
    before = [step for step in steps if step != last][-1:]

    held = {(0, 0): density}
    for step in steps:
        held[step, 0] = send(after(density), dims, 0, step)
    for hop in hops:
        held[0, hop] = send(after(density), dims, 1, hop)
    packed = jnp.concatenate(
        [density_pattern, square_pattern, cube_pattern, after(block_order)[None]], axis=0
    )
    table, panel_keep, square_keep, cube_keep = call(
        functools.partial(prepare_kernel, reps), "prepare", PLACE, 2 * band_bytes,
        [((order // BLOCK, TILE, cols), bf16), ((reps, rows, cols), bf16),
         ((rows, cols), f32), ((rows, cols), f32)],
        [packed], spec=[IN_SMEM],
    )
    for step in steps:
        for hop in hops:
            ready = [table] if step == last else []
            held[step, hop] = send(after(held[step, 0], *ready), dims, 1, hop)
    panel = shifted(after(density), reps)
    left, own = call(
        functools.partial(panel_kernel, reps), "panel", 4 * PLACE, 2 * band_bytes,
        [((rows, reps * cols), bf16), ((rows, cols), bf16)],
        [panel_keep, after(density), *panel],
    )

    lone = [(0, 0)] + [key for key in held if key[0] == last]
    lone += [key for key in held if key[0] in before and key[1]]
    stack = [key for key in held if key not in lone]
    whole = lambda key, core: (*key, core, 0, rows)
    early, late = [], []
    for key in lone:
        group = late if key[0] == last and key[1] else early
        group.append(([whole(key, 0)], held[key] if key != (0, 0) else own))
        if pair > 1:
            value = after(held[key], *([] if group is late else [left]))
            group.append(([whole(key, 1)], send(value, dims, 2, 1)))
    early += [([whole(key, 0)], held[key]) for key in stack]
    if pair > 1 and stack:
        ready = panel + ([held[last, 0]] if hops else [])
        (stacked,) = call(
            stack_kernel, "stack", 0, 0, [((len(stack) * rows, cols), bf16)],
            [after(held[key], *ready) for key in stack],
        )
        early.append(([whole(key, 1) for key in stack], send(after(stacked), dims, 2, 1)))
    late_pieces, late_values = [piece[0] for piece, _ in late], [value for _, value in late]

    band, partial = call(
        functools.partial(early_kernel, [pieces for pieces, _ in early], late_pieces, dims),
        "square_early", 2 * rows * order * cols, 2 * band_bytes,
        [((order, cols), bf16), ((rows, cols), f32)],
        [left, table, *[value for _, value in early]],
    )
    span = BLOCK - math.gcd(pair * rows, BLOCK) + pair * rows
    span = min((span + BLOCK - 1) // BLOCK * BLOCK, order)
    band, tripled, square_half = call(
        functools.partial(late_kernel, late_pieces, dims), "square_late",
        2 * rows * span * cols, 4 * rows * cols,
        [((order, cols), bf16), ((rows, cols), f32), ((rows, cols), bf16)],
        [table, square_keep, left, band, partial, *late_values],
        input_output_aliases={3: 0},
        scratch_shapes=[pltpu.VMEM((span, cols), bf16)],
    )
    out = tripled
    halves = [square_half] + shifted(square_half, reps)
    for shift, half in enumerate(halves):
        final = shift == len(halves) - 1
        scratch = [pltpu.VMEM((rows, cols), f32), pltpu.SemaphoreType.DMA((rows // TILE,))]
        (out,) = call(
            functools.partial(cube_kernel, shift), "cube_part",
            2 * rows * cols * cols, band_bytes // reps, [((rows, cols), f32)],
            [cube_keep, half, band, out], scratch_shapes=scratch if final else [],
            out_specs=[pl.BlockSpec(memory_space=pl.ANY)] if final else None,
        )
    return out


def solution(mesh):
    placed = (P("grid", "rep"), P(), P(), P(), P())
    return jax.shard_map(
        functools.partial(on_device, mesh.shape["grid"], mesh.shape["rep"]),
        mesh=mesh, in_specs=placed, out_specs=P("grid", "rep"), check_vma=False,
    )
```

```python
import functools
import math

import jax
import jax.numpy as jnp
from jax import lax
from jax.experimental import pallas as pl
from jax.experimental.pallas import tpu as pltpu
from jax.sharding import PartitionSpec as P

BLOCK = 128
TILE = 16
PLACE = 10**9
IN_SMEM = pl.BlockSpec(memory_space=pltpu.SMEM)
IN_VMEM = pl.BlockSpec(memory_space=pltpu.VMEM)


def factors(size):
    pair = 2 if size % 2 == 0 else 1
    rest = size // pair
    outer = 4 if rest % 4 == 0 else 1
    return outer, rest // outer, pair


def send(value, dims, axis, step):
    outer, inner, pair = dims
    pairs = []
    for source in range(outer * inner * pair):
        place = [source // (inner * pair), source // pair % inner, source % pair]
        place[axis] = (place[axis] + step) % dims[axis]
        pairs.append((source, (place[0] * inner + place[1]) * pair + place[2]))
    return lax.ppermute(value, "grid", pairs)


def send_planes(value, dims, moves):
    plane = dims[1] * dims[2]
    pairs = [(a * plane + i, b * plane + i) for a, b in moves for i in range(plane)]
    return lax.ppermute(value, "grid", pairs)


def source_row(piece, dims, rows):
    outer, inner, pair = dims
    here = lax.axis_index("grid")
    at = (here // (inner * pair), here // pair % inner, here % pair)
    z, x, c = [lax.rem(a - k + d, d) for a, k, d in zip(at, piece[:3], dims)]
    return pl.multiple_of(((z * inner + x) * pair + c) * rows + piece[3], TILE)


def after(value, *others):
    return lax.optimization_barrier((value,) + others)[0]


def pick(pattern, order, row_block, col_block):
    return pattern[order[row_block], order[col_block]].astype(jnp.float32)


def rows_mask(pattern, order, first_row, rows, first_col_block, col_blocks):
    top = first_row // BLOCK
    low = (first_row + rows - 1) // BLOCK
    split = (top + 1) * BLOCK - first_row
    upper = lax.broadcasted_iota(jnp.int32, (rows, BLOCK), 0) < split
    tiles = []
    for j in range(col_blocks):
        a = pick(pattern, order, top, first_col_block + j)
        b = pick(pattern, order, low, first_col_block + j)
        tiles.append(jnp.where(upper, a, b))
    return jnp.concatenate(tiles, axis=1)


def parts_of(packed):
    count = packed.shape[1]
    patterns = [packed.at[pl.ds(at * count, count), :] for at in range(3)]
    return (*patterns, packed.at[3 * count])


def prepare_kernel(reps, packed, table, panel_keep, square_keep, cube_keep):
    density_pattern, square_pattern, cube_pattern, order = parts_of(packed)
    here, rep = lax.axis_index("grid"), lax.axis_index("rep")
    row_blocks, _, cols = table.shape
    rows = square_keep.shape[0]
    col_blocks = cols // BLOCK
    first_col = rep * col_blocks

    def fill(i, _):
        for j in range(col_blocks):
            keep = pick(density_pattern, order, i, first_col + j)
            tile = jnp.full((TILE, BLOCK), keep, jnp.float32).astype(jnp.bfloat16)
            table[i, :, j * BLOCK:(j + 1) * BLOCK] = tile
        return 0

    lax.fori_loop(0, row_blocks, fill, 0, unroll=row_blocks <= 16)
    for q in range(reps):
        at = lax.rem(rep - q + reps, reps) * col_blocks
        keep = rows_mask(density_pattern, order, here * rows, rows, at, col_blocks)
        panel_keep[q] = keep.astype(jnp.bfloat16)
    for pattern, keep in ((square_pattern, square_keep), (cube_pattern, cube_keep)):
        keep[...] = rows_mask(pattern, order, here * rows, rows, first_col, col_blocks)


def panel_kernel(reps, panel_keep, *refs):
    panel, (left, own) = refs[:reps], refs[reps:]
    rep = lax.axis_index("rep")
    cols = panel[0].shape[1]
    for q in range(reps):
        at = pl.multiple_of(lax.rem(rep - q + reps, reps) * cols, BLOCK)
        part = panel[q][...] * panel_keep[q]
        left[:, pl.ds(at, cols)] = part
        if q == 0:
            own[...] = part


def masked_tile(source, at, table, stored_row):
    return source[at:at + TILE, :] * table[stored_row // BLOCK]


def merge_kernel(one, other, out):
    out[...] = one[...] + other[...]


def stack_kernel(*refs):
    out, done = refs[-1], 0
    for ref in refs[:-1]:
        out[done:done + ref.shape[0], :] = ref[...]
        done += ref.shape[0]


def early_kernel(groups, late, dims, left, table, *refs):
    held, (band, partial) = refs[:len(groups)], refs[len(groups):]
    rows, cols = partial.shape
    for pieces, ref in zip(groups, held):
        done = 0
        for piece in pieces:
            row = source_row(piece, dims, rows)
            for at in range(0, piece[4] - piece[3], TILE):
                tile = masked_tile(ref, done, table, row + at)
                band[pl.ds(pl.multiple_of(row + at, TILE), TILE), :] = tile
                done += TILE
    for piece in late:
        count = piece[4] - piece[3]
        band[pl.ds(source_row(piece, dims, rows), count), :] = jnp.zeros((count, cols), band.dtype)
    partial[...] = jnp.dot(left[...], band[...], preferred_element_type=jnp.float32)


def late_kernel(late, dims, table, square_keep, left, old_band, partial, *refs):
    pieces, (band, tripled, square_half, window) = refs[:len(late)], refs[len(late):]
    rows, cols = partial.shape
    pair = dims[2]
    total = partial[...]
    for first in range(0, len(late), pair):
        base = late[first]
        start = source_row(base, dims, rows)
        start = start - lax.rem(start, rows * pair)
        low = jnp.minimum(start // BLOCK * BLOCK, band.shape[0] - window.shape[0])
        low = pl.multiple_of(low, BLOCK)
        window[...] = jnp.zeros(window.shape, window.dtype)
        for piece, ref in zip(late[first:first + pair], pieces[first:first + pair]):
            row = source_row(piece, dims, rows)
            for at in range(0, ref.shape[0], TILE):
                tile = masked_tile(ref, at, table, row + at)
                window[pl.ds(pl.multiple_of(row + at - low, TILE), TILE), :] = tile
                band[pl.ds(pl.multiple_of(row + at, TILE), TILE), :] = tile
        total += jnp.dot(
            left[:, pl.ds(low, window.shape[0])], window[...], preferred_element_type=jnp.float32
        )
    total *= square_keep[...]
    tripled[...] = 3.0 * total
    square_half[...] = total.astype(jnp.bfloat16)


def cube_kernel(shift, keep, half, band, before, out):
    rep, reps = lax.axis_index("rep"), lax.axis_size("rep")
    cols = before.shape[1]
    at = lax.rem(rep - shift + reps, reps)
    right = band[pl.ds(pl.multiple_of(at * cols, BLOCK), cols), :]
    part = jnp.dot(half[...], right, preferred_element_type=jnp.float32)
    out[...] = before[...] - 2.0 * (part * keep[...])


def shifted(own, reps):
    return [
        lax.ppermute(own, "rep", [(s, (s + q) % reps) for s in range(reps)])
        for q in range(1, reps)
    ]


def on_device(grid, reps, density, density_pattern, square_pattern, cube_pattern, block_order):
    rows, cols = density.shape
    order = grid * rows
    dims = factors(grid)
    outer, inner, pair = dims
    band_bytes = order * cols * 2
    room = min(3 * band_bytes + (4 << 20), 56 << 20)
    bf16, f32 = jnp.bfloat16, jnp.float32

    def call(kernel, name, flops, moved, out, operands, spec=None, **more):
        return pl.pallas_call(
            kernel,
            out_shape=[jax.ShapeDtypeStruct(shape, dtype) for shape, dtype in out],
            in_specs=spec or [IN_VMEM] * len(operands),
            out_specs=[IN_VMEM] * len(out),
            compiler_params=pltpu.CompilerParams(vmem_limit_bytes=room),
            cost_estimate=pl.CostEstimate(flops=flops, bytes_accessed=moved, transcendentals=0),
            name=name,
            **more,
        )(*operands)

    steps, hops = list(range(1, outer)), list(range(1, inner))
    last = outer // 2 if steps and hops else None
    before = [step for step in steps if step != last][-1:]

    held = {(0, 0): density}
    for step in steps:
        if step != last:
            held[step, 0] = send(after(density), dims, 0, step)
    for hop in hops:
        held[0, hop] = send(after(density), dims, 1, hop)
    if last:
        first = send_planes(after(density), dims, ((0, 2), (1, 3), (2, 0)))
        held_back = after(density, held[1, 0], *[held[0, hop] for hop in hops])
        second = send_planes(held_back, dims, ((3, 1),))
        (held[last, 0],) = call(
            merge_kernel, "merge", 0, 0, [((rows, cols), bf16)], [first, second]
        )
    packed = jnp.concatenate(
        [density_pattern, square_pattern, cube_pattern, after(block_order)[None]], axis=0
    )
    table, panel_keep, square_keep, cube_keep = call(
        functools.partial(prepare_kernel, reps), "prepare", PLACE, 2 * band_bytes,
        [((order // BLOCK, TILE, cols), bf16), ((reps, rows, cols), bf16),
         ((rows, cols), f32), ((rows, cols), f32)],
        [packed], spec=[IN_SMEM],
    )
    for step in steps:
        for hop in hops:
            held[step, hop] = send(after(held[step, 0]), dims, 1, hop)
    panel = shifted(after(density), reps)
    left, own = call(
        functools.partial(panel_kernel, reps), "panel", 4 * PLACE, 2 * band_bytes,
        [((rows, reps * cols), bf16), ((rows, cols), bf16)],
        [panel_keep, after(density), *panel],
    )

    keys = [(0, 0)] + [(0, hop) for hop in hops] + [(step, 0) for step in steps]
    keys += [(step, hop) for step in steps for hop in hops]
    lone = [(0, 0)] + [key for key in keys if key[0] == last or key[0] in before and key[1]]
    stack = [key for key in keys if key not in lone]
    whole = lambda key, core: (*key, core, 0, rows)
    early, late = [], []
    for key in keys:
        group = late if key[0] == last and key[1] else early
        group.append(([whole(key, 0)], held[key] if key != (0, 0) else own))
        if pair > 1 and key in lone:
            value = after(held[key], *([] if group is late else [left]))
            group.append(([whole(key, 1)], send(value, dims, 2, 1)))
    if pair > 1 and stack:
        ready = panel + ([held[last, 0], table] if last else [])
        (stacked,) = call(
            stack_kernel, "stack", 0, 0, [((len(stack) * rows, cols), bf16)],
            [after(held[key], *ready) for key in stack],
        )
        early.append(([whole(key, 1) for key in stack], send(after(stacked), dims, 2, 1)))
    late_pieces, late_values = [piece[0] for piece, _ in late], [value for _, value in late]

    band, partial = call(
        functools.partial(early_kernel, [pieces for pieces, _ in early], late_pieces, dims),
        "square_early", 2 * rows * order * cols, 2 * band_bytes,
        [((order, cols), bf16), ((rows, cols), f32)],
        [left, table, *[value for _, value in early]],
    )
    span = BLOCK - math.gcd(pair * rows, BLOCK) + pair * rows
    span = min((span + BLOCK - 1) // BLOCK * BLOCK, order)
    band, tripled, square_half = call(
        functools.partial(late_kernel, late_pieces, dims), "square_late",
        2 * rows * span * cols, 4 * rows * cols,
        [((order, cols), bf16), ((rows, cols), f32), ((rows, cols), bf16)],
        [table, square_keep, left, band, partial, *late_values],
        input_output_aliases={3: 0},
        scratch_shapes=[pltpu.VMEM((span, cols), bf16)],
    )
    out = tripled
    for shift, half in enumerate([square_half] + shifted(square_half, reps)):
        (out,) = call(
            functools.partial(cube_kernel, shift), "cube_part",
            2 * rows * cols * cols, band_bytes // reps, [((rows, cols), f32)],
            [cube_keep, half, band, out],
        )
    return out


def solution(mesh):
    placed = (P("grid", "rep"), P(), P(), P(), P())
    return jax.shard_map(
        functools.partial(on_device, mesh.shape["grid"], mesh.shape["rep"]),
        mesh=mesh, in_specs=placed, out_specs=P("grid", "rep"), check_vma=False,
    )
```

```python
import functools
import math

import jax
import jax.numpy as jnp
from jax import lax
from jax.experimental import pallas as pl
from jax.experimental.pallas import tpu as pltpu
from jax.sharding import PartitionSpec as P

BLOCK = 128
TILE = 16
PLACE = 10**9
IN_SMEM = pl.BlockSpec(memory_space=pltpu.SMEM)
IN_VMEM = pl.BlockSpec(memory_space=pltpu.VMEM)


def factors(size):
    pair = 2 if size % 2 == 0 else 1
    rest = size // pair
    outer = 4 if rest % 4 == 0 else 1
    return outer, rest // outer, pair


def send(value, dims, axis, step):
    outer, inner, pair = dims
    pairs = []
    for source in range(outer * inner * pair):
        place = [source // (inner * pair), source // pair % inner, source % pair]
        place[axis] = (place[axis] + step) % dims[axis]
        pairs.append((source, (place[0] * inner + place[1]) * pair + place[2]))
    return lax.ppermute(value, "grid", pairs)


def source_row(piece, dims, rows):
    outer, inner, pair = dims
    here = lax.axis_index("grid")
    at = (here // (inner * pair), here // pair % inner, here % pair)
    z, x, c = [lax.rem(a - k + d, d) for a, k, d in zip(at, piece[:3], dims)]
    return pl.multiple_of(((z * inner + x) * pair + c) * rows + piece[3], TILE)


def after(value, *others):
    return lax.optimization_barrier((value,) + others)[0]


def pick(pattern, order, row_block, col_block):
    return pattern[order[row_block], order[col_block]].astype(jnp.float32)


def rows_mask(pattern, order, first_row, rows, first_col_block, col_blocks):
    top = first_row // BLOCK
    low = (first_row + rows - 1) // BLOCK
    split = (top + 1) * BLOCK - first_row
    upper = lax.broadcasted_iota(jnp.int32, (rows, BLOCK), 0) < split
    tiles = []
    for j in range(col_blocks):
        a = pick(pattern, order, top, first_col_block + j)
        b = pick(pattern, order, low, first_col_block + j)
        tiles.append(jnp.where(upper, a, b))
    return jnp.concatenate(tiles, axis=1)


def parts_of(packed):
    count = packed.shape[1]
    patterns = [packed.at[pl.ds(at * count, count), :] for at in range(3)]
    return (*patterns, packed.at[3 * count])


def prepare_kernel(reps, packed, table, panel_keep, square_keep, cube_keep):
    density_pattern, square_pattern, cube_pattern, order = parts_of(packed)
    here, rep = lax.axis_index("grid"), lax.axis_index("rep")
    row_blocks, _, cols = table.shape
    rows = square_keep.shape[0]
    col_blocks = cols // BLOCK
    first_col = rep * col_blocks

    def fill(i, _):
        for j in range(col_blocks):
            keep = pick(density_pattern, order, i, first_col + j)
            tile = jnp.full((TILE, BLOCK), keep, jnp.float32).astype(jnp.bfloat16)
            table[i, :, j * BLOCK:(j + 1) * BLOCK] = tile
        return 0

    lax.fori_loop(0, row_blocks, fill, 0, unroll=row_blocks <= 16)
    for q in range(reps):
        at = lax.rem(rep - q + reps, reps) * col_blocks
        keep = rows_mask(density_pattern, order, here * rows, rows, at, col_blocks)
        panel_keep[q] = keep.astype(jnp.bfloat16)
    for pattern, keep in ((square_pattern, square_keep), (cube_pattern, cube_keep)):
        keep[...] = rows_mask(pattern, order, here * rows, rows, first_col, col_blocks)


def panel_kernel(reps, panel_keep, *refs):
    panel, (left, own) = refs[:reps], refs[reps:]
    rep = lax.axis_index("rep")
    cols = panel[0].shape[1]
    for q in range(reps):
        at = pl.multiple_of(lax.rem(rep - q + reps, reps) * cols, BLOCK)
        part = panel[q][...] * panel_keep[q]
        left[:, pl.ds(at, cols)] = part
        if q == 0:
            own[...] = part


def masked_tile(source, at, table, stored_row):
    return source[at:at + TILE, :] * table[stored_row // BLOCK]


def stack_kernel(*refs):
    out, done = refs[-1], 0
    for ref in refs[:-1]:
        out[done:done + ref.shape[0], :] = ref[...]
        done += ref.shape[0]


def early_kernel(groups, late, dims, left, table, *refs):
    held, (band, partial) = refs[:len(groups)], refs[len(groups):]
    rows, cols = partial.shape
    for pieces, ref in zip(groups, held):
        done = 0
        for piece in pieces:
            row = source_row(piece, dims, rows)
            for at in range(0, piece[4] - piece[3], TILE):
                tile = masked_tile(ref, done, table, row + at)
                band[pl.ds(pl.multiple_of(row + at, TILE), TILE), :] = tile
                done += TILE
    for piece in late:
        count = piece[4] - piece[3]
        band[pl.ds(source_row(piece, dims, rows), count), :] = jnp.zeros((count, cols), band.dtype)
    partial[...] = jnp.dot(left[...], band[...], preferred_element_type=jnp.float32)


def late_kernel(late, dims, table, square_keep, left, old_band, partial, *refs):
    pieces, (band, tripled, square_half, window) = refs[:len(late)], refs[len(late):]
    rows, cols = partial.shape
    pair = dims[2]
    total = partial[...]
    for first in range(0, len(late), pair):
        base = late[first]
        start = source_row(base, dims, rows)
        start = start - lax.rem(start, rows * pair)
        low = jnp.minimum(start // BLOCK * BLOCK, band.shape[0] - window.shape[0])
        low = pl.multiple_of(low, BLOCK)
        window[...] = jnp.zeros(window.shape, window.dtype)
        for piece, ref in zip(late[first:first + pair], pieces[first:first + pair]):
            row = source_row(piece, dims, rows)
            for at in range(0, ref.shape[0], TILE):
                tile = masked_tile(ref, at, table, row + at)
                window[pl.ds(pl.multiple_of(row + at - low, TILE), TILE), :] = tile
                band[pl.ds(pl.multiple_of(row + at, TILE), TILE), :] = tile
        total += jnp.dot(
            left[:, pl.ds(low, window.shape[0])], window[...], preferred_element_type=jnp.float32
        )
    total *= square_keep[...]
    tripled[...] = 3.0 * total
    square_half[...] = total.astype(jnp.bfloat16)


def cube_kernel(shift, keep, half, band, before, out):
    rep, reps = lax.axis_index("rep"), lax.axis_size("rep")
    cols = before.shape[1]
    at = lax.rem(rep - shift + reps, reps)
    right = band[pl.ds(pl.multiple_of(at * cols, BLOCK), cols), :]
    part = jnp.dot(half[...], right, preferred_element_type=jnp.float32)
    out[...] = before[...] - 2.0 * (part * keep[...])


def shifted(own, reps):
    return [
        lax.ppermute(own, "rep", [(s, (s + q) % reps) for s in range(reps)])
        for q in range(1, reps)
    ]


def on_device(grid, reps, density, density_pattern, square_pattern, cube_pattern, block_order):
    rows, cols = density.shape
    order = grid * rows
    dims = factors(grid)
    outer, inner, pair = dims
    band_bytes = order * cols * 2
    room = min(3 * band_bytes + (4 << 20), 56 << 20)
    bf16, f32 = jnp.bfloat16, jnp.float32

    def call(kernel, name, flops, moved, out, operands, spec=None, **more):
        return pl.pallas_call(
            kernel,
            out_shape=[jax.ShapeDtypeStruct(shape, dtype) for shape, dtype in out],
            in_specs=spec or [IN_VMEM] * len(operands),
            out_specs=[IN_VMEM] * len(out),
            compiler_params=pltpu.CompilerParams(vmem_limit_bytes=room),
            cost_estimate=pl.CostEstimate(flops=flops, bytes_accessed=moved, transcendentals=0),
            name=name,
            **more,
        )(*operands)

    steps, hops = list(range(1, outer)), list(range(1, inner))
    last = outer // 2 if steps and hops else None
    before = [step for step in steps if step != last][-1:]

    held = {(0, 0): density}
    for step in steps:
        held[step, 0] = send(after(density), dims, 0, step)
    for hop in hops:
        held[0, hop] = send(after(density), dims, 1, hop)
    packed = jnp.concatenate(
        [density_pattern, square_pattern, cube_pattern, after(block_order)[None]], axis=0
    )
    table, panel_keep, square_keep, cube_keep = call(
        functools.partial(prepare_kernel, reps), "prepare", PLACE, 2 * band_bytes,
        [((order // BLOCK, TILE, cols), bf16), ((reps, rows, cols), bf16),
         ((rows, cols), f32), ((rows, cols), f32)],
        [packed], spec=[IN_SMEM],
    )
    for step in steps:
        for hop in hops:
            ready = [table] if step == last else []
            held[step, hop] = send(after(held[step, 0], *ready), dims, 1, hop)
    panel = shifted(after(density), reps)
    left, own = call(
        functools.partial(panel_kernel, reps), "panel", 4 * PLACE, 2 * band_bytes,
        [((rows, reps * cols), bf16), ((rows, cols), bf16)],
        [panel_keep, after(density), *panel],
    )

    keys = [(0, 0)] + [(step, 0) for step in steps if step not in before]
    keys += [(0, hop) for hop in hops] + [(step, 0) for step in before]
    keys += [(step, hop) for step in steps for hop in hops]
    lone = [(0, 0)] + [key for key in keys if key[0] == last or key[0] in before and key[1]]
    stack = [key for key in keys if key not in lone]
    whole = lambda key, core: (*key, core, 0, rows)
    early, late = [], []
    for key in keys:
        group = late if key[0] == last and key[1] else early
        group.append(([whole(key, 0)], held[key] if key != (0, 0) else own))
        if pair > 1 and key in lone:
            value = after(held[key], *([] if group is late else [left]))
            group.append(([whole(key, 1)], send(value, dims, 2, 1)))
    if pair > 1 and stack:
        ready = panel + ([held[last, 0]] if hops else [])
        (stacked,) = call(
            stack_kernel, "stack", 0, 0, [((len(stack) * rows, cols), bf16)],
            [after(held[key], *ready) for key in stack],
        )
        early.append(([whole(key, 1) for key in stack], send(after(stacked), dims, 2, 1)))
    late_pieces, late_values = [piece[0] for piece, _ in late], [value for _, value in late]

    band, partial = call(
        functools.partial(early_kernel, [pieces for pieces, _ in early], late_pieces, dims),
        "square_early", 2 * rows * order * cols, 2 * band_bytes,
        [((order, cols), bf16), ((rows, cols), f32)],
        [left, table, *[value for _, value in early]],
    )
    span = BLOCK - math.gcd(pair * rows, BLOCK) + pair * rows
    span = min((span + BLOCK - 1) // BLOCK * BLOCK, order)
    band, tripled, square_half = call(
        functools.partial(late_kernel, late_pieces, dims), "square_late",
        2 * rows * span * cols, 4 * rows * cols,
        [((order, cols), bf16), ((rows, cols), f32), ((rows, cols), bf16)],
        [table, square_keep, left, band, partial, *late_values],
        input_output_aliases={3: 0},
        scratch_shapes=[pltpu.VMEM((span, cols), bf16)],
    )
    out = tripled
    for shift, half in enumerate([square_half] + shifted(square_half, reps)):
        (out,) = call(
            functools.partial(cube_kernel, shift), "cube_part",
            2 * rows * cols * cols, band_bytes // reps, [((rows, cols), f32)],
            [cube_keep, half, band, out],
        )
    return out


def solution(mesh):
    placed = (P("grid", "rep"), P(), P(), P(), P())
    return jax.shard_map(
        functools.partial(on_device, mesh.shape["grid"], mesh.shape["rep"]),
        mesh=mesh, in_specs=placed, out_specs=P("grid", "rep"), check_vma=False,
    )
```

```python
import functools
import math

import jax
import jax.numpy as jnp
from jax import lax
from jax.experimental import pallas as pl
from jax.experimental.pallas import tpu as pltpu
from jax.sharding import PartitionSpec as P

BLOCK = 128
TILE = 16
SOURCES = ((0, 1, 2, 3), (1, 0, 3, 2), (2, 3, 1, 0), (3, 2, 0, 1))
PLACE = 10**9
IN_SMEM = pl.BlockSpec(memory_space=pltpu.SMEM)
IN_VMEM = pl.BlockSpec(memory_space=pltpu.VMEM)


def factors(size):
    pair = 2 if size % 2 == 0 else 1
    rest = size // pair
    outer = 4 if rest % 4 == 0 else 1
    return outer, rest // outer, pair


def send(value, dims, axis, step):
    outer, inner, pair = dims
    pairs = []
    for target in range(outer * inner * pair):
        place = [target // (inner * pair), target // pair % inner, target % pair]
        if axis == 0:
            place[0] = SOURCES[step][place[0]]
        else:
            place[axis] = (place[axis] - step) % dims[axis]
        pairs.append(((place[0] * inner + place[1]) * pair + place[2], target))
    return lax.ppermute(value, "grid", sorted(pairs))


def source_row(piece, dims, rows):
    outer, inner, pair = dims
    here = lax.axis_index("grid")
    at = (here // (inner * pair), here // pair % inner, here % pair)
    z = at[0]
    if piece[0]:
        z = jnp.int32(SOURCES[piece[0]][0])
        for plane in range(1, outer):
            z = jnp.where(at[0] == plane, SOURCES[piece[0]][plane], z)
    x, c = [lax.rem(a - k + d, d) for a, k, d in zip(at[1:], piece[1:3], dims[1:])]
    return pl.multiple_of(((z * inner + x) * pair + c) * rows + piece[3], TILE)


def after(value, *others):
    return lax.optimization_barrier((value,) + others)[0]


def pick(pattern, order, row_block, col_block):
    return pattern[order[row_block], order[col_block]].astype(jnp.float32)


def rows_mask(pattern, order, first_row, rows, first_col_block, col_blocks):
    top = first_row // BLOCK
    low = (first_row + rows - 1) // BLOCK
    split = (top + 1) * BLOCK - first_row
    upper = lax.broadcasted_iota(jnp.int32, (rows, BLOCK), 0) < split
    tiles = []
    for j in range(col_blocks):
        a = pick(pattern, order, top, first_col_block + j)
        b = pick(pattern, order, low, first_col_block + j)
        tiles.append(jnp.where(upper, a, b))
    return jnp.concatenate(tiles, axis=1)


def parts_of(packed):
    count = packed.shape[1]
    patterns = [packed.at[pl.ds(at * count, count), :] for at in range(3)]
    return (*patterns, packed.at[3 * count])


def prepare_kernel(reps, packed, table, panel_keep, square_keep, cube_keep):
    density_pattern, square_pattern, cube_pattern, order = parts_of(packed)
    here, rep = lax.axis_index("grid"), lax.axis_index("rep")
    row_blocks, _, cols = table.shape
    rows = square_keep.shape[0]
    col_blocks = cols // BLOCK
    first_col = rep * col_blocks

    def fill(i, _):
        for j in range(col_blocks):
            keep = pick(density_pattern, order, i, first_col + j)
            tile = jnp.full((TILE, BLOCK), keep, jnp.float32).astype(jnp.bfloat16)
            table[i, :, j * BLOCK:(j + 1) * BLOCK] = tile
        return 0

    lax.fori_loop(0, row_blocks, fill, 0, unroll=row_blocks <= 16)
    for q in range(reps):
        at = lax.rem(rep - q + reps, reps) * col_blocks
        keep = rows_mask(density_pattern, order, here * rows, rows, at, col_blocks)
        panel_keep[q] = keep.astype(jnp.bfloat16)
    for pattern, keep in ((square_pattern, square_keep), (cube_pattern, cube_keep)):
        keep[...] = rows_mask(pattern, order, here * rows, rows, first_col, col_blocks)


def panel_kernel(reps, panel_keep, *refs):
    panel, (left, own) = refs[:reps], refs[reps:]
    rep = lax.axis_index("rep")
    cols = panel[0].shape[1]
    for q in range(reps):
        at = pl.multiple_of(lax.rem(rep - q + reps, reps) * cols, BLOCK)
        part = panel[q][...] * panel_keep[q]
        left[:, pl.ds(at, cols)] = part
        if q == 0:
            own[...] = part


def masked_tile(source, at, table, stored_row):
    return source[at:at + TILE, :] * table[stored_row // BLOCK]


def stack_kernel(*refs):
    out, done = refs[-1], 0
    for ref in refs[:-1]:
        out[done:done + ref.shape[0], :] = ref[...]
        done += ref.shape[0]


def early_kernel(groups, late, dims, left, table, *refs):
    held, (band, partial) = refs[:len(groups)], refs[len(groups):]
    rows, cols = partial.shape
    for pieces, ref in zip(groups, held):
        done = 0
        for piece in pieces:
            row = source_row(piece, dims, rows)
            for at in range(0, piece[4] - piece[3], TILE):
                tile = masked_tile(ref, done, table, row + at)
                band[pl.ds(pl.multiple_of(row + at, TILE), TILE), :] = tile
                done += TILE
    for piece in late:
        count = piece[4] - piece[3]
        band[pl.ds(source_row(piece, dims, rows), count), :] = jnp.zeros((count, cols), band.dtype)
    partial[...] = jnp.dot(left[...], band[...], preferred_element_type=jnp.float32)


def late_kernel(late, dims, table, square_keep, left, old_band, partial, *refs):
    pieces, (band, tripled, square_half, window) = refs[:len(late)], refs[len(late):]
    rows, cols = partial.shape
    pair = dims[2]
    total = partial[...]
    for first in range(0, len(late), pair):
        base = late[first]
        start = source_row(base, dims, rows)
        start = start - lax.rem(start, rows * pair)
        low = jnp.minimum(start // BLOCK * BLOCK, band.shape[0] - window.shape[0])
        low = pl.multiple_of(low, BLOCK)
        window[...] = jnp.zeros(window.shape, window.dtype)
        for piece, ref in zip(late[first:first + pair], pieces[first:first + pair]):
            row = source_row(piece, dims, rows)
            for at in range(0, ref.shape[0], TILE):
                tile = masked_tile(ref, at, table, row + at)
                window[pl.ds(pl.multiple_of(row + at - low, TILE), TILE), :] = tile
                band[pl.ds(pl.multiple_of(row + at, TILE), TILE), :] = tile
        total += jnp.dot(
            left[:, pl.ds(low, window.shape[0])], window[...], preferred_element_type=jnp.float32
        )
    total *= square_keep[...]
    tripled[...] = 3.0 * total
    square_half[...] = total.astype(jnp.bfloat16)


def cube_kernel(shift, keep, half, band, before, out):
    rep, reps = lax.axis_index("rep"), lax.axis_size("rep")
    cols = before.shape[1]
    at = lax.rem(rep - shift + reps, reps)
    right = band[pl.ds(pl.multiple_of(at * cols, BLOCK), cols), :]
    part = jnp.dot(half[...], right, preferred_element_type=jnp.float32)
    out[...] = before[...] - 2.0 * (part * keep[...])


def shifted(own, reps):
    return [
        lax.ppermute(own, "rep", [(s, (s + q) % reps) for s in range(reps)])
        for q in range(1, reps)
    ]


def on_device(grid, reps, density, density_pattern, square_pattern, cube_pattern, block_order):
    rows, cols = density.shape
    order = grid * rows
    dims = factors(grid)
    outer, inner, pair = dims
    band_bytes = order * cols * 2
    room = min(3 * band_bytes + (4 << 20), 56 << 20)
    bf16, f32 = jnp.bfloat16, jnp.float32

    def call(kernel, name, flops, moved, out, operands, spec=None, **more):
        return pl.pallas_call(
            kernel,
            out_shape=[jax.ShapeDtypeStruct(shape, dtype) for shape, dtype in out],
            in_specs=spec or [IN_VMEM] * len(operands),
            out_specs=[IN_VMEM] * len(out),
            compiler_params=pltpu.CompilerParams(vmem_limit_bytes=room),
            cost_estimate=pl.CostEstimate(flops=flops, bytes_accessed=moved, transcendentals=0),
            name=name,
            **more,
        )(*operands)

    steps, hops = list(range(1, outer)), list(range(1, inner))
    last = steps[-1] if steps and hops else None
    before = [step for step in steps if step != last][-1:]

    held = {(0, 0): density}
    for step in steps:
        held[step, 0] = send(after(density), dims, 0, step)
    for hop in hops:
        held[0, hop] = send(after(density), dims, 1, hop)
    packed = jnp.concatenate(
        [density_pattern, square_pattern, cube_pattern, after(block_order)[None]], axis=0
    )
    table, panel_keep, square_keep, cube_keep = call(
        functools.partial(prepare_kernel, reps), "prepare", PLACE, 2 * band_bytes,
        [((order // BLOCK, TILE, cols), bf16), ((reps, rows, cols), bf16),
         ((rows, cols), f32), ((rows, cols), f32)],
        [packed], spec=[IN_SMEM],
    )
    for step in steps:
        for hop in hops:
            ready = [table] if step == last else []
            held[step, hop] = send(after(held[step, 0], *ready), dims, 1, hop)
    panel = shifted(after(density), reps)
    left, own = call(
        functools.partial(panel_kernel, reps), "panel", 4 * PLACE, 2 * band_bytes,
        [((rows, reps * cols), bf16), ((rows, cols), bf16)],
        [panel_keep, after(density), *panel],
    )

    keys = [(0, 0)] + [(step, 0) for step in steps if step not in before]
    keys += [(0, hop) for hop in hops] + [(step, 0) for step in before]
    keys += [(step, hop) for step in steps for hop in hops]
    lone = [(0, 0)] + [key for key in keys if key[0] == last or key[0] in before and key[1]]
    stack = [key for key in keys if key not in lone]
    whole = lambda key, core: (*key, core, 0, rows)
    early, late = [], []
    for key in keys:
        group = late if key[0] == last and key[1] else early
        group.append(([whole(key, 0)], held[key] if key != (0, 0) else own))
        if pair > 1 and key in lone:
            value = after(held[key], *([] if group is late else [left]))
            group.append(([whole(key, 1)], send(value, dims, 2, 1)))
    if pair > 1 and stack:
        ready = panel + ([held[last, 0]] if hops else [])
        (stacked,) = call(
            stack_kernel, "stack", 0, 0, [((len(stack) * rows, cols), bf16)],
            [after(held[key], *ready) for key in stack],
        )
        early.append(([whole(key, 1) for key in stack], send(after(stacked), dims, 2, 1)))
    late_pieces, late_values = [piece[0] for piece, _ in late], [value for _, value in late]

    band, partial = call(
        functools.partial(early_kernel, [pieces for pieces, _ in early], late_pieces, dims),
        "square_early", 2 * rows * order * cols, 2 * band_bytes,
        [((order, cols), bf16), ((rows, cols), f32)],
        [left, table, *[value for _, value in early]],
    )
    span = BLOCK - math.gcd(pair * rows, BLOCK) + pair * rows
    span = min((span + BLOCK - 1) // BLOCK * BLOCK, order)
    band, tripled, square_half = call(
        functools.partial(late_kernel, late_pieces, dims), "square_late",
        2 * rows * span * cols, 4 * rows * cols,
        [((order, cols), bf16), ((rows, cols), f32), ((rows, cols), bf16)],
        [table, square_keep, left, band, partial, *late_values],
        input_output_aliases={3: 0},
        scratch_shapes=[pltpu.VMEM((span, cols), bf16)],
    )
    out = tripled
    for shift, half in enumerate([square_half] + shifted(square_half, reps)):
        (out,) = call(
            functools.partial(cube_kernel, shift), "cube_part",
            2 * rows * cols * cols, band_bytes // reps, [((rows, cols), f32)],
            [cube_keep, half, band, out],
        )
    return out


def solution(mesh):
    placed = (P("grid", "rep"), P(), P(), P(), P())
    return jax.shard_map(
        functools.partial(on_device, mesh.shape["grid"], mesh.shape["rep"]),
        mesh=mesh, in_specs=placed, out_specs=P("grid", "rep"), check_vma=False,
    )
```

```python
import functools
import math

import jax
import jax.numpy as jnp
from jax import lax
from jax.experimental import pallas as pl
from jax.experimental.pallas import tpu as pltpu
from jax.sharding import PartitionSpec as P

BLOCK = 128
TILE = 16
PLACE = 10**9
IN_SMEM = pl.BlockSpec(memory_space=pltpu.SMEM)
IN_VMEM = pl.BlockSpec(memory_space=pltpu.VMEM)


def factors(size):
    pair = 2 if size % 2 == 0 else 1
    rest = size // pair
    outer = 4 if rest % 4 == 0 else 1
    return outer, rest // outer, pair


def send(value, dims, axis, step):
    outer, inner, pair = dims
    pairs = []
    for source in range(outer * inner * pair):
        place = [source // (inner * pair), source // pair % inner, source % pair]
        place[axis] = (place[axis] + step) % dims[axis]
        pairs.append((source, (place[0] * inner + place[1]) * pair + place[2]))
    return lax.ppermute(value, "grid", pairs)


def source_row(piece, dims, rows):
    outer, inner, pair = dims
    here = lax.axis_index("grid")
    at = (here // (inner * pair), here // pair % inner, here % pair)
    z, x, c = [lax.rem(a - k + d, d) for a, k, d in zip(at, piece[:3], dims)]
    return pl.multiple_of(((z * inner + x) * pair + c) * rows + piece[3], TILE)


def after(value, *others):
    return lax.optimization_barrier((value,) + others)[0]


def pick(pattern, order, row_block, col_block):
    return pattern[order[row_block], order[col_block]].astype(jnp.float32)


def rows_mask(pattern, order, first_row, rows, first_col_block, col_blocks):
    top = first_row // BLOCK
    low = (first_row + rows - 1) // BLOCK
    split = (top + 1) * BLOCK - first_row
    upper = lax.broadcasted_iota(jnp.int32, (rows, BLOCK), 0) < split
    tiles = []
    for j in range(col_blocks):
        a = pick(pattern, order, top, first_col_block + j)
        b = pick(pattern, order, low, first_col_block + j)
        tiles.append(jnp.where(upper, a, b))
    return jnp.concatenate(tiles, axis=1)


def parts_of(packed):
    count = packed.shape[1]
    patterns = [packed.at[pl.ds(at * count, count), :] for at in range(3)]
    return (*patterns, packed.at[3 * count])


def prepare_kernel(reps, packed, table, panel_keep, square_keep, cube_keep):
    density_pattern, square_pattern, cube_pattern, order = parts_of(packed)
    here, rep = lax.axis_index("grid"), lax.axis_index("rep")
    row_blocks, _, cols = table.shape
    rows = square_keep.shape[0]
    col_blocks = cols // BLOCK
    first_col = rep * col_blocks

    def fill(i, _):
        for j in range(col_blocks):
            keep = pick(density_pattern, order, i, first_col + j)
            tile = jnp.full((TILE, BLOCK), keep, jnp.float32).astype(jnp.bfloat16)
            table[i, :, j * BLOCK:(j + 1) * BLOCK] = tile
        return 0

    lax.fori_loop(0, row_blocks, fill, 0, unroll=row_blocks <= 16)
    for q in range(reps):
        at = lax.rem(rep - q + reps, reps) * col_blocks
        keep = rows_mask(density_pattern, order, here * rows, rows, at, col_blocks)
        panel_keep[q] = keep.astype(jnp.bfloat16)
    for pattern, keep in ((square_pattern, square_keep), (cube_pattern, cube_keep)):
        keep[...] = rows_mask(pattern, order, here * rows, rows, first_col, col_blocks)


def panel_kernel(reps, panel_keep, *refs):
    panel, (left, own) = refs[:reps], refs[reps:]
    rep = lax.axis_index("rep")
    cols = panel[0].shape[1]
    for q in range(reps):
        at = pl.multiple_of(lax.rem(rep - q + reps, reps) * cols, BLOCK)
        part = panel[q][...] * panel_keep[q]
        left[:, pl.ds(at, cols)] = part
        if q == 0:
            own[...] = part


def masked_tile(source, at, table, stored_row):
    return source[at:at + TILE, :] * table[stored_row // BLOCK]


def stack_kernel(*refs):
    out, done = refs[-1], 0
    for ref in refs[:-1]:
        out[done:done + ref.shape[0], :] = ref[...]
        done += ref.shape[0]


def early_kernel(groups, late, dims, left, table, *refs):
    held, (band, partial) = refs[:len(groups)], refs[len(groups):]
    rows, cols = partial.shape
    for pieces, ref in zip(groups, held):
        done = 0
        for piece in pieces:
            row = source_row(piece, dims, rows)
            for at in range(0, piece[4] - piece[3], TILE):
                tile = masked_tile(ref, done, table, row + at)
                band[pl.ds(pl.multiple_of(row + at, TILE), TILE), :] = tile
                done += TILE
    for piece in late:
        count = piece[4] - piece[3]
        band[pl.ds(source_row(piece, dims, rows), count), :] = jnp.zeros((count, cols), band.dtype)
    partial[...] = jnp.dot(left[...], band[...], preferred_element_type=jnp.float32)


def late_kernel(late, dims, table, square_keep, left, old_band, partial, *refs):
    pieces, (band, tripled, square_half, window) = refs[:len(late)], refs[len(late):]
    rows, cols = partial.shape
    pair = dims[2]
    total = partial[...]
    for first in range(0, len(late), pair):
        base = late[first]
        start = source_row(base, dims, rows)
        start = start - lax.rem(start, rows * pair)
        low = jnp.minimum(start // BLOCK * BLOCK, band.shape[0] - window.shape[0])
        low = pl.multiple_of(low, BLOCK)
        window[...] = jnp.zeros(window.shape, window.dtype)
        for piece, ref in zip(late[first:first + pair], pieces[first:first + pair]):
            row = source_row(piece, dims, rows)
            for at in range(0, ref.shape[0], TILE):
                tile = masked_tile(ref, at, table, row + at)
                window[pl.ds(pl.multiple_of(row + at - low, TILE), TILE), :] = tile
                band[pl.ds(pl.multiple_of(row + at, TILE), TILE), :] = tile
        total += jnp.dot(
            left[:, pl.ds(low, window.shape[0])], window[...], preferred_element_type=jnp.float32
        )
    total *= square_keep[...]
    tripled[...] = 3.0 * total
    for copy in range(square_half.shape[0]):
        square_half[copy] = total.astype(jnp.bfloat16)


def cube_kernel(reps, keep, halves, band, before, out):
    cols = before.shape[1]
    part = jnp.zeros(before.shape, jnp.float32)
    for at in range(reps):
        part += jnp.dot(
            halves[at], band[at * cols:(at + 1) * cols, :], preferred_element_type=jnp.float32
        )
    out[...] = before[...] - 2.0 * (part * keep[...])


def shifted(own, reps):
    return [
        lax.ppermute(own, "rep", [(s, (s + q) % reps) for s in range(reps)])
        for q in range(1, reps)
    ]


def on_device(grid, reps, density, density_pattern, square_pattern, cube_pattern, block_order):
    rows, cols = density.shape
    order = grid * rows
    dims = factors(grid)
    outer, inner, pair = dims
    band_bytes = order * cols * 2
    room = min(3 * band_bytes + (4 << 20), 56 << 20)
    bf16, f32 = jnp.bfloat16, jnp.float32

    def call(kernel, name, flops, moved, out, operands, spec=None, **more):
        return pl.pallas_call(
            kernel,
            out_shape=[jax.ShapeDtypeStruct(shape, dtype) for shape, dtype in out],
            in_specs=spec or [IN_VMEM] * len(operands),
            out_specs=[IN_VMEM] * len(out),
            compiler_params=pltpu.CompilerParams(vmem_limit_bytes=room),
            cost_estimate=pl.CostEstimate(flops=flops, bytes_accessed=moved, transcendentals=0),
            name=name,
            **more,
        )(*operands)

    steps, hops = list(range(1, outer)), list(range(1, inner))
    last = outer // 2 if steps and hops else None
    before = [step for step in steps if step != last][-1:]

    held = {(0, 0): density}
    for step in steps:
        held[step, 0] = send(after(density), dims, 0, step)
    for hop in hops:
        held[0, hop] = send(after(density), dims, 1, hop)
    packed = jnp.concatenate(
        [density_pattern, square_pattern, cube_pattern, after(block_order)[None]], axis=0
    )
    table, panel_keep, square_keep, cube_keep = call(
        functools.partial(prepare_kernel, reps), "prepare", PLACE, 2 * band_bytes,
        [((order // BLOCK, TILE, cols), bf16), ((reps, rows, cols), bf16),
         ((rows, cols), f32), ((rows, cols), f32)],
        [packed], spec=[IN_SMEM],
    )
    for step in steps:
        for hop in hops:
            ready = [table] if step == last else []
            held[step, hop] = send(after(held[step, 0], *ready), dims, 1, hop)
    panel = shifted(after(density), reps)
    left, own = call(
        functools.partial(panel_kernel, reps), "panel", 4 * PLACE, 2 * band_bytes,
        [((rows, reps * cols), bf16), ((rows, cols), bf16)],
        [panel_keep, after(density), *panel],
    )

    keys = [(0, 0)] + [(step, 0) for step in steps if step not in before]
    keys += [(0, hop) for hop in hops] + [(step, 0) for step in before]
    keys += [(step, hop) for step in steps for hop in hops]
    lone = [(0, 0)] + [key for key in keys if key[0] == last or key[0] in before and key[1]]
    stack = [key for key in keys if key not in lone]
    whole = lambda key, core: (*key, core, 0, rows)
    early, late = [], []
    for key in keys:
        group = late if key[0] == last and key[1] else early
        group.append(([whole(key, 0)], held[key] if key != (0, 0) else own))
        if pair > 1 and key in lone:
            value = after(held[key], *([] if group is late else [left]))
            group.append(([whole(key, 1)], send(value, dims, 2, 1)))
    if pair > 1 and stack:
        ready = panel + ([held[last, 0]] if hops else [])
        (stacked,) = call(
            stack_kernel, "stack", 0, 0, [((len(stack) * rows, cols), bf16)],
            [after(held[key], *ready) for key in stack],
        )
        early.append(([whole(key, 1) for key in stack], send(after(stacked), dims, 2, 1)))
    late_pieces, late_values = [piece[0] for piece, _ in late], [value for _, value in late]

    band, partial = call(
        functools.partial(early_kernel, [pieces for pieces, _ in early], late_pieces, dims),
        "square_early", 2 * rows * order * cols, 2 * band_bytes,
        [((order, cols), bf16), ((rows, cols), f32)],
        [left, table, *[value for _, value in early]],
    )
    span = BLOCK - math.gcd(pair * rows, BLOCK) + pair * rows
    span = min((span + BLOCK - 1) // BLOCK * BLOCK, order)
    band, tripled, square_half = call(
        functools.partial(late_kernel, late_pieces, dims), "square_late",
        2 * rows * span * cols, 4 * rows * cols,
        [((order, cols), bf16), ((rows, cols), f32), ((reps, rows, cols), bf16)],
        [table, square_keep, left, band, partial, *late_values],
        input_output_aliases={3: 0},
        scratch_shapes=[pltpu.VMEM((span, cols), bf16)],
    )
    halves = lax.all_to_all(square_half, "rep", 0, 0)
    (out,) = call(
        functools.partial(cube_kernel, reps), "cube",
        2 * rows * order * cols, band_bytes, [((rows, cols), f32)],
        [cube_keep, halves, band, tripled],
    )
    return out


def solution(mesh):
    placed = (P("grid", "rep"), P(), P(), P(), P())
    return jax.shard_map(
        functools.partial(on_device, mesh.shape["grid"], mesh.shape["rep"]),
        mesh=mesh, in_specs=placed, out_specs=P("grid", "rep"), check_vma=False,
    )
```

```python
import functools
import math

import jax
import jax.numpy as jnp
from jax import lax
from jax.experimental import pallas as pl
from jax.experimental.pallas import tpu as pltpu
from jax.sharding import PartitionSpec as P

BLOCK = 128
TILE = 16
SOURCES = ((0, 1, 2, 3), (1, 0, 3, 2), (2, 3, 1, 0), (3, 2, 0, 1))
PLACE = 10**9
IN_SMEM = pl.BlockSpec(memory_space=pltpu.SMEM)
IN_VMEM = pl.BlockSpec(memory_space=pltpu.VMEM)


def factors(size):
    pair = 2 if size % 2 == 0 else 1
    rest = size // pair
    outer = 4 if rest % 4 == 0 else 1
    return outer, rest // outer, pair


def send(value, dims, axis, step):
    outer, inner, pair = dims
    pairs = []
    for target in range(outer * inner * pair):
        place = [target // (inner * pair), target // pair % inner, target % pair]
        if axis == 0:
            place[0] = SOURCES[step][place[0]]
        else:
            place[axis] = (place[axis] - step) % dims[axis]
        pairs.append(((place[0] * inner + place[1]) * pair + place[2], target))
    return lax.ppermute(value, "grid", sorted(pairs))


def source_row(piece, dims, rows):
    outer, inner, pair = dims
    here = lax.axis_index("grid")
    at = (here // (inner * pair), here // pair % inner, here % pair)
    z = at[0]
    if piece[0]:
        z = jnp.int32(SOURCES[piece[0]][0])
        for plane in range(1, outer):
            z = jnp.where(at[0] == plane, SOURCES[piece[0]][plane], z)
    x, c = [lax.rem(a - k + d, d) for a, k, d in zip(at[1:], piece[1:3], dims[1:])]
    return pl.multiple_of(((z * inner + x) * pair + c) * rows + piece[3], TILE)


def after(value, *others):
    return lax.optimization_barrier((value,) + others)[0]


def pick(pattern, order, row_block, col_block):
    return pattern[order[row_block], order[col_block]].astype(jnp.float32)


def rows_mask(pattern, order, first_row, rows, first_col_block, col_blocks):
    top = first_row // BLOCK
    low = (first_row + rows - 1) // BLOCK
    split = (top + 1) * BLOCK - first_row
    upper = lax.broadcasted_iota(jnp.int32, (rows, BLOCK), 0) < split
    tiles = []
    for j in range(col_blocks):
        a = pick(pattern, order, top, first_col_block + j)
        b = pick(pattern, order, low, first_col_block + j)
        tiles.append(jnp.where(upper, a, b))
    return jnp.concatenate(tiles, axis=1)


def parts_of(packed):
    count = packed.shape[1]
    patterns = [packed.at[pl.ds(at * count, count), :] for at in range(3)]
    return (*patterns, packed.at[3 * count])


def prepare_kernel(reps, packed, table, panel_keep, square_keep, cube_keep):
    density_pattern, square_pattern, cube_pattern, order = parts_of(packed)
    here, rep = lax.axis_index("grid"), lax.axis_index("rep")
    row_blocks, _, cols = table.shape
    rows = square_keep.shape[0]
    col_blocks = cols // BLOCK
    first_col = rep * col_blocks

    def fill(i, _):
        for j in range(col_blocks):
            keep = pick(density_pattern, order, i, first_col + j)
            tile = jnp.full((TILE, BLOCK), keep, jnp.float32).astype(jnp.bfloat16)
            table[i, :, j * BLOCK:(j + 1) * BLOCK] = tile
        return 0

    lax.fori_loop(0, row_blocks, fill, 0, unroll=row_blocks <= 16)
    for q in range(reps):
        at = lax.rem(rep - q + reps, reps) * col_blocks
        keep = rows_mask(density_pattern, order, here * rows, rows, at, col_blocks)
        panel_keep[q] = keep.astype(jnp.bfloat16)
    for pattern, keep in ((square_pattern, square_keep), (cube_pattern, cube_keep)):
        keep[...] = rows_mask(pattern, order, here * rows, rows, first_col, col_blocks)


def panel_kernel(reps, panel_keep, *refs):
    panel, (left, own) = refs[:reps], refs[reps:]
    rep = lax.axis_index("rep")
    cols = panel[0].shape[1]
    for q in range(reps):
        at = pl.multiple_of(lax.rem(rep - q + reps, reps) * cols, BLOCK)
        part = panel[q][...] * panel_keep[q]
        left[:, pl.ds(at, cols)] = part
        if q == 0:
            own[...] = part


def masked_tile(source, at, table, stored_row):
    return source[at:at + TILE, :] * table[stored_row // BLOCK]


def stack_kernel(*refs):
    out, done = refs[-1], 0
    for ref in refs[:-1]:
        out[done:done + ref.shape[0], :] = ref[...]
        done += ref.shape[0]


def early_kernel(groups, late, dims, left, table, *refs):
    held, (band, partial) = refs[:len(groups)], refs[len(groups):]
    rows, cols = partial.shape
    for pieces, ref in zip(groups, held):
        done = 0
        for piece in pieces:
            row = source_row(piece, dims, rows)
            for at in range(0, piece[4] - piece[3], TILE):
                tile = masked_tile(ref, done, table, row + at)
                band[pl.ds(pl.multiple_of(row + at, TILE), TILE), :] = tile
                done += TILE
    for piece in late:
        count = piece[4] - piece[3]
        band[pl.ds(source_row(piece, dims, rows), count), :] = jnp.zeros((count, cols), band.dtype)
    partial[...] = jnp.dot(left[...], band[...], preferred_element_type=jnp.float32)


def late_kernel(late, dims, table, square_keep, left, old_band, partial, *refs):
    pieces, (band, tripled, square_half, window) = refs[:len(late)], refs[len(late):]
    rows, cols = partial.shape
    pair = dims[2]
    total = partial[...]
    for first in range(0, len(late), pair):
        base = late[first]
        start = source_row(base, dims, rows)
        start = start - lax.rem(start, rows * pair)
        low = jnp.minimum(start // BLOCK * BLOCK, band.shape[0] - window.shape[0])
        low = pl.multiple_of(low, BLOCK)
        window[...] = jnp.zeros(window.shape, window.dtype)
        for piece, ref in zip(late[first:first + pair], pieces[first:first + pair]):
            row = source_row(piece, dims, rows)
            for at in range(0, ref.shape[0], TILE):
                tile = masked_tile(ref, at, table, row + at)
                window[pl.ds(pl.multiple_of(row + at - low, TILE), TILE), :] = tile
                band[pl.ds(pl.multiple_of(row + at, TILE), TILE), :] = tile
        total += jnp.dot(
            left[:, pl.ds(low, window.shape[0])], window[...], preferred_element_type=jnp.float32
        )
    total *= square_keep[...]
    tripled[...] = 3.0 * total
    square_half[...] = total.astype(jnp.bfloat16)


def cube_kernel(shift, keep, half, band, before, out):
    rep, reps = lax.axis_index("rep"), lax.axis_size("rep")
    cols = before.shape[1]
    at = lax.rem(rep - shift + reps, reps)
    right = band[pl.ds(pl.multiple_of(at * cols, BLOCK), cols), :]
    part = jnp.dot(half[...], right, preferred_element_type=jnp.float32)
    out[...] = before[...] - 2.0 * (part * keep[...])


def shifted(own, reps):
    return [
        lax.ppermute(own, "rep", [(s, (s + q) % reps) for s in range(reps)])
        for q in range(1, reps)
    ]


def on_device(grid, reps, density, density_pattern, square_pattern, cube_pattern, block_order):
    rows, cols = density.shape
    order = grid * rows
    dims = factors(grid)
    outer, inner, pair = dims
    band_bytes = order * cols * 2
    room = min(3 * band_bytes + (4 << 20), 56 << 20)
    bf16, f32 = jnp.bfloat16, jnp.float32

    def call(kernel, name, flops, moved, out, operands, spec=None, **more):
        return pl.pallas_call(
            kernel,
            out_shape=[jax.ShapeDtypeStruct(shape, dtype) for shape, dtype in out],
            in_specs=spec or [IN_VMEM] * len(operands),
            out_specs=[IN_VMEM] * len(out),
            compiler_params=pltpu.CompilerParams(vmem_limit_bytes=room),
            cost_estimate=pl.CostEstimate(flops=flops, bytes_accessed=moved, transcendentals=0),
            name=name,
            **more,
        )(*operands)

    steps, hops = list(range(1, outer)), list(range(1, inner))
    last = outer // 2 if steps and hops else None
    before = [step for step in steps if step != last][-1:]

    held = {(0, 0): density}
    for step in steps:
        held[step, 0] = send(after(density), dims, 0, step)
    for hop in hops:
        held[0, hop] = send(after(density), dims, 1, hop)
    packed = jnp.concatenate(
        [density_pattern, square_pattern, cube_pattern, after(block_order)[None]], axis=0
    )
    table, panel_keep, square_keep, cube_keep = call(
        functools.partial(prepare_kernel, reps), "prepare", PLACE, 2 * band_bytes,
        [((order // BLOCK, TILE, cols), bf16), ((reps, rows, cols), bf16),
         ((rows, cols), f32), ((rows, cols), f32)],
        [packed], spec=[IN_SMEM],
    )
    for step in steps:
        for hop in hops:
            ready = [table] if step == last else []
            held[step, hop] = send(after(held[step, 0], *ready), dims, 1, hop)
    panel = shifted(after(density), reps)
    left, own = call(
        functools.partial(panel_kernel, reps), "panel", 4 * PLACE, 2 * band_bytes,
        [((rows, reps * cols), bf16), ((rows, cols), bf16)],
        [panel_keep, after(density), *panel],
    )

    keys = [(0, 0)] + [(step, 0) for step in steps if step not in before]
    keys += [(0, hop) for hop in hops] + [(step, 0) for step in before]
    keys += [(step, hop) for step in steps for hop in hops]
    lone = [(0, 0)] + [key for key in keys if key[0] == last or key[0] in before and key[1]]
    stack = [key for key in keys if key not in lone]
    whole = lambda key, core: (*key, core, 0, rows)
    early, late = [], []
    for key in keys:
        group = late if key[0] == last and key[1] else early
        group.append(([whole(key, 0)], held[key] if key != (0, 0) else own))
        if pair > 1 and key in lone:
            value = after(held[key], *([] if group is late else [left]))
            group.append(([whole(key, 1)], send(value, dims, 2, 1)))
    if pair > 1 and stack:
        ready = panel + ([held[last, 0]] if hops else [])
        (stacked,) = call(
            stack_kernel, "stack", 0, 0, [((len(stack) * rows, cols), bf16)],
            [after(held[key], *ready) for key in stack],
        )
        early.append(([whole(key, 1) for key in stack], send(after(stacked), dims, 2, 1)))
    late_pieces, late_values = [piece[0] for piece, _ in late], [value for _, value in late]

    band, partial = call(
        functools.partial(early_kernel, [pieces for pieces, _ in early], late_pieces, dims),
        "square_early", 2 * rows * order * cols, 2 * band_bytes,
        [((order, cols), bf16), ((rows, cols), f32)],
        [left, table, *[value for _, value in early]],
    )
    span = BLOCK - math.gcd(pair * rows, BLOCK) + pair * rows
    span = min((span + BLOCK - 1) // BLOCK * BLOCK, order)
    band, tripled, square_half = call(
        functools.partial(late_kernel, late_pieces, dims), "square_late",
        2 * rows * span * cols, 4 * rows * cols,
        [((order, cols), bf16), ((rows, cols), f32), ((rows, cols), bf16)],
        [table, square_keep, left, band, partial, *late_values],
        input_output_aliases={3: 0},
        scratch_shapes=[pltpu.VMEM((span, cols), bf16)],
    )
    out = tripled
    for shift, half in enumerate([square_half] + shifted(square_half, reps)):
        (out,) = call(
            functools.partial(cube_kernel, shift), "cube_part",
            2 * rows * cols * cols, band_bytes // reps, [((rows, cols), f32)],
            [cube_keep, half, band, out],
        )
    return out


def solution(mesh):
    placed = (P("grid", "rep"), P(), P(), P(), P())
    return jax.shard_map(
        functools.partial(on_device, mesh.shape["grid"], mesh.shape["rep"]),
        mesh=mesh, in_specs=placed, out_specs=P("grid", "rep"), check_vma=False,
    )
```

```python
import functools
import math

import jax
import jax.numpy as jnp
from jax import lax
from jax.experimental import pallas as pl
from jax.experimental.pallas import tpu as pltpu
from jax.sharding import PartitionSpec as P

BLOCK = 128
TILE = 16
SOURCES = ((0, 1, 2, 3), (1, 0, 3, 2), (2, 3, 1, 0), (3, 2, 0, 1))
PLACE = 10**9
IN_SMEM = pl.BlockSpec(memory_space=pltpu.SMEM)
IN_VMEM = pl.BlockSpec(memory_space=pltpu.VMEM)


def factors(size):
    pair = 2 if size % 2 == 0 else 1
    rest = size // pair
    outer = 4 if rest % 4 == 0 else 1
    return outer, rest // outer, pair


def send(value, dims, axis, step):
    outer, inner, pair = dims
    pairs = []
    for target in range(outer * inner * pair):
        place = [target // (inner * pair), target // pair % inner, target % pair]
        if axis == 0:
            place[0] = SOURCES[step][place[0]]
        else:
            place[axis] = (place[axis] - step) % dims[axis]
        pairs.append(((place[0] * inner + place[1]) * pair + place[2], target))
    return lax.ppermute(value, "grid", sorted(pairs))


def source_row(piece, dims, rows):
    outer, inner, pair = dims
    here = lax.axis_index("grid")
    at = (here // (inner * pair), here // pair % inner, here % pair)
    z = at[0]
    if piece[0]:
        z = jnp.int32(SOURCES[piece[0]][0])
        for plane in range(1, outer):
            z = jnp.where(at[0] == plane, SOURCES[piece[0]][plane], z)
    x, c = [lax.rem(a - k + d, d) for a, k, d in zip(at[1:], piece[1:3], dims[1:])]
    return pl.multiple_of(((z * inner + x) * pair + c) * rows + piece[3], TILE)


def after(value, *others):
    return lax.optimization_barrier((value,) + others)[0]


def pick(pattern, order, row_block, col_block):
    return pattern[order[row_block], order[col_block]].astype(jnp.float32)


def rows_mask(pattern, order, first_row, rows, first_col_block, col_blocks):
    top = first_row // BLOCK
    low = (first_row + rows - 1) // BLOCK
    split = (top + 1) * BLOCK - first_row
    upper = lax.broadcasted_iota(jnp.int32, (rows, BLOCK), 0) < split
    tiles = []
    for j in range(col_blocks):
        a = pick(pattern, order, top, first_col_block + j)
        b = pick(pattern, order, low, first_col_block + j)
        tiles.append(jnp.where(upper, a, b))
    return jnp.concatenate(tiles, axis=1)


def parts_of(packed):
    count = packed.shape[1]
    patterns = [packed.at[pl.ds(at * count, count), :] for at in range(3)]
    return (*patterns, packed.at[3 * count])


def prepare_kernel(reps, packed, table, panel_keep, square_keep, cube_keep):
    density_pattern, square_pattern, cube_pattern, order = parts_of(packed)
    here, rep = lax.axis_index("grid"), lax.axis_index("rep")
    row_blocks, _, cols = table.shape
    rows = square_keep.shape[0]
    col_blocks = cols // BLOCK
    first_col = rep * col_blocks

    def fill(i, _):
        for j in range(col_blocks):
            keep = pick(density_pattern, order, i, first_col + j)
            tile = jnp.full((TILE, BLOCK), keep, jnp.float32).astype(jnp.bfloat16)
            table[i, :, j * BLOCK:(j + 1) * BLOCK] = tile
        return 0

    lax.fori_loop(0, row_blocks, fill, 0, unroll=row_blocks <= 16)
    for q in range(reps):
        at = lax.rem(rep - q + reps, reps) * col_blocks
        keep = rows_mask(density_pattern, order, here * rows, rows, at, col_blocks)
        panel_keep[q] = keep.astype(jnp.bfloat16)
    for pattern, keep in ((square_pattern, square_keep), (cube_pattern, cube_keep)):
        keep[...] = rows_mask(pattern, order, here * rows, rows, first_col, col_blocks)


def panel_kernel(reps, panel_keep, *refs):
    panel, (left, own) = refs[:reps], refs[reps:]
    rep = lax.axis_index("rep")
    cols = panel[0].shape[1]
    for q in range(reps):
        at = pl.multiple_of(lax.rem(rep - q + reps, reps) * cols, BLOCK)
        part = panel[q][...] * panel_keep[q]
        left[:, pl.ds(at, cols)] = part
        if q == 0:
            own[...] = part


def masked_tile(source, at, table, stored_row):
    return source[at:at + TILE, :] * table[stored_row // BLOCK]


def stack_kernel(*refs):
    out, done = refs[-1], 0
    for ref in refs[:-1]:
        out[done:done + ref.shape[0], :] = ref[...]
        done += ref.shape[0]


def early_kernel(groups, late, dims, left, table, *refs):
    held, (band, partial) = refs[:len(groups)], refs[len(groups):]
    rows, cols = partial.shape
    for pieces, ref in zip(groups, held):
        done = 0
        for piece in pieces:
            row = source_row(piece, dims, rows)
            for at in range(0, piece[4] - piece[3], TILE):
                tile = masked_tile(ref, done, table, row + at)
                band[pl.ds(pl.multiple_of(row + at, TILE), TILE), :] = tile
                done += TILE
    for piece in late:
        count = piece[4] - piece[3]
        band[pl.ds(source_row(piece, dims, rows), count), :] = jnp.zeros((count, cols), band.dtype)
    partial[...] = jnp.dot(left[...], band[...], preferred_element_type=jnp.float32)


def late_kernel(late, dims, table, square_keep, left, old_band, partial, *refs):
    pieces, (band, tripled, square_half, window) = refs[:len(late)], refs[len(late):]
    rows, cols = partial.shape
    pair = dims[2]
    total = partial[...]
    for first in range(0, len(late), pair):
        base = late[first]
        start = source_row(base, dims, rows)
        start = start - lax.rem(start, rows * pair)
        low = jnp.minimum(start // BLOCK * BLOCK, band.shape[0] - window.shape[0])
        low = pl.multiple_of(low, BLOCK)
        window[...] = jnp.zeros(window.shape, window.dtype)
        for piece, ref in zip(late[first:first + pair], pieces[first:first + pair]):
            row = source_row(piece, dims, rows)
            for at in range(0, ref.shape[0], TILE):
                tile = masked_tile(ref, at, table, row + at)
                window[pl.ds(pl.multiple_of(row + at - low, TILE), TILE), :] = tile
                band[pl.ds(pl.multiple_of(row + at, TILE), TILE), :] = tile
        total += jnp.dot(
            left[:, pl.ds(low, window.shape[0])], window[...], preferred_element_type=jnp.float32
        )
    total *= square_keep[...]
    tripled[...] = 3.0 * total
    square_half[...] = total.astype(jnp.bfloat16)


def cube_kernel(shift, keep, half, band, before, out):
    rep, reps = lax.axis_index("rep"), lax.axis_size("rep")
    cols = before.shape[1]
    at = lax.rem(rep - shift + reps, reps)
    right = band[pl.ds(pl.multiple_of(at * cols, BLOCK), cols), :]
    part = jnp.dot(half[...], right, preferred_element_type=jnp.float32)
    out[...] = before[...] - 2.0 * (part * keep[...])


def shifted(own, reps):
    return [
        lax.ppermute(own, "rep", [(s, (s + q) % reps) for s in range(reps)])
        for q in range(1, reps)
    ]


def on_device(grid, reps, density, density_pattern, square_pattern, cube_pattern, block_order):
    rows, cols = density.shape
    order = grid * rows
    dims = factors(grid)
    outer, inner, pair = dims
    band_bytes = order * cols * 2
    room = min(3 * band_bytes + (4 << 20), 56 << 20)
    bf16, f32 = jnp.bfloat16, jnp.float32

    def call(kernel, name, flops, moved, out, operands, spec=None, **more):
        return pl.pallas_call(
            kernel,
            out_shape=[jax.ShapeDtypeStruct(shape, dtype) for shape, dtype in out],
            in_specs=spec or [IN_VMEM] * len(operands),
            out_specs=[IN_VMEM] * len(out),
            compiler_params=pltpu.CompilerParams(vmem_limit_bytes=room),
            cost_estimate=pl.CostEstimate(flops=flops, bytes_accessed=moved, transcendentals=0),
            name=name,
            **more,
        )(*operands)

    steps, hops = list(range(1, outer)), list(range(1, inner))
    last = steps[-1] if steps and hops else None
    before = [step for step in steps if step != last][-1:]

    held = {(0, 0): density}
    for step in steps:
        held[step, 0] = send(after(density), dims, 0, step)
    for hop in hops:
        held[0, hop] = send(after(density), dims, 1, hop)
    packed = jnp.concatenate(
        [density_pattern, square_pattern, cube_pattern, after(block_order)[None]], axis=0
    )
    table, panel_keep, square_keep, cube_keep = call(
        functools.partial(prepare_kernel, reps), "prepare", PLACE, 2 * band_bytes,
        [((order // BLOCK, TILE, cols), bf16), ((reps, rows, cols), bf16),
         ((rows, cols), f32), ((rows, cols), f32)],
        [packed], spec=[IN_SMEM],
    )
    for step in steps:
        for hop in hops:
            ready = [table] if step == last else []
            held[step, hop] = send(after(held[step, 0], *ready), dims, 1, hop)
    panel = shifted(after(density), reps)
    left, own = call(
        functools.partial(panel_kernel, reps), "panel", 4 * PLACE, 2 * band_bytes,
        [((rows, reps * cols), bf16), ((rows, cols), bf16)],
        [panel_keep, after(density), *panel],
    )

    keys = [(0, 0)] + [(3, 0)] + [(1, 0)] + [(2, 0)] + [(0, hop) for hop in hops]
    keys += [(step, hop) for step in steps for hop in hops]
    lone = [(0, 0)] + [key for key in keys if key[0] == last or key[0] in before and key[1]]
    stack = [key for key in keys if key not in lone]
    whole = lambda key, core: (*key, core, 0, rows)
    early, late = [], []
    for key in keys:
        group = late if key[0] == last and key[1] else early
        group.append(([whole(key, 0)], held[key] if key != (0, 0) else own))
        if pair > 1 and key in lone:
            value = after(held[key], *([] if group is late else [left]))
            group.append(([whole(key, 1)], send(value, dims, 2, 1)))
    if pair > 1 and stack:
        ready = panel + ([held[last, 0]] if hops else [])
        (stacked,) = call(
            stack_kernel, "stack", 0, 0, [((len(stack) * rows, cols), bf16)],
            [after(held[key], *ready) for key in stack],
        )
        early.append(([whole(key, 1) for key in stack], send(after(stacked), dims, 2, 1)))
    late_pieces, late_values = [piece[0] for piece, _ in late], [value for _, value in late]

    band, partial = call(
        functools.partial(early_kernel, [pieces for pieces, _ in early], late_pieces, dims),
        "square_early", 2 * rows * order * cols, 2 * band_bytes,
        [((order, cols), bf16), ((rows, cols), f32)],
        [left, table, *[value for _, value in early]],
    )
    span = BLOCK - math.gcd(pair * rows, BLOCK) + pair * rows
    span = min((span + BLOCK - 1) // BLOCK * BLOCK, order)
    band, tripled, square_half = call(
        functools.partial(late_kernel, late_pieces, dims), "square_late",
        2 * rows * span * cols, 4 * rows * cols,
        [((order, cols), bf16), ((rows, cols), f32), ((rows, cols), bf16)],
        [table, square_keep, left, band, partial, *late_values],
        input_output_aliases={3: 0},
        scratch_shapes=[pltpu.VMEM((span, cols), bf16)],
    )
    out = tripled
    for shift, half in enumerate([square_half] + shifted(square_half, reps)):
        (out,) = call(
            functools.partial(cube_kernel, shift), "cube_part",
            2 * rows * cols * cols, band_bytes // reps, [((rows, cols), f32)],
            [cube_keep, half, band, out],
        )
    return out


def solution(mesh):
    placed = (P("grid", "rep"), P(), P(), P(), P())
    return jax.shard_map(
        functools.partial(on_device, mesh.shape["grid"], mesh.shape["rep"]),
        mesh=mesh, in_specs=placed, out_specs=P("grid", "rep"), check_vma=False,
    )
```
